32 devices in a mesh: items: 4 (over y, x), strips: 8 (over z, core).
Axes of the slice: x: 2, y: 2, z: 4, core: 2. Of those that a mesh axis runs over, the one named last changes fastest.
Arguments:
- latents: bfloat16 [8, 64, 64, 768], P('items', 'strips'), may hold values from -24 to 24
- timesteps: int32 [8], P('items'), may hold values from 0 to 999
- labels: int32 [8], P('items'), may hold values from 0 to 1000
- time_in_weight: bfloat16 [256, 768], replicated, may hold values from -0.375 to 0.375
- time_in_bias: bfloat16 [768], replicated, may hold values from -3 to 3
- time_out_weight: bfloat16 [768, 768], replicated, may hold values from -0.21875 to 0.21875
- time_out_bias: bfloat16 [768], replicated, may hold values from -3 to 3
- label_table: bfloat16 [768, 1001], replicated, may hold values from -6 to 6
- ada_weight: bfloat16 [768, 4608], replicated, may hold values from -0.3125 to 0.3125
- ada_bias: bfloat16 [4608], replicated, may hold values from -3 to 3
- down_kernel: bfloat16 [768, 9], replicated, may hold values from -2 to 2
- down_bias: bfloat16 [768], replicated, may hold values from -3 to 3
- input_weight: bfloat16 [768, 2304], replicated, may hold values from -0.21875 to 0.21875
- query_bias: bfloat16 [768], replicated, may hold values from -3 to 3
- value_bias: bfloat16 [768], replicated, may hold values from -0.625 to 0.625
- output_weight: bfloat16 [768, 768], replicated, may hold values from -2.5 to 2.5
- output_bias: bfloat16 [768], replicated, may hold values from -3 to 3
- expand_weight: bfloat16 [768, 3072], replicated, may hold values from -0.21875 to 0.21875
- expand_bias: bfloat16 [3072], replicated, may hold values from -3 to 3
- mixer_kernel: bfloat16 [3072, 9], replicated, may hold values from -2 to 2
- mixer_bias: bfloat16 [3072], replicated, may hold values from -3 to 3
- shrink_weight: bfloat16 [3072, 768], replicated, may hold values from -0.109375 to 0.109375
- shrink_bias: bfloat16 [768], replicated, may hold values from -6 to 6
- cotangent: bfloat16 [8, 64, 64, 768], P('items', 'strips'), may hold values from -6 to 6
Outputs:
- result: bfloat16 [8, 64, 64, 768], P('items', 'strips')
- grad_latents: bfloat16 [8, 64, 64, 768], P('items', 'strips')
- grad_time_in_weight: float32 [256, 768], P(('items', 'strips'))
- grad_time_in_bias: float32 [768], P(('items', 'strips'))
- grad_time_out_weight: float32 [768, 768], P(('items', 'strips'))
- grad_time_out_bias: float32 [768], P(('items', 'strips'))
- grad_label_table: float32 [768, 1001], P(('items', 'strips'))
- grad_ada_weight: float32 [768, 4608], P(('items', 'strips'))
- grad_ada_bias: float32 [4608], P(('items', 'strips'))
- grad_down_kernel: float32 [768, 9], P(('items', 'strips'))
- grad_down_bias: float32 [768], P(('items', 'strips'))
- grad_input_weight: float32 [768, 2304], P(('items', 'strips'))
- grad_query_bias: float32 [768], P(('items', 'strips'))
- grad_value_bias: float32 [768], P(('items', 'strips'))
- grad_output_weight: float32 [768, 768], P(('items', 'strips'))
- grad_output_bias: float32 [768], P(('items', 'strips'))
- grad_expand_weight: float32 [768, 3072], P(('items', 'strips'))
- grad_expand_bias: float32 [3072], P(('items', 'strips'))
- grad_mixer_kernel: float32 [3072, 9], P(('items', 'strips'))
- grad_mixer_bias: float32 [3072], P(('items', 'strips'))
- grad_shrink_weight: float32 [3072, 768], P(('items', 'strips'))
- grad_shrink_bias: float32 [768], P(('items', 'strips'))
The draws below stay inside these ranges and needn't reach their ends.
All inputs are finite; a program needn't handle non-finite values.
Results may differ from the reference program's by a relative error of at most 0.025.
Values may be sent and summed in bfloat16 or wider, within the bound.
No kernel may reach another device: no remote copies, remote signals or barrier semaphores. Data moves between devices by JAX's collectives and lax.ppermute only.
A program may use at most 384 MiB of HBM per device.

```python
import math
import jax
import jax.numpy as jnp
from jax import lax

D = 768
HEADS = 12
HEAD_DIM = 64
FF = 3072
COND = 256
CLASSES = 1001
GRID = 64
LATENTS = 8


def draw_latents(key, part):
    key_noise, key_rows, key_columns = jax.random.split(jax.random.fold_in(key, 11), 3)
    shape = (LATENTS, GRID, GRID, D)
    row_scale = jnp.exp(jax.random.uniform(key_rows, (LATENTS, GRID, GRID, 1), minval=math.log(0.3), maxval=math.log(3.0)))
    column_scale = jnp.exp(jax.random.uniform(key_columns, (1, 1, 1, D), minval=math.log(0.5), maxval=math.log(2.0)))
    noise = jnp.clip(jax.random.normal(key_noise, shape), -4.0, 4.0)
    return (noise * row_scale * column_scale).astype(jnp.bfloat16)


def with_ends(result, key, smallest, largest):
    place = [jax.random.randint(jax.random.fold_in(key, axis), (), 0, length) for axis, length in enumerate(result.shape)]
    longest = result.shape.index(max(result.shape))
    beside = place[:longest] + [(place[longest] + 1) % result.shape[longest]] + place[longest + 1:]
    return result.at[tuple(place)].set(smallest).at[tuple(beside)].set(largest)


def levels(key, dims, pieces, low, high):
    gain = 1.0
    for axis_at, blocks in pieces:
        heights = jax.random.uniform(jax.random.fold_in(jax.random.fold_in(key, 6), axis_at), (blocks,), jnp.float32, low / len(pieces), high / len(pieces))
        gain = gain * jnp.repeat(jnp.exp(heights), dims[axis_at] // blocks).reshape((-1,) + (1,) * (len(dims) - 1 - axis_at))
    return gain


def gaussian(key, shape, width, limit, cuts=(), held_as=jnp.bfloat16):
    result = jax.random.normal(key, shape, jnp.float32) * width
    if len(cuts) > 0:
        result = levels(key, shape, cuts, -0.22, 0.18) * result
    return jnp.clip(result, min=-limit, max=limit).astype(held_as)


def setup_inputs(seed: int = 0) -> dict:
    key_of = jax.random.split(jax.random.key(seed), 25)
    return {
        "latents": draw_latents(jax.random.fold_in(key_of[24], 71), 0),
        "timesteps": with_ends(jax.random.randint(key_of[1], (LATENTS,), 0, 1000), jax.random.fold_in(key_of[1], 1), 0, 999).astype(jnp.int32),
        "labels": with_ends(jax.random.randint(key_of[2], (LATENTS,), 0, CLASSES), jax.random.fold_in(key_of[2], 1), 0, CLASSES - 1).astype(jnp.int32),
        "time_in_weight": gaussian(key_of[3], (COND, D), COND ** -0.5, 0.375),
        "time_in_bias": gaussian(key_of[4], (D,), 0.5, 3.0),
        "time_out_weight": gaussian(key_of[5], (D, D), D ** -0.5, 0.21875),
        "time_out_bias": gaussian(key_of[6], (D,), 0.5, 3.0),
        "label_table": gaussian(key_of[7], (D, CLASSES), 1.0, 6.0),
        "ada_weight": gaussian(key_of[8], (D, 6 * D), (D // 2) ** -0.5, 0.3125),
        "ada_bias": gaussian(key_of[9], (6 * D,), 0.5, 3.0),
        "down_kernel": gaussian(key_of[10], (D, 9), 9 ** -0.5, 2.0),
        "down_bias": gaussian(key_of[11], (D,), 0.5, 3.0),
        "input_weight": gaussian(key_of[12], (D, 3 * D), D ** -0.5, 0.21875),
        "query_bias": gaussian(key_of[13], (D,), 0.5, 3.0),
        "value_bias": gaussian(key_of[14], (D,), 0.1, 0.625),
        "output_weight": gaussian(key_of[15], (D, D), (D // 128) ** -0.5, 2.5),
        "output_bias": gaussian(key_of[16], (D,), 0.5, 3.0),
        "expand_weight": gaussian(key_of[17], (D, FF), D ** -0.5, 0.21875),
        "expand_bias": gaussian(key_of[18], (FF,), 0.5, 3.0),
        "mixer_kernel": gaussian(key_of[19], (FF, 9), 9 ** -0.5, 2.0),
        "mixer_bias": gaussian(key_of[20], (FF,), 0.5, 3.0),
        "shrink_weight": gaussian(key_of[21], (FF, D), FF ** -0.5, 0.109375),
        "shrink_bias": gaussian(key_of[22], (D,), 1.0, 6.0),
        "cotangent": gaussian(key_of[23], (LATENTS, GRID, GRID, D), 1.0, 6.0, ((0, 4), (1, 8))),
    }


highest = lax.Precision.HIGHEST
epsilon = 1e-06

@jax.custom_vjp
def low(v):
    return lax.optimization_barrier(v.astype(jnp.bfloat16)).astype(jnp.float32)

@jax.custom_vjp
def low_back(v):
    return v

def low_keep(v):
    return (low(v), None)

def low_pass(kept, grad):
    return (grad,)

def back_keep(v):
    return (v, None)

def back_low(kept, grad):
    return (low(grad),)
low.defvjp(low_keep, low_pass)
low_back.defvjp(back_keep, back_low)

def layer_norm(value):
    center = value - lax.optimization_barrier(jnp.mean(value, axis=-1, keepdims=True))
    spread = lax.optimization_barrier(jnp.mean(center * center, axis=-1, keepdims=True))
    return center * lax.rsqrt(spread + epsilon)

def time_features(timesteps, halves):
    frequency = jnp.exp(-math.log(10000.0) * jnp.arange(halves, dtype=jnp.float32) / halves)
    phase = timesteps.astype(jnp.float32)[:, None] * frequency[None, :]
    return jnp.concatenate([jnp.cos(phase), jnp.sin(phase)], axis=1)

def condition(timesteps, labels, time_in_weight, time_in_bias, time_out_weight, time_out_bias, label_table, ada_weight, ada_bias):
    sinus = time_features(timesteps, time_in_weight.shape[0] // 2)
    inner = jax.nn.silu(jnp.dot(sinus, time_in_weight, precision=highest) + time_in_bias)
    time_vector = jnp.dot(inner, time_out_weight, precision=highest) + time_out_bias
    onehot = (labels[:, None] == jnp.arange(label_table.shape[1], dtype=jnp.int32)[None, :]).astype(jnp.float32)
    class_vector = lax.dot_general(onehot, label_table, (((1,), (1,)), ((), ())), precision=highest)
    cond_vector = time_vector + class_vector
    return jnp.dot(jax.nn.silu(cond_vector), ada_weight, precision=highest) + ada_bias

def depthwise(image, kernel, offset):
    height, span = (image.shape[0], image.shape[1])
    padded = jnp.pad(image, ((1, 1), (1, 1), (0, 0)))
    total = offset + jnp.zeros_like(image)
    for row_step in range(3):
        for column_step in range(3):
            total = total + kernel[:, row_step * 3 + column_step] * padded[row_step:row_step + height, column_step:column_step + span, :]
    return total

def to_groups(image):
    count, rows, columns, features = image.shape
    split = image.reshape(count, rows // 2, 2, columns // 2, 2, features).transpose(0, 2, 4, 1, 3, 5)
    return split.reshape(count, 4, rows // 2 * (columns // 2), features)

def from_groups(grouped, rows, columns):
    count, features = (grouped.shape[0], grouped.shape[3])
    split = grouped.reshape(count, 2, 2, rows // 2, columns // 2, features).transpose(0, 3, 1, 4, 2, 5)
    return split.reshape(count, rows, columns, features)

def split_heads(array):
    return array.reshape(array.shape[0], array.shape[1], HEADS, HEAD_DIM)

def one_latent(image, modulation, weights):
    down_kernel, down_bias, input_weight, query_bias, value_bias, output_weight, output_bias, expand_weight, expand_bias, mixer_kernel, mixer_bias, shrink_weight, shrink_bias = weights
    features = image.shape[-1]
    scale = 1.0 / math.sqrt(HEAD_DIM)
    shift_a, scale_a, gate_a = (modulation[0], modulation[1], modulation[2])
    shift_b, scale_b, gate_b = (modulation[3], modulation[4], modulation[5])
    normed_a = low(layer_norm(image) * (1.0 + scale_a) + shift_a)
    reduced = low_back(low(depthwise(normed_a, down_kernel, down_bias)))
    grouped = to_groups(reduced[None])[0]
    projected = jnp.einsum('gsd,de->gse', grouped, input_weight, precision=highest)
    query = low_back(low(projected[..., :features] + query_bias))
    key = low_back(low(projected[..., features:2 * features]))
    value = low_back(low(projected[..., 2 * features:] + value_bias))
    scores = low_back(jnp.einsum('gqhe,gkhe->ghqk', split_heads(query), split_heads(key), precision=highest) * scale)
    softened = jax.nn.softmax(scores, axis=-1)
    mixed = jnp.einsum('ghqk,gkhe->gqhe', low(softened), split_heads(value), precision=highest)
    mixed = low_back(low(mixed.reshape(4, -1, features)))
    attended = low_back(jnp.einsum('gsd,de->gse', mixed, output_weight, precision=highest) + output_bias)
    attended_image = from_groups(attended[None], image.shape[0], image.shape[1])[0]
    middle = image + gate_a * attended_image
    normed_b = low(layer_norm(middle) * (1.0 + scale_b) + shift_b)
    hidden = low_back(low(jnp.einsum('rcd,df->rcf', normed_b, expand_weight, precision=highest) + expand_bias))
    conved = low_back(depthwise(hidden, mixer_kernel, mixer_bias))
    activated = low(jax.nn.gelu(conved, approximate=True))
    branch = low_back(jnp.einsum('rcf,fd->rcd', activated, shrink_weight, precision=highest) + shrink_bias)
    return middle + gate_b * branch

def reference(latents, timesteps, labels, time_in_weight, time_in_bias, time_out_weight, time_out_bias, label_table, ada_weight, ada_bias, down_kernel, down_bias, input_weight, query_bias, value_bias, output_weight, output_bias, expand_weight, expand_bias, mixer_kernel, mixer_bias, shrink_weight, shrink_bias, cotangent):
    primals = tuple((array.astype(jnp.float32) for array in (latents, time_in_weight, time_in_bias, time_out_weight, time_out_bias, label_table, ada_weight, ada_bias, down_kernel, down_bias, input_weight, query_bias, value_bias, output_weight, output_bias, expand_weight, expand_bias, mixer_kernel, mixer_bias, shrink_weight, shrink_bias)))

    def forward(image, w_time_in, b_time_in, w_time_out, b_time_out, table, w_ada, b_ada, k_down, b_down, w_input, b_query, b_value, w_output, b_output, w_expand, b_expand, k_mixer, b_mixer, w_shrink, b_shrink):
        modulation = condition(timesteps, labels, w_time_in, b_time_in, w_time_out, b_time_out, table, w_ada, b_ada)
        modulation = modulation.reshape(-1, 6, image.shape[-1])
        weights = (k_down, b_down, w_input, b_query, b_value, w_output, b_output, w_expand, b_expand, k_mixer, b_mixer, w_shrink, b_shrink)

        def per_latent(paired):
            return one_latent(paired[0], paired[1], weights)
        return lax.map(jax.checkpoint(per_latent), (image, modulation))
    output, pullback = jax.vjp(forward, *primals)
    g_image, g_time_in_w, g_time_in_b, g_time_out_w, g_time_out_b, g_table, g_ada_w, g_ada_b, g_down_k, g_down_b, g_input_w, g_query_b, g_value_b, g_output_w, g_output_b, g_expand_w, g_expand_b, g_mixer_k, g_mixer_b, g_shrink_w, g_shrink_b = pullback(cotangent.astype(jnp.float32))
    return (output.astype(jnp.bfloat16), g_image.astype(jnp.bfloat16), g_time_in_w, g_time_in_b, g_time_out_w, g_time_out_b, g_table, g_ada_w, g_ada_b, g_down_k, g_down_b, g_input_w, g_query_b, g_value_b, g_output_w, g_output_b, g_expand_w, g_expand_b, g_mixer_k, g_mixer_b, g_shrink_w, g_shrink_b)
```

```python
from functools import partial
import math

import jax
import jax.numpy as jnp
from jax import lax
from jax.experimental import pallas as pl
from jax.experimental.pallas import tpu as pltpu
from jax.sharding import PartitionSpec as P

HEADS = 12
HEAD_DIM = 64
LANES = 128
COLUMN_PARTS = 4
CHUNKS = 2
VMEM_BYTES = 60 * 1024 * 1024

highest = lax.Precision.HIGHEST
epsilon = 1e-06
bfloat = jnp.bfloat16
single = jnp.float32
both = ("items", "strips")


def params():
    return pltpu.CompilerParams(vmem_limit_bytes=VMEM_BYTES)


def cost(flops, moved, exps=0):
    return pl.CostEstimate(flops=int(flops), bytes_accessed=int(moved), transcendentals=int(exps))


def dot(a, b):
    return lax.dot_general(a, b, (((1,), (0,)), ((), ())), preferred_element_type=single)


def dot_nt(a, b):
    return lax.dot_general(a, b, (((1,), (1,)), ((), ())), preferred_element_type=single)


def dot_tn(a, b):
    return lax.dot_general(a, b, (((0,), (0,)), ((), ())), preferred_element_type=single)


def column_order(columns, back):
    sub = columns // COLUMN_PARTS
    first = lax.broadcasted_iota(jnp.int32, (columns, columns), 0)
    second = lax.broadcasted_iota(jnp.int32, (columns, columns), 1)
    kept, column = (second, first) if back else (first, second)
    return (column == COLUMN_PARTS * (kept % sub) + kept // sub).astype(bfloat)


def norm_parts(value):
    center = value - jnp.mean(value, axis=-1, keepdims=True)
    inverse = lax.rsqrt(jnp.mean(center * center, axis=-1, keepdims=True) + epsilon)
    return center * inverse, inverse


def norm_back(normed, inverse, grad):
    return inverse * (
        grad
        - jnp.mean(grad, axis=-1, keepdims=True)
        - normed * jnp.mean(grad * normed, axis=-1, keepdims=True)
    )


def put_wide(ref, row, cells):
    sub = cells.shape[1]
    place = lax.broadcasted_iota(jnp.int32, cells.shape[1:], 0)
    ref[row, 1 : COLUMN_PARTS + 1] = cells
    ref[row, 0] = jnp.where(place == 0, 0.0, pltpu.roll(cells[COLUMN_PARTS - 1], 1, 0))
    ref[row, COLUMN_PARTS + 1] = jnp.where(
        place == sub - 1, 0.0, pltpu.roll(cells[0], sub - 1, 0)
    )


def conv_row(ref, row, taps, start):
    total = start
    for i in range(3):
        for j in range(3):
            total = total + taps[3 * i + j] * ref[row + i, j : j + COLUMN_PARTS]
    return total


def conv_back_row(ref, row, taps):
    total = None
    for i in range(3):
        for j in range(3):
            term = taps[3 * i + j] * ref[row + 2 - i, 2 - j : 2 - j + COLUMN_PARTS]
            total = term if total is None else total + term
    return total


def front_kernel(
    edge_ref, x_ref, top_ref, bottom_ref, scale_ref, shift_ref, taps_ref, bias_ref,
    grouped_ref, normed_ref, kept_ref, wide,
):
    rows, columns, features = x_ref.shape[1:]
    sub = columns // COLUMN_PARTS
    order = column_order(columns, False)
    scale = 1.0 + scale_ref[0]
    shift = shift_ref[0]

    def fill(row, raw, keep):
        cells = dot(order, raw)
        normed = (norm_parts(cells)[0] * scale + shift) * keep
        low = normed.astype(bfloat)
        normed_ref[0, row] = low
        put_wide(wide, row, low.astype(single).reshape(COLUMN_PARTS, sub, features))
        return cells

    fill(0, top_ref[0, 0], edge_ref[0])
    fill(rows + 1, bottom_ref[0, 0], edge_ref[1])

    @pl.loop(0, rows)
    def _(row):
        kept_ref[0, row] = fill(row + 1, x_ref[0, row], 1.0).astype(bfloat)

    taps = [taps_ref[t : t + 1] for t in range(9)]
    bias = bias_ref[...]

    @pl.loop(0, rows // 2)
    def _(pair):
        for a in range(2):
            for lane in range(0, features, LANES):
                at = pl.ds(lane, LANES)
                total = jnp.zeros((COLUMN_PARTS, sub, LANES), single) + bias[:, lane : lane + LANES]
                for i in range(3):
                    for j in range(3):
                        total = total + taps[3 * i + j][:, lane : lane + LANES] * wide[
                            pair * 2 + a + i, j : j + COLUMN_PARTS, :, at
                        ]
                low = total.astype(bfloat)
                for j in range(COLUMN_PARTS):
                    grouped_ref[
                        0, 2 * a + j % 2, pl.ds(pl.multiple_of((pair * 2 + j // 2) * sub, sub), sub), at
                    ] = low[j]


def front(edge, latents, top, bottom, scale, shift, taps, bias):
    count, rows, columns, features = latents.shape
    quarter = rows * columns // 4
    sub = columns // COLUMN_PARTS
    image = lambda r: pl.BlockSpec((1, r, columns, features), lambda l: (l, 0, 0, 0))
    vector = pl.BlockSpec((1, 1, features), lambda l: (l, 0, 0))
    return pl.pallas_call(
        front_kernel,
        grid=(count,),
        in_specs=[
            pl.BlockSpec(memory_space=pltpu.SMEM),
            image(rows), image(1), image(1), vector, vector,
            pl.BlockSpec((16, features), lambda l: (0, 0)),
            pl.BlockSpec((1, features), lambda l: (0, 0)),
        ],
        out_specs=[
            pl.BlockSpec((1, 4, quarter, features), lambda l: (l, 0, 0, 0)),
            image(rows + 2), image(rows),
        ],
        out_shape=[
            jax.ShapeDtypeStruct((count, 4, quarter, features), bfloat),
            jax.ShapeDtypeStruct((count, rows + 2, columns, features), bfloat),
            jax.ShapeDtypeStruct((count, rows, columns, features), bfloat),
        ],
        scratch_shapes=[pltpu.VMEM((rows + 2, COLUMN_PARTS + 2, sub, features), single)],
        compiler_params=params(),
        cost_estimate=cost(count * rows * columns * features * 150, count * rows * columns * features * 8),
        name="front",
    )(edge, latents, top, bottom, scale, shift, taps, bias)


def upstream_kernel(g_ref, top_ref, bottom_ref, gate_ref, kept_ref, branch_ref, bias_ref):
    rows, columns, features = g_ref.shape[1:]
    order = column_order(columns, False)
    gate = gate_ref[0]

    def low(raw):
        cells = dot(order, raw)
        return cells, (cells * gate).astype(bfloat)

    branch_ref[0, 0] = low(top_ref[0, 0])[1]
    branch_ref[0, rows + 1] = low(bottom_ref[0, 0])[1]

    def step(row, total):
        cells, grad = low(g_ref[0, row])
        kept_ref[0, row] = cells.astype(bfloat)
        branch_ref[0, row + 1] = grad
        return total + jnp.sum(grad.astype(single), axis=0, keepdims=True)

    bias_ref[0] = lax.fori_loop(0, rows, step, jnp.zeros((1, features), single))


def upstream_parts(cotangent, top, bottom, gate):
    count, rows, columns, features = cotangent.shape
    image = lambda r: pl.BlockSpec((1, r, columns, features), lambda l: (l, 0, 0, 0))
    vector = pl.BlockSpec((1, 1, features), lambda l: (l, 0, 0))
    return pl.pallas_call(
        upstream_kernel,
        grid=(count,),
        in_specs=[image(rows), image(1), image(1), vector],
        out_specs=[image(rows), image(rows + 2), vector],
        out_shape=[
            jax.ShapeDtypeStruct((count, rows, columns, features), bfloat),
            jax.ShapeDtypeStruct((count, rows + 2, columns, features), bfloat),
            jax.ShapeDtypeStruct((count, 1, features), single),
        ],
        compiler_params=params(),
        cost_estimate=cost(count * rows * columns * features * 130, count * rows * columns * features * 6),
        name="upstream",
    )(cotangent, top, bottom, gate)


QUERY_STEP = 256


def attend_kernel(
    x_ref, wq_ref, wk_ref, wv_ref, bq_ref, bv_ref, q_ref, k_ref, v_ref, mixed_ref, log_ref
):
    tokens = x_ref.shape[0]
    base = math.log2(math.e) / math.sqrt(HEAD_DIM)
    x = x_ref[...]
    q_ref[...] = (dot(x, wq_ref[...]) + bq_ref[...]).astype(bfloat)
    k_ref[...] = dot(x, wk_ref[...]).astype(bfloat)
    v_ref[...] = (dot(x, wv_ref[...]) + bv_ref[...]).astype(bfloat)
    keys = k_ref[...]
    values = v_ref[...].T
    lane = lax.broadcasted_iota(jnp.int32, (QUERY_STEP, LANES), 1)
    for at in range(0, tokens, QUERY_STEP):
        part = q_ref[at : at + QUERY_STEP]
        outs = []
        for head in range(LANES // HEAD_DIM):
            own = jnp.where(lane // HEAD_DIM == head, part, jnp.zeros_like(part))
            scores = dot_nt(keys, own)
            peak = jnp.max(scores, axis=0, keepdims=True) * base
            soft = jnp.exp2(scores * base - peak)
            total = jnp.sum(soft, axis=0, keepdims=True)
            log_ref[0, head : head + 1, at : at + QUERY_STEP] = peak + jnp.log2(total)
            out = dot(values[head * HEAD_DIM : (head + 1) * HEAD_DIM], soft.astype(bfloat))
            outs.append(out * (1.0 / total))
        mixed_ref[at : at + QUERY_STEP] = jnp.concatenate(outs, axis=0).T.astype(bfloat)


def attend(x, wq, wk, wv, bq, bv):
    tokens, features = x.shape
    width = wq.shape[1]
    pairs = width // LANES
    weight = pl.BlockSpec((features, LANES), lambda h: (0, h))
    bias = pl.BlockSpec((1, LANES), lambda h: (0, h))
    column = pl.BlockSpec((tokens, LANES), lambda h: (0, h))
    lows = jax.ShapeDtypeStruct((tokens, width), bfloat)
    return pl.pallas_call(
        attend_kernel,
        grid=(pairs,),
        in_specs=[pl.BlockSpec((tokens, features), lambda h: (0, 0)), weight, weight, weight, bias, bias],
        out_specs=[column] * 4 + [pl.BlockSpec((1, 2, tokens), lambda h: (h, 0, 0))],
        out_shape=[lows] * 4 + [jax.ShapeDtypeStruct((pairs, 2, tokens), single)],
        compiler_params=params(),
        cost_estimate=cost(
            6 * tokens * features * width + 16 * tokens * tokens * width,
            2 * tokens * features + 8 * tokens * width + 6 * features * width,
            2 * pairs * tokens * tokens,
        ),
        name="attend",
    )(x, wq, wk, wv, bq, bv)


def attend_back_kernel(
    q_ref, k_ref, v_ref, mixed_ref, grad_ref, log_ref, dq_ref, dk_ref, dv_ref, dk_sum, dv_sum
):
    tokens = q_ref.shape[0]
    scale = 1.0 / math.sqrt(HEAD_DIM)
    base = math.log2(math.e) * scale
    keys = k_ref[...]
    values = v_ref[...]
    keys_turned = keys.T
    lane = lax.broadcasted_iota(jnp.int32, (QUERY_STEP, LANES), 1)
    for at in range(0, tokens, QUERY_STEP):
        rows = slice(at, at + QUERY_STEP)
        part = q_ref[rows]
        grad = grad_ref[rows]
        shares = (grad.astype(single) * mixed_ref[rows].astype(single)).T
        outs = []
        for head in range(LANES // HEAD_DIM):
            mine = lane // HEAD_DIM == head
            own = jnp.where(mine, part, jnp.zeros_like(part))
            own_grad = jnp.where(mine, grad, jnp.zeros_like(grad))
            share = jnp.sum(
                shares[head * HEAD_DIM : (head + 1) * HEAD_DIM], axis=0, keepdims=True
            )
            soft = jnp.exp2(dot_nt(keys, own) * base - log_ref[0, head : head + 1, rows])
            d_scores = (soft * (dot_nt(values, own_grad) - share)).astype(bfloat)
            dv_part = dot(soft.astype(bfloat), own_grad)
            dk_part = dot(d_scores, own)
            if at == 0 and head == 0:
                dv_sum[...] = dv_part
                dk_sum[...] = dk_part
            else:
                dv_sum[...] += dv_part
                dk_sum[...] += dk_part
            outs.append(dot(keys_turned[head * HEAD_DIM : (head + 1) * HEAD_DIM], d_scores))
        dq_ref[rows] = (jnp.concatenate(outs, axis=0) * scale).T.astype(bfloat)
    dk_ref[...] = (dk_sum[...] * scale).astype(bfloat)
    dv_ref[...] = dv_sum[...].astype(bfloat)


def attend_back(q, k, v, mixed, grad, logs):
    tokens, width = q.shape
    pairs = width // LANES
    column = pl.BlockSpec((tokens, LANES), lambda h: (0, h))
    lows = jax.ShapeDtypeStruct((tokens, width), bfloat)
    return pl.pallas_call(
        attend_back_kernel,
        grid=(pairs,),
        in_specs=[column] * 5 + [pl.BlockSpec((1, 2, tokens), lambda h: (h, 0, 0))],
        out_specs=[column] * 3,
        out_shape=[lows] * 3,
        scratch_shapes=[pltpu.VMEM((tokens, LANES), single)] * 2,
        compiler_params=params(),
        cost_estimate=cost(
            40 * tokens * tokens * width, 16 * tokens * width, 2 * pairs * tokens * tokens
        ),
        name="attend_back",
    )(q, k, v, mixed, grad, logs)


def middle_kernel(
    parts, *refs
):
    mixed_refs = refs[:parts]
    weight_ref, bias_ref, x_ref, gate_ref, scale_ref, shift_ref = refs[parts : parts + 6]
    attended_ref, middle_ref, normed_ref, grouped = refs[parts + 6 :]
    rows, columns, features = x_ref.shape[1:]
    sub = columns // COLUMN_PARTS
    quarter = rows * columns // 4
    total = bias_ref[...]
    at = 0
    for ref in mixed_refs:
        width = ref.shape[-1]
        total = total + dot(ref[0].reshape(4 * quarter, width), weight_ref[at : at + width])
        at += width
    grouped[...] = total.reshape(4, quarter, features)
    gate = gate_ref[0]
    scale = 1.0 + scale_ref[0]
    shift = shift_ref[0]

    @pl.loop(0, rows // 2)
    def _(pair):
        for a in range(2):
            row = pair * 2 + a
            cells = jnp.concatenate(
                [
                    grouped[2 * a + j % 2, pl.ds(pl.multiple_of((pair * 2 + j // 2) * sub, sub), sub)]
                    for j in range(COLUMN_PARTS)
                ],
                axis=0,
            )
            attended_ref[0, row] = cells
            middle = x_ref[0, row].astype(single) + gate * cells
            middle_ref[0, row] = middle
            normed_ref[0, row] = (norm_parts(middle)[0] * scale + shift).astype(bfloat)


def middle_part(mixed, weight, bias, kept, gate, scale, shift):
    count, rows, columns, features = kept.shape
    quarter = rows * columns // 4
    image = pl.BlockSpec((1, rows, columns, features), lambda l: (l, 0, 0, 0))
    vector = pl.BlockSpec((1, 1, features), lambda l: (l, 0, 0))
    return pl.pallas_call(
        partial(middle_kernel, len(mixed)),
        grid=(count,),
        in_specs=[
            pl.BlockSpec((1, 4, quarter, m.shape[-1]), lambda l: (l, 0, 0, 0)) for m in mixed
        ]
        + [
            pl.BlockSpec((features, features), lambda l: (0, 0)),
            pl.BlockSpec((1, features), lambda l: (0, 0)),
            image, vector, vector, vector,
        ],
        out_specs=[image] * 3,
        out_shape=[
            jax.ShapeDtypeStruct(kept.shape, single),
            jax.ShapeDtypeStruct(kept.shape, single),
            jax.ShapeDtypeStruct(kept.shape, bfloat),
        ],
        scratch_shapes=[pltpu.VMEM((4, quarter, features), single)],
        compiler_params=params(),
        cost_estimate=cost(2 * kept.size * features, 14 * kept.size),
        name="middle",
    )(*mixed, weight, bias, kept, gate, scale, shift)


def feed_kernel(
    edge_ref, nb_ref, top_ref, bottom_ref, db_ref, we_ref, be_ref, taps_ref, bm_ref, ws_ref,
    branch_ref, e_ref, gws_ref, gwe_ref, small_ref,
    nb_wide, nb_turned, db_own, hidden, d_act, act, d_hid, wide, d_wide,
):
    count, rows, columns, features = nb_ref.shape
    sub = columns // COLUMN_PARTS
    block = we_ref.shape[1]
    own = rows * columns
    tall = (rows + 4) * columns
    mid = (rows + 2) * columns
    first = pl.program_id(0) == 0

    @pl.when(first)
    def _():
        for l in range(count):
            nb_wide[l * tall : l * tall + 2 * columns] = top_ref[l].reshape(2 * columns, features)
            nb_wide[l * tall + 2 * columns : (l + 1) * tall - 2 * columns] = nb_ref[l].reshape(
                own, features
            )
            nb_wide[(l + 1) * tall - 2 * columns : (l + 1) * tall] = bottom_ref[l].reshape(
                2 * columns, features
            )
            nb_turned[:, l * own : (l + 1) * own] = nb_ref[l].reshape(own, features).T
            db_own[l * own : (l + 1) * own] = db_ref[l, 1 : rows + 1].reshape(own, features)
        branch_ref[...] = jnp.zeros_like(branch_ref)
        e_ref[...] = jnp.zeros_like(e_ref)

    hidden[...] = dot(nb_wide[...], we_ref[...]) + be_ref[...]
    d_act[...] = dot_nt(db_ref[...].reshape(count * mid, features), ws_ref[...])
    small_ref[...] = jnp.zeros_like(small_ref)

    c0 = math.sqrt(2.0 / math.pi)
    c1 = c0 * 0.044715

    @pl.loop(0, count * (block // LANES))
    def _(index):
        l = index // (block // LANES)
        at = pl.ds(pl.multiple_of((index % (block // LANES)) * LANES, LANES), LANES)
        taps = [taps_ref[t : t + 1, at] for t in range(9)]
        bias = bm_ref[:, at]
        for row in range(rows + 4):
            cells = hidden[pl.ds(pl.multiple_of(l * tall + row * columns, columns), columns), at]
            cells = cells.astype(bfloat).astype(single)
            if row < 2:
                cells = cells * edge_ref[0]
            if row >= rows + 2:
                cells = cells * edge_ref[1]
            put_wide(wide, row, cells.reshape(COLUMN_PARTS, sub, LANES))
        start = jnp.zeros((COLUMN_PARTS, sub, LANES), single) + bias
        for row in range(rows + 2):
            v = conv_row(wide, row, taps, start)
            cube = (v * v) * c1
            half = 0.5 * jnp.tanh(v * (cube + c0)) + 0.5
            gelu = v * half
            slope = half + gelu * (1.0 - half) * (6.0 * cube + 2.0 * c0)
            if 1 <= row <= rows:
                act[pl.ds(pl.multiple_of(l * own + (row - 1) * columns, columns), columns), at] = (
                    gelu.reshape(columns, LANES).astype(bfloat)
                )
            grad = d_act[pl.ds(pl.multiple_of(l * mid + row * columns, columns), columns), at]
            grad = (grad.reshape(COLUMN_PARTS, sub, LANES) * slope).astype(bfloat).astype(single)
            put_wide(d_wide, row, grad)
        sums = [jnp.zeros((sub, LANES), single) for _ in range(11)]
        for row in range(rows):
            d_in = conv_back_row(d_wide, row, taps).astype(bfloat)
            d_hid[pl.ds(pl.multiple_of(l * own + row * columns, columns), columns), at] = (
                d_in.reshape(columns, LANES)
            )
            center = d_wide[row + 1, 1 : COLUMN_PARTS + 1]
            for i in range(3):
                for j in range(3):
                    sums[3 * i + j] += jnp.sum(
                        center * wide[row + 1 + i, j : j + COLUMN_PARTS], axis=0
                    )
            sums[9] += jnp.sum(center, axis=0)
            sums[10] += jnp.sum(d_in.astype(single), axis=0)
        for t in range(11):
            small_ref[t : t + 1, at] += jnp.sum(sums[t], axis=0, keepdims=True)

    branch_ref[...] += dot(act[...], ws_ref[...])
    e_ref[...] += dot_nt(d_hid[...], we_ref[...])
    gws_ref[...] = dot_tn(act[...], db_own[...]).astype(bfloat)
    gwe_ref[0] = dot(nb_turned[...], d_hid[...]).astype(bfloat)


def feed_forward(edge, nb, top, bottom, db, we, be, taps, bm, ws):
    count, rows, columns, features = nb.shape
    hidden = we.shape[1]
    block = features
    steps = hidden // block
    tokens = count * rows * columns
    tall = count * (rows + 4) * columns
    mid = count * (rows + 2) * columns
    sub = columns // COLUMN_PARTS
    whole = lambda a: pl.BlockSpec(a.shape, lambda s: (0,) * a.ndim)
    return pl.pallas_call(
        feed_kernel,
        grid=(steps,),
        in_specs=[
            pl.BlockSpec(memory_space=pltpu.SMEM),
            whole(nb), whole(top), whole(bottom), whole(db),
            pl.BlockSpec((features, block), lambda s: (0, s)),
            pl.BlockSpec((1, block), lambda s: (0, s)),
            pl.BlockSpec((16, block), lambda s: (0, s)),
            pl.BlockSpec((1, block), lambda s: (0, s)),
            pl.BlockSpec((block, features), lambda s: (s, 0)),
        ],
        out_specs=[
            pl.BlockSpec((tokens, features), lambda s: (0, 0)),
            pl.BlockSpec((tokens, features), lambda s: (0, 0)),
            pl.BlockSpec((block, features), lambda s: (s, 0)),
            pl.BlockSpec((1, features, block), lambda s: (s, 0, 0)),
            pl.BlockSpec((16, block), lambda s: (0, s)),
        ],
        out_shape=[
            jax.ShapeDtypeStruct((tokens, features), single),
            jax.ShapeDtypeStruct((tokens, features), single),
            jax.ShapeDtypeStruct((hidden, features), bfloat),
            jax.ShapeDtypeStruct((steps, features, block), bfloat),
            jax.ShapeDtypeStruct((16, hidden), single),
        ],
        scratch_shapes=[
            pltpu.VMEM((tall, features), bfloat),
            pltpu.VMEM((features, tokens), bfloat),
            pltpu.VMEM((tokens, features), bfloat),
            pltpu.VMEM((tall, block), single),
            pltpu.VMEM((mid, block), single),
            pltpu.VMEM((tokens, block), bfloat),
            pltpu.VMEM((tokens, block), bfloat),
            pltpu.VMEM((rows + 4, COLUMN_PARTS + 2, sub, LANES), single),
            pltpu.VMEM((rows + 2, COLUMN_PARTS + 2, sub, LANES), single),
        ],
        compiler_params=params(),
        cost_estimate=cost(
            2 * features * hidden * (tall + mid + 4 * tokens),
            8 * tokens * features + 8 * features * hidden,
            mid * hidden,
        ),
        name="feed_forward",
    )(edge, nb, top, bottom, db, we, be, taps, bm, ws)


def turn_kernel(parts, *refs):
    (
        branch_ref, e_ref, middle_ref, attended_ref, g_ref,
        gate_b_ref, scale_ref, gate_a_ref, bias_ref, weight_ref,
    ) = refs[:10]
    mixed_refs = refs[10 : 10 + parts]
    result_ref, d_middle_ref = refs[10 + parts : 12 + parts]
    d_mixed_refs = refs[12 + parts : 12 + 2 * parts]
    gw_ref, sums_ref, gw_sum, grouped = refs[12 + 2 * parts :]
    rows, columns, features = g_ref.shape[1:]
    sub = columns // COLUMN_PARTS
    quarter = rows * columns // 4
    back = column_order(columns, True)
    gate_b = gate_b_ref[0]
    scale = 1.0 + scale_ref[0]
    gate_a = gate_a_ref[0]

    def step(pair, sums):
        for a in range(2):
            row = pair * 2 + a
            at = pl.ds(pl.multiple_of(row * columns, columns), columns)
            branch = branch_ref[at] + bias_ref[...]
            middle = middle_ref[0, row]
            g = g_ref[0, row].astype(single)
            result = (middle + gate_b * branch).astype(bfloat)
            result_ref[0, row] = dot(back, result).astype(bfloat)
            normed, inverse = norm_parts(middle)
            e = e_ref[at]
            d_middle = g + norm_back(normed, inverse, e * scale)
            d_middle_ref[0, row] = d_middle
            low = (d_middle * gate_a).astype(bfloat)
            for j in range(COLUMN_PARTS):
                grouped[
                    2 * a + j % 2, pl.ds(pl.multiple_of((pair * 2 + j // 2) * sub, sub), sub)
                ] = low[j * sub : (j + 1) * sub]
            terms = (g * branch, e, e * normed, d_middle * attended_ref[0, row], low.astype(single))
            sums = tuple(
                s + jnp.sum(t.reshape(columns // 8, 8, features), axis=0) for s, t in zip(sums, terms)
            )
        return sums

    sums = lax.fori_loop(
        0, rows // 2, step, tuple(jnp.zeros((8, features), single) for _ in range(5))
    )
    for t in range(5):
        sums_ref[0, t : t + 1] = jnp.sum(sums[t], axis=0, keepdims=True)
    sums_ref[0, 5:8] = jnp.zeros((3, features), single)
    grad = grouped[...].reshape(4 * quarter, features)
    at = 0
    for mixed_ref, d_ref in zip(mixed_refs, d_mixed_refs):
        width = mixed_ref.shape[-1]
        piece = slice(at, at + width)
        d_ref[0] = dot_nt(grad, weight_ref[piece]).astype(bfloat).reshape(4, quarter, width)
        part = dot_tn(mixed_ref[0].reshape(4 * quarter, width), grad)

        @pl.when(pl.program_id(0) == 0)
        def _():
            gw_sum[piece] = part

        @pl.when(pl.program_id(0) > 0)
        def _():
            gw_sum[piece] += part

        at += width

    @pl.when(pl.program_id(0) == pl.num_programs(0) - 1)
    def _():
        gw_ref[...] = gw_sum[...].astype(bfloat)


def turn(branch, e, middle, attended, g, gate_b, scale, gate_a, bias, weight, mixed):
    count, rows, columns, features = g.shape
    quarter = rows * columns // 4
    own = rows * columns
    image = pl.BlockSpec((1, rows, columns, features), lambda l: (l, 0, 0, 0))
    flat = pl.BlockSpec((own, features), lambda l: (l, 0))
    vector = pl.BlockSpec((1, 1, features), lambda l: (l, 0, 0))
    groups = [pl.BlockSpec((1, 4, quarter, m.shape[-1]), lambda l: (l, 0, 0, 0)) for m in mixed]
    square = pl.BlockSpec((features, features), lambda l: (0, 0))
    return pl.pallas_call(
        partial(turn_kernel, len(mixed)),
        grid=(count,),
        in_specs=[flat, flat, image, image, image, vector, vector, vector]
        + [pl.BlockSpec((1, features), lambda l: (0, 0)), square]
        + groups,
        out_specs=[image, image] + groups + [square, pl.BlockSpec((1, 8, features), lambda l: (l, 0, 0))],
        out_shape=[
            jax.ShapeDtypeStruct(g.shape, bfloat),
            jax.ShapeDtypeStruct(g.shape, single),
        ]
        + [jax.ShapeDtypeStruct(m.shape, bfloat) for m in mixed]
        + [
            jax.ShapeDtypeStruct((features, features), bfloat),
            jax.ShapeDtypeStruct((count, 8, features), single),
        ],
        scratch_shapes=[
            pltpu.VMEM((features, features), single),
            pltpu.VMEM((4, quarter, features), bfloat),
        ],
        compiler_params=params(),
        cost_estimate=cost(4 * g.size * features, 26 * g.size),
        name="turn",
    )(branch, e, middle, attended, g, gate_b, scale, gate_a, bias, weight, *mixed)


def final_kernel(
    d_ref, top_ref, bottom_ref, normed_ref, x_ref, d_middle_ref, scale_ref, taps_ref,
    out_ref, taps_out_ref, sums_ref, wide, d_wide,
):
    rows, columns, features = x_ref.shape[1:]
    sub = columns // COLUMN_PARTS
    back = column_order(columns, True)
    scale = 1.0 + scale_ref[0]

    def piece(ref, a, start):
        parts = [
            ref[0, 2 * a + j % 2, pl.ds(pl.multiple_of(start + (j // 2) * sub, sub), sub)]
            for j in range(COLUMN_PARTS)
        ]
        return jnp.stack(parts, axis=0).astype(single)

    def halo(ref):
        parts = [
            ref[0, j % 2, pl.ds((j // 2) * sub, sub)] for j in range(COLUMN_PARTS)
        ]
        return jnp.stack(parts, axis=0).astype(single)

    put_wide(d_wide, 0, halo(top_ref))
    put_wide(d_wide, rows + 1, halo(bottom_ref))

    @pl.loop(0, rows // 2)
    def _(pair):
        for a in range(2):
            put_wide(d_wide, pair * 2 + a + 1, piece(d_ref, a, pair * 2 * sub))

    @pl.loop(0, rows + 2)
    def _(row):
        put_wide(wide, row, normed_ref[0, row].astype(single).reshape(COLUMN_PARTS, sub, features))

    @pl.when(pl.program_id(0) == 0)
    def _():
        taps_out_ref[...] = jnp.zeros_like(taps_out_ref)

    d_normed = wide
    for lane in range(0, features, LANES):
        at = pl.ds(lane, LANES)
        taps = [taps_ref[t : t + 1, at] for t in range(9)]

        def step(row, sums):
            total = None
            center = d_wide[row + 1, 1 : COLUMN_PARTS + 1, :, at]
            sums = list(sums)
            for i in range(3):
                for j in range(3):
                    term = taps[3 * i + j] * d_wide[row + 2 - i, 2 - j : 2 - j + COLUMN_PARTS, :, at]
                    total = term if total is None else total + term
                    sums[3 * i + j] = sums[3 * i + j] + jnp.sum(
                        center * wide[row + i, j : j + COLUMN_PARTS, :, at], axis=0
                    )
            sums[9] = sums[9] + jnp.sum(center, axis=0)
            d_normed[row, 1 : COLUMN_PARTS + 1, :, at] = total
            return tuple(sums)

        sums = lax.fori_loop(
            0, rows, step, tuple(jnp.zeros((sub, LANES), single) for _ in range(10))
        )
        for t in range(10):
            taps_out_ref[t : t + 1, at] += jnp.sum(sums[t], axis=0, keepdims=True)

    def last(row, sums):
        cells = d_normed[row, 1 : COLUMN_PARTS + 1].reshape(columns, features)
        normed, inverse = norm_parts(x_ref[0, row].astype(single))
        grad = d_middle_ref[0, row] + norm_back(normed, inverse, cells * scale)
        out_ref[0, row] = dot(back, grad.astype(bfloat)).astype(bfloat)
        return tuple(
            s + jnp.sum(t.reshape(columns // 8, 8, features), axis=0)
            for s, t in zip(sums, (cells, cells * normed))
        )

    sums = lax.fori_loop(0, rows, last, tuple(jnp.zeros((8, features), single) for _ in range(2)))
    for t in range(2):
        sums_ref[0, t : t + 1] = jnp.sum(sums[t], axis=0, keepdims=True)
    sums_ref[0, 2:8] = jnp.zeros((6, features), single)


def final(d_reduced, top, bottom, normed, kept, d_middle, scale, taps):
    count, rows, columns, features = kept.shape
    quarter = rows * columns // 4
    sub = columns // COLUMN_PARTS
    image = lambda r: pl.BlockSpec((1, r, columns, features), lambda l: (l, 0, 0, 0))
    vector = pl.BlockSpec((1, 1, features), lambda l: (l, 0, 0))
    side = pl.BlockSpec((1, 2, 2 * sub, features), lambda l: (l, 0, 0, 0))
    return pl.pallas_call(
        final_kernel,
        grid=(count,),
        in_specs=[
            pl.BlockSpec((1, 4, quarter, features), lambda l: (l, 0, 0, 0)),
            side, side, image(rows + 2), image(rows), image(rows), vector,
            pl.BlockSpec((16, features), lambda l: (0, 0)),
        ],
        out_specs=[
            image(rows),
            pl.BlockSpec((16, features), lambda l: (0, 0)),
            pl.BlockSpec((1, 8, features), lambda l: (l, 0, 0)),
        ],
        out_shape=[
            jax.ShapeDtypeStruct(kept.shape, bfloat),
            jax.ShapeDtypeStruct((16, features), single),
            jax.ShapeDtypeStruct((count, 8, features), single),
        ],
        scratch_shapes=[pltpu.VMEM((rows + 2, COLUMN_PARTS + 2, sub, features), single)] * 2,
        compiler_params=params(),
        cost_estimate=cost(kept.size * 180, kept.size * 12),
        name="final",
    )(d_reduced, top, bottom, normed, kept, d_middle, scale, taps)


def from_above(tail):
    count = lax.axis_size("strips")
    return lax.ppermute(tail, "strips", [(i, i + 1) for i in range(count - 1)])


def from_below(head):
    count = lax.axis_size("strips")
    return lax.ppermute(head, "strips", [(i + 1, i) for i in range(count - 1)])


def time_features(timesteps, halves):
    frequency = jnp.exp(-math.log(10000.0) * jnp.arange(halves, dtype=jnp.float32) / halves)
    phase = timesteps.astype(jnp.float32)[:, None] * frequency[None, :]
    return jnp.concatenate([jnp.cos(phase), jnp.sin(phase)], axis=1)


def exact(a, b):
    return jnp.dot(a, b, precision=highest)


def exact_nt(a, b):
    return lax.dot_general(a, b, (((1,), (1,)), ((), ())), precision=highest)


def exact_tn(a, b):
    return lax.dot_general(a, b, (((0,), (0,)), ((), ())), precision=highest)


def silu_slope(value):
    gate = jax.nn.sigmoid(value)
    return gate * (1.0 + value * (1.0 - gate))


def tap_rows(kernel):
    return jnp.pad(kernel.astype(single).T, ((0, 7), (0, 0)))


def per_device(
    latents,
    timesteps,
    labels,
    time_in_weight,
    time_in_bias,
    time_out_weight,
    time_out_bias,
    label_table,
    ada_weight,
    ada_bias,
    down_kernel,
    down_bias,
    input_weight,
    query_bias,
    value_bias,
    output_weight,
    output_bias,
    expand_weight,
    expand_bias,
    mixer_kernel,
    mixer_bias,
    shrink_weight,
    shrink_bias,
    cotangent,
):
    count, rows, columns, features = latents.shape
    strips = lax.axis_size("strips")
    items = lax.axis_size("items")
    devices = strips * items
    strip = lax.axis_index("strips")
    item = lax.axis_index("items")
    me = item * strips + strip
    sub = columns // COLUMN_PARTS
    quarter = rows * columns // 4
    groups = count * 4
    share = strips // groups
    width = features // share
    row_vector = lambda v: v.astype(single).reshape(1, -1)
    edge = jnp.stack([strip > 0, strip < strips - 1]).astype(single)

    all_times = lax.all_gather(timesteps, "items", axis=0, tiled=True)
    all_labels = lax.all_gather(labels, "items", axis=0, tiled=True)
    time_in, time_out, table, ada = (
        w.astype(single) for w in (time_in_weight, time_out_weight, label_table, ada_weight)
    )
    sinus = time_features(all_times, time_in_weight.shape[0] // 2)
    before = exact(sinus, time_in) + time_in_bias.astype(single)
    inner = jax.nn.silu(before)
    onehot = (all_labels[:, None] == jnp.arange(table.shape[1], dtype=jnp.int32)[None, :]).astype(
        single
    )
    cond = exact(inner, time_out) + time_out_bias.astype(single) + exact_nt(onehot, table)
    active = jax.nn.silu(cond)
    own_active = lax.dynamic_slice_in_dim(active, item * count, count, axis=0)
    modulation = exact(own_active, ada) + ada_bias.astype(single)
    shift_a, scale_a, gate_a, shift_b, scale_b, gate_b = (
        modulation[:, None, i * features : (i + 1) * features] for i in range(6)
    )

    ends = jnp.concatenate([latents[:, -1:], cotangent[:, -1:]], axis=1)
    starts = jnp.concatenate([latents[:, :1], cotangent[:, :1]], axis=1)
    above = from_above(ends)
    below = from_below(starts)

    down_taps = tap_rows(down_kernel)
    grouped, normed_a, kept = front(
        edge, latents, above[:, :1], below[:, :1], scale_a, shift_a, down_taps, row_vector(down_bias)
    )

    def spread(array):
        flat = array.reshape(groups, quarter, array.shape[-1])
        if share > 1:
            flat = jnp.repeat(flat, share, axis=0)
        got = lax.all_to_all(flat, "strips", 0, 0, tiled=True)
        return got.reshape(strips * quarter, array.shape[-1])

    def collect(array):
        flat = array.reshape(strips, quarter, array.shape[-1])
        return lax.all_to_all(flat, "strips", 0, 0, tiled=True)

    group = spread(grouped)
    g_kept, d_branch, grad_shrink_bias = upstream_parts(
        cotangent, above[:, 1:], below[:, 1:], gate_b
    )

    head_at = (strip % share) * width
    def own_columns(array, axis):
        return array if share == 1 else lax.dynamic_slice_in_dim(array, head_at, width, axis=axis)

    wq, wk, wv = (
        own_columns(input_weight[:, i * features : (i + 1) * features], 1) for i in range(3)
    )
    bq = own_columns(row_vector(query_bias), 1)
    bv = own_columns(row_vector(value_bias), 1)
    piece = width // CHUNKS
    saved = []
    mixed = []
    for c in range(CHUNKS):
        at = slice(c * piece, (c + 1) * piece)
        saved.append(attend(group, wq[:, at], wk[:, at], wv[:, at], bq[:, at], bv[:, at]))
        mixed.append(collect(saved[c][3]))
    if share == 1:
        mixed = [m.reshape(count, 4, quarter, piece) for m in mixed]
    else:
        joined = jnp.concatenate(mixed, axis=-1).reshape(groups, share, quarter, width)
        joined = joined.transpose(0, 2, 1, 3).reshape(count, 4, quarter, features)
        mixed = [joined]

    attended, middle, normed_b = middle_part(
        mixed, output_weight, row_vector(output_bias), kept, gate_a, scale_b, shift_b
    )
    branch, e, grad_shrink, grad_expand, feed_small = feed_forward(
        edge,
        normed_b,
        from_above(normed_b[:, -2:]),
        from_below(normed_b[:, :2]),
        d_branch,
        expand_weight,
        row_vector(expand_bias),
        tap_rows(mixer_kernel),
        row_vector(mixer_bias),
        shrink_weight,
    )
    turned = turn(
        branch, e, middle, attended, g_kept, gate_b, scale_b, gate_a, row_vector(shrink_bias),
        output_weight, mixed,
    )
    result, d_middle = turned[:2]
    d_mixed = turned[2:-2]
    grad_output, turn_sums = turned[-2:]

    hidden = expand_weight.shape[1]
    steps = hidden // features
    early = jnp.concatenate(
        [
            grad_shrink.reshape(devices, hidden // devices, features),
            grad_expand.reshape(steps, devices, features // devices, features)
            .transpose(1, 0, 2, 3)
            .reshape(devices, hidden // devices, features),
            grad_output.reshape(devices, features // devices, features),
        ],
        axis=1,
    )
    early_sum = lax.psum_scatter(early, both, scatter_dimension=0, tiled=False).astype(single)

    if share == 1:
        d_mixed = [spread(d) for d in d_mixed]
    else:
        parts = d_mixed[0].reshape(groups, quarter, share, width).transpose(0, 2, 1, 3)
        got = lax.all_to_all(parts.reshape(strips, quarter, width), "strips", 0, 0, tiled=True)
        got = got.reshape(strips * quarter, width)
        d_mixed = [got[:, c * piece : (c + 1) * piece] for c in range(CHUNKS)]
    grads = []
    for c in range(CHUNKS):
        q, k, v, out, logs = saved[c]
        grads.append(attend_back(q, k, v, out, d_mixed[c], logs))
    d_query, d_key, d_value = (
        jnp.concatenate([grads[c][i] for c in range(CHUNKS)], axis=1) for i in range(3)
    )
    d_projected = jnp.concatenate([d_query, d_key, d_value], axis=1)
    own_weight = jnp.concatenate([wq, wk, wv], axis=1)
    d_group = dot_nt(d_projected, own_weight).astype(bfloat)
    d_reduced = collect(d_group)
    if share > 1:
        d_reduced = jnp.sum(
            d_reduced.reshape(groups, share, quarter, features).astype(single), axis=1
        ).astype(bfloat)
    d_reduced = d_reduced.reshape(count, 4, quarter, features)
    grad_input = dot_tn(group, d_projected).astype(bfloat)
    d_query_sum = jnp.sum(d_query.astype(single), axis=0)
    d_value_sum = jnp.sum(d_value.astype(single), axis=0)
    if share > 1:
        zero = jnp.zeros((features, 3, features), bfloat)
        grad_input = lax.dynamic_update_slice(
            zero, grad_input.reshape(features, 3, width), (0, 0, head_at)
        ).reshape(features, 3 * features)
        flat = jnp.zeros((features,), single)
        d_query_sum = lax.dynamic_update_slice(flat, d_query_sum, (head_at,))
        d_value_sum = lax.dynamic_update_slice(flat, d_value_sum, (head_at,))
    late_sum = lax.psum_scatter(grad_input, both, scatter_dimension=0, tiled=True).astype(single)

    grad_latents, down_small, final_sums = final(
        d_reduced,
        from_above(d_reduced[:, 2:, -2 * sub :]),
        from_below(d_reduced[:, :2, : 2 * sub]),
        normed_a,
        kept,
        d_middle,
        scale_a,
        down_taps,
    )

    d_gate_b, d_shift_b, d_scale_b, d_gate_a, output_bias_part = (
        turn_sums[:, t] for t in range(5)
    )
    narrow = jnp.stack(
        [
            jnp.sum(output_bias_part, axis=0),
            jnp.sum(grad_shrink_bias[:, 0], axis=0),
            d_query_sum,
            d_value_sum,
        ]
    )
    narrow = jnp.concatenate([narrow, down_small[:10]], axis=0)
    small = jnp.concatenate(
        [
            feed_small[:11].reshape(11, devices, hidden // devices).transpose(1, 0, 2).reshape(devices, -1),
            narrow.reshape(14, devices, features // devices).transpose(1, 0, 2).reshape(devices, -1),
        ],
        axis=1,
    )
    small = jnp.sum(lax.all_to_all(small, both, 0, 0, tiled=True), axis=0)
    cut = 11 * (hidden // devices)
    feed_sum = small[:cut].reshape(11, hidden // devices)
    narrow_sum = small[cut:].reshape(14, features // devices)

    d_modulation = jnp.concatenate(
        [final_sums[:, 0], final_sums[:, 1], d_gate_a, d_shift_b, d_scale_b, d_gate_b], axis=1
    )
    d_modulation = jnp.sum(lax.all_gather(d_modulation, "strips", axis=0), axis=0)
    d_modulation = lax.all_gather(d_modulation, "items", axis=0, tiled=True)
    d_cond = exact_nt(d_modulation, ada) * silu_slope(cond)
    d_before = exact_nt(d_cond, time_out) * silu_slope(before)

    def mine(array):
        size = array.shape[-1] // devices
        return lax.dynamic_slice_in_dim(array, me * size, size, axis=array.ndim - 1)

    feed_rows = hidden // devices
    return (
        result,
        grad_latents,
        exact_tn(mine(sinus), d_before),
        jnp.sum(mine(d_before), axis=0),
        exact_tn(mine(inner), d_cond),
        jnp.sum(mine(d_cond), axis=0),
        exact_tn(mine(d_cond), onehot),
        exact_tn(mine(active), d_modulation),
        jnp.sum(mine(d_modulation), axis=0),
        narrow_sum[4:13].T,
        narrow_sum[13],
        late_sum,
        narrow_sum[2],
        narrow_sum[3],
        early_sum[2 * feed_rows :],
        narrow_sum[0],
        early_sum[feed_rows : 2 * feed_rows]
        .reshape(steps, features // devices, features)
        .transpose(1, 0, 2)
        .reshape(features // devices, hidden),
        feed_sum[10],
        feed_sum[:9].T,
        feed_sum[9],
        early_sum[:feed_rows],
        narrow_sum[1],
    )


def solution(mesh):
    image = P("items", "strips", None, None)
    split = P(both, None)
    line = P(both)
    return jax.shard_map(
        per_device,
        mesh=mesh,
        in_specs=(image, P("items"), P("items")) + (P(),) * 20 + (image,),
        out_specs=(
            image, image, split, line, split, line, split, split, line, split, line,
            split, line, line, split, line, split, line, split, line, split, line,
        ),
        check_vma=False,
    )
```

```python
from functools import partial
import math

import jax
import jax.numpy as jnp
from jax import lax
from jax.experimental import pallas as pl
from jax.experimental.pallas import tpu as pltpu
from jax.sharding import PartitionSpec as P

HEADS = 12
HEAD_DIM = 64
LANES = 128
COLUMN_PARTS = 4
CHUNKS = 2
VMEM_BYTES = 60 * 1024 * 1024

highest = lax.Precision.HIGHEST
epsilon = 1e-06
bfloat = jnp.bfloat16
single = jnp.float32
both = ("items", "strips")


def params():
    return pltpu.CompilerParams(vmem_limit_bytes=VMEM_BYTES)


def cost(flops, moved, exps=0):
    return pl.CostEstimate(flops=int(flops), bytes_accessed=int(moved), transcendentals=int(exps))


def dot(a, b):
    return lax.dot_general(a, b, (((1,), (0,)), ((), ())), preferred_element_type=single)


def dot_nt(a, b):
    return lax.dot_general(a, b, (((1,), (1,)), ((), ())), preferred_element_type=single)


def dot_tn(a, b):
    return lax.dot_general(a, b, (((0,), (0,)), ((), ())), preferred_element_type=single)


def column_order(columns, back):
    sub = columns // COLUMN_PARTS
    first = lax.broadcasted_iota(jnp.int32, (columns, columns), 0)
    second = lax.broadcasted_iota(jnp.int32, (columns, columns), 1)
    kept, column = (second, first) if back else (first, second)
    return (column == COLUMN_PARTS * (kept % sub) + kept // sub).astype(bfloat)


def norm_parts(value):
    center = value - jnp.mean(value, axis=-1, keepdims=True)
    inverse = lax.rsqrt(jnp.mean(center * center, axis=-1, keepdims=True) + epsilon)
    return center * inverse, inverse


def norm_back(normed, inverse, grad):
    return inverse * (
        grad
        - jnp.mean(grad, axis=-1, keepdims=True)
        - normed * jnp.mean(grad * normed, axis=-1, keepdims=True)
    )


def put_wide(ref, row, cells):
    sub = cells.shape[1]
    place = lax.broadcasted_iota(jnp.int32, cells.shape[1:], 0)
    ref[row, 1 : COLUMN_PARTS + 1] = cells
    ref[row, 0] = jnp.where(place == 0, 0.0, pltpu.roll(cells[COLUMN_PARTS - 1], 1, 0))
    ref[row, COLUMN_PARTS + 1] = jnp.where(
        place == sub - 1, 0.0, pltpu.roll(cells[0], sub - 1, 0)
    )


def conv_row(ref, row, taps, start):
    total = start
    for i in range(3):
        for j in range(3):
            total = total + taps[3 * i + j] * ref[row + i, j : j + COLUMN_PARTS]
    return total


def conv_back_row(ref, row, taps):
    total = None
    for i in range(3):
        for j in range(3):
            term = taps[3 * i + j] * ref[row + 2 - i, 2 - j : 2 - j + COLUMN_PARTS]
            total = term if total is None else total + term
    return total


def front_kernel(
    edge_ref, x_ref, top_ref, bottom_ref, scale_ref, shift_ref, taps_ref, bias_ref,
    grouped_ref, normed_ref, kept_ref, wide,
):
    rows, columns, features = x_ref.shape[1:]
    sub = columns // COLUMN_PARTS
    order = column_order(columns, False)
    scale = 1.0 + scale_ref[0]
    shift = shift_ref[0]

    def fill(row, raw, keep):
        cells = dot(order, raw)
        normed = (norm_parts(cells)[0] * scale + shift) * keep
        low = normed.astype(bfloat)
        normed_ref[0, row] = low
        put_wide(wide, row, low.astype(single).reshape(COLUMN_PARTS, sub, features))
        return cells

    fill(0, top_ref[0, 0], edge_ref[0])
    fill(rows + 1, bottom_ref[0, 0], edge_ref[1])

    @pl.loop(0, rows)
    def _(row):
        kept_ref[0, row] = fill(row + 1, x_ref[0, row], 1.0).astype(bfloat)

    taps = [taps_ref[t : t + 1] for t in range(9)]
    bias = bias_ref[...]

    @pl.loop(0, rows // 2)
    def _(pair):
        for a in range(2):
            for lane in range(0, features, LANES):
                at = pl.ds(lane, LANES)
                total = jnp.zeros((COLUMN_PARTS, sub, LANES), single) + bias[:, lane : lane + LANES]
                for i in range(3):
                    for j in range(3):
                        total = total + taps[3 * i + j][:, lane : lane + LANES] * wide[
                            pair * 2 + a + i, j : j + COLUMN_PARTS, :, at
                        ]
                low = total.astype(bfloat)
                for j in range(COLUMN_PARTS):
                    grouped_ref[
                        0, 2 * a + j % 2, pl.ds(pl.multiple_of((pair * 2 + j // 2) * sub, sub), sub), at
                    ] = low[j]


def front(edge, latents, top, bottom, scale, shift, taps, bias):
    count, rows, columns, features = latents.shape
    quarter = rows * columns // 4
    sub = columns // COLUMN_PARTS
    image = lambda r: pl.BlockSpec((1, r, columns, features), lambda l: (l, 0, 0, 0))
    vector = pl.BlockSpec((1, 1, features), lambda l: (l, 0, 0))
    return pl.pallas_call(
        front_kernel,
        grid=(count,),
        in_specs=[
            pl.BlockSpec(memory_space=pltpu.SMEM),
            image(rows), image(1), image(1), vector, vector,
            pl.BlockSpec((16, features), lambda l: (0, 0)),
            pl.BlockSpec((1, features), lambda l: (0, 0)),
        ],
        out_specs=[
            pl.BlockSpec((1, 4, quarter, features), lambda l: (l, 0, 0, 0)),
            image(rows + 2), image(rows),
        ],
        out_shape=[
            jax.ShapeDtypeStruct((count, 4, quarter, features), bfloat),
            jax.ShapeDtypeStruct((count, rows + 2, columns, features), bfloat),
            jax.ShapeDtypeStruct((count, rows, columns, features), bfloat),
        ],
        scratch_shapes=[pltpu.VMEM((rows + 2, COLUMN_PARTS + 2, sub, features), single)],
        compiler_params=params(),
        cost_estimate=cost(count * rows * columns * features * 150, count * rows * columns * features * 8),
        name="front",
    )(edge, latents, top, bottom, scale, shift, taps, bias)


def upstream_kernel(g_ref, top_ref, bottom_ref, gate_ref, kept_ref, branch_ref, bias_ref):
    rows, columns, features = g_ref.shape[1:]
    order = column_order(columns, False)
    gate = gate_ref[0]

    def low(raw):
        cells = dot(order, raw)
        return cells, (cells * gate).astype(bfloat)

    branch_ref[0, 0] = low(top_ref[0, 0])[1]
    branch_ref[0, rows + 1] = low(bottom_ref[0, 0])[1]

    def step(row, total):
        cells, grad = low(g_ref[0, row])
        kept_ref[0, row] = cells.astype(bfloat)
        branch_ref[0, row + 1] = grad
        return total + jnp.sum(grad.astype(single), axis=0, keepdims=True)

    bias_ref[0] = lax.fori_loop(0, rows, step, jnp.zeros((1, features), single))


def upstream_parts(cotangent, top, bottom, gate):
    count, rows, columns, features = cotangent.shape
    image = lambda r: pl.BlockSpec((1, r, columns, features), lambda l: (l, 0, 0, 0))
    vector = pl.BlockSpec((1, 1, features), lambda l: (l, 0, 0))
    return pl.pallas_call(
        upstream_kernel,
        grid=(count,),
        in_specs=[image(rows), image(1), image(1), vector],
        out_specs=[image(rows), image(rows + 2), vector],
        out_shape=[
            jax.ShapeDtypeStruct((count, rows, columns, features), bfloat),
            jax.ShapeDtypeStruct((count, rows + 2, columns, features), bfloat),
            jax.ShapeDtypeStruct((count, 1, features), single),
        ],
        compiler_params=params(),
        cost_estimate=cost(count * rows * columns * features * 130, count * rows * columns * features * 6),
        name="upstream",
    )(cotangent, top, bottom, gate)


QUERY_STEP = 512
QUERY_STEP_BACK = 256


def attend_kernel(
    x_ref, wq_ref, wk_ref, wv_ref, bq_ref, bv_ref, q_ref, k_ref, v_ref, mixed_ref, log_ref
):
    tokens = x_ref.shape[0]
    base = math.log2(math.e) / math.sqrt(HEAD_DIM)
    x = x_ref[...]
    q_ref[...] = (dot(x, wq_ref[...]) + bq_ref[...]).astype(bfloat)
    k_ref[...] = dot(x, wk_ref[...]).astype(bfloat)
    v_ref[...] = (dot(x, wv_ref[...]) + bv_ref[...]).astype(bfloat)
    keys = k_ref[...]
    values = v_ref[...].T
    lane = lax.broadcasted_iota(jnp.int32, (QUERY_STEP, LANES), 1)
    for at in range(0, tokens, QUERY_STEP):
        part = q_ref[at : at + QUERY_STEP]
        outs = []
        for head in range(LANES // HEAD_DIM):
            own = jnp.where(lane // HEAD_DIM == head, part, jnp.zeros_like(part))
            scores = dot_nt(keys, own)
            peak = jnp.max(scores, axis=0, keepdims=True) * base
            soft = jnp.exp2(scores * base - peak)
            total = jnp.sum(soft, axis=0, keepdims=True)
            log_ref[0, head : head + 1, at : at + QUERY_STEP] = peak + jnp.log2(total)
            out = dot(values[head * HEAD_DIM : (head + 1) * HEAD_DIM], soft.astype(bfloat))
            outs.append(out * (1.0 / total))
        mixed_ref[at : at + QUERY_STEP] = jnp.concatenate(outs, axis=0).T.astype(bfloat)


def attend(x, weights, biases, first, width):
    tokens, features = x.shape
    pairs = width // LANES
    start = first // LANES
    stride = weights.shape[1] // 3 // LANES
    weight = lambda i: pl.BlockSpec((features, LANES), lambda h: (0, i * stride + start + h))
    bias = lambda i: pl.BlockSpec((1, LANES), lambda h: (0, i * stride + start + h))
    column = pl.BlockSpec((tokens, LANES), lambda h: (0, h))
    lows = jax.ShapeDtypeStruct((tokens, width), bfloat)
    return pl.pallas_call(
        attend_kernel,
        grid=(pairs,),
        in_specs=[pl.BlockSpec((tokens, features), lambda h: (0, 0))]
        + [weight(0), weight(1), weight(2), bias(0), bias(1)],
        out_specs=[column] * 4 + [pl.BlockSpec((1, 2, tokens), lambda h: (h, 0, 0))],
        out_shape=[lows] * 4 + [jax.ShapeDtypeStruct((pairs, 2, tokens), single)],
        compiler_params=params(),
        cost_estimate=cost(
            6 * tokens * features * width + 16 * tokens * tokens * width,
            2 * tokens * features + 8 * tokens * width + 6 * features * width,
            2 * pairs * tokens * tokens,
        ),
        name="attend",
    )(x, weights, weights, weights, biases, biases)


def attend_back_kernel(
    q_ref, k_ref, v_ref, mixed_ref, grad_ref, log_ref, dq_ref, dk_ref, dv_ref, dk_sum, dv_sum
):
    tokens = q_ref.shape[0]
    scale = 1.0 / math.sqrt(HEAD_DIM)
    base = math.log2(math.e) * scale
    keys = k_ref[...]
    values = v_ref[...]
    keys_turned = keys.T
    lane = lax.broadcasted_iota(jnp.int32, (QUERY_STEP_BACK, LANES), 1)
    for at in range(0, tokens, QUERY_STEP_BACK):
        rows = slice(at, at + QUERY_STEP_BACK)
        part = q_ref[rows]
        grad = grad_ref[rows]
        shares = (grad.astype(single) * mixed_ref[rows].astype(single)).T
        outs = []
        for head in range(LANES // HEAD_DIM):
            mine = lane // HEAD_DIM == head
            own = jnp.where(mine, part, jnp.zeros_like(part))
            own_grad = jnp.where(mine, grad, jnp.zeros_like(grad))
            share = jnp.sum(
                shares[head * HEAD_DIM : (head + 1) * HEAD_DIM], axis=0, keepdims=True
            )
            soft = jnp.exp2(dot_nt(keys, own) * base - log_ref[0, head : head + 1, rows])
            d_scores = (soft * (dot_nt(values, own_grad) - share)).astype(bfloat)
            dv_part = dot(soft.astype(bfloat), own_grad)
            dk_part = dot(d_scores, own)
            if at == 0 and head == 0:
                dv_sum[...] = dv_part
                dk_sum[...] = dk_part
            else:
                dv_sum[...] += dv_part
                dk_sum[...] += dk_part
            outs.append(dot(keys_turned[head * HEAD_DIM : (head + 1) * HEAD_DIM], d_scores))
        dq_ref[rows] = (jnp.concatenate(outs, axis=0) * scale).T.astype(bfloat)
    dk_ref[...] = (dk_sum[...] * scale).astype(bfloat)
    dv_ref[...] = dv_sum[...].astype(bfloat)


def attend_back(q, k, v, mixed, grad, logs):
    tokens, width = q.shape
    pairs = width // LANES
    column = pl.BlockSpec((tokens, LANES), lambda h: (0, h))
    lows = jax.ShapeDtypeStruct((tokens, width), bfloat)
    return pl.pallas_call(
        attend_back_kernel,
        grid=(pairs,),
        in_specs=[column] * 5 + [pl.BlockSpec((1, 2, tokens), lambda h: (h, 0, 0))],
        out_specs=[column] * 3,
        out_shape=[lows] * 3,
        scratch_shapes=[pltpu.VMEM((tokens, LANES), single)] * 2,
        compiler_params=params(),
        cost_estimate=cost(
            40 * tokens * tokens * width, 16 * tokens * width, 2 * pairs * tokens * tokens
        ),
        name="attend_back",
    )(q, k, v, mixed, grad, logs)


def regroup_kernel(*refs):
    parts, weight_ref, out_ref = refs[:-2], refs[-2], refs[-1]
    count = len(parts) // 3
    piece = parts[0].shape[1]
    third = weight_ref.shape[1] // 3
    total = None
    for c in range(count):
        for i in range(3):
            at = i * third + c * piece
            term = dot_nt(parts[3 * c + i][...], weight_ref[:, at : at + piece])
            total = term if total is None else total + term
    out_ref[...] = total.astype(bfloat)


def regroup(parts, weight):
    tokens, piece = parts[0].shape
    features = weight.shape[0]
    step = min(256, tokens)
    return pl.pallas_call(
        regroup_kernel,
        grid=(tokens // step,),
        in_specs=[pl.BlockSpec((step, piece), lambda t: (t, 0))] * len(parts)
        + [pl.BlockSpec(weight.shape, lambda t: (0, 0))],
        out_specs=pl.BlockSpec((step, features), lambda t: (t, 0)),
        out_shape=jax.ShapeDtypeStruct((tokens, features), bfloat),
        compiler_params=params(),
        cost_estimate=cost(2 * tokens * features * weight.shape[1], 2 * tokens * features * 4),
        name="regroup",
    )(*parts, weight)


def input_grad_kernel(*refs):
    x_ref, other_ref = refs[0], refs[1]
    parts = refs[2:-2]
    out_ref, sums_ref = refs[-2:]
    count = len(parts) // 3
    tokens, piece = parts[0].shape
    third = count * piece
    turned = x_ref[...].T
    for c in range(count):
        for i in range(3):
            at = i * third + c * piece
            out_ref[:, at : at + piece] = dot(turned, parts[3 * c + i][...]).astype(bfloat)
    out_ref[:, 3 * third :] = other_ref[...]

    @pl.when(pl.program_id(0) == 0)
    def _():
        ones = jnp.ones((16, tokens), bfloat)
        for c in range(count):
            for i in (0, 2):
                total = dot(ones, parts[3 * c + i][...])
                sums_ref[:, i // 2 * third + c * piece : i // 2 * third + (c + 1) * piece] = total[:8]


def input_grad(x, other, parts):
    tokens, features = x.shape
    piece = parts[0].shape[1]
    third = piece * len(parts) // 3
    step = 256
    return pl.pallas_call(
        input_grad_kernel,
        grid=(features // step,),
        in_specs=[
            pl.BlockSpec((tokens, step), lambda t: (0, t)),
            pl.BlockSpec((step, other.shape[1]), lambda t: (t, 0)),
        ]
        + [pl.BlockSpec((tokens, piece), lambda t: (0, 0))] * len(parts),
        out_specs=[
            pl.BlockSpec((step, 3 * third + other.shape[1]), lambda t: (t, 0)),
            pl.BlockSpec((8, 2 * third), lambda t: (0, 0)),
        ],
        out_shape=[
            jax.ShapeDtypeStruct((features, 3 * third + other.shape[1]), bfloat),
            jax.ShapeDtypeStruct((8, 2 * third), single),
        ],
        compiler_params=params(),
        cost_estimate=cost(6 * tokens * features * third, 2 * tokens * features * 5),
        name="input_grad",
    )(x, other, *parts)


def middle_kernel(
    parts, *refs
):
    mixed_refs = refs[:parts]
    weight_ref, bias_ref, x_ref, gate_ref, scale_ref, shift_ref = refs[parts : parts + 6]
    attended_ref, middle_ref, normed_ref, grouped = refs[parts + 6 :]
    rows, columns, features = x_ref.shape[1:]
    sub = columns // COLUMN_PARTS
    quarter = rows * columns // 4
    total = bias_ref[...]
    at = 0
    for ref in mixed_refs:
        width = ref.shape[-1]
        total = total + dot(ref[0].reshape(4 * quarter, width), weight_ref[at : at + width])
        at += width
    grouped[...] = total.reshape(4, quarter, features)
    gate = gate_ref[0]
    scale = 1.0 + scale_ref[0]
    shift = shift_ref[0]

    @pl.loop(0, rows // 2)
    def _(pair):
        for a in range(2):
            row = pair * 2 + a
            cells = jnp.concatenate(
                [
                    grouped[2 * a + j % 2, pl.ds(pl.multiple_of((pair * 2 + j // 2) * sub, sub), sub)]
                    for j in range(COLUMN_PARTS)
                ],
                axis=0,
            )
            attended_ref[0, row] = cells
            middle = x_ref[0, row].astype(single) + gate * cells
            middle_ref[0, row] = middle
            normed_ref[0, row] = (norm_parts(middle)[0] * scale + shift).astype(bfloat)


def middle_part(mixed, weight, bias, kept, gate, scale, shift):
    count, rows, columns, features = kept.shape
    quarter = rows * columns // 4
    image = pl.BlockSpec((1, rows, columns, features), lambda l: (l, 0, 0, 0))
    vector = pl.BlockSpec((1, 1, features), lambda l: (l, 0, 0))
    return pl.pallas_call(
        partial(middle_kernel, len(mixed)),
        grid=(count,),
        in_specs=[
            pl.BlockSpec((1, 4, quarter, m.shape[-1]), lambda l: (l, 0, 0, 0)) for m in mixed
        ]
        + [
            pl.BlockSpec((features, features), lambda l: (0, 0)),
            pl.BlockSpec((1, features), lambda l: (0, 0)),
            image, vector, vector, vector,
        ],
        out_specs=[image] * 3,
        out_shape=[
            jax.ShapeDtypeStruct(kept.shape, single),
            jax.ShapeDtypeStruct(kept.shape, single),
            jax.ShapeDtypeStruct(kept.shape, bfloat),
        ],
        scratch_shapes=[pltpu.VMEM((4, quarter, features), single)],
        compiler_params=params(),
        cost_estimate=cost(2 * kept.size * features, 14 * kept.size),
        name="middle",
    )(*mixed, weight, bias, kept, gate, scale, shift)


def feed_upstream_kernel(db_ref, ws_ref, out_ref):
    out_ref[...] = dot_nt(db_ref[...], ws_ref[...]).astype(bfloat)


def feed_upstream(db, ws):
    count, tall, columns, features = db.shape
    hidden = ws.shape[0]
    lines = count * tall * columns
    return pl.pallas_call(
        feed_upstream_kernel,
        grid=(hidden // features,),
        in_specs=[
            pl.BlockSpec((lines, features), lambda s: (0, 0)),
            pl.BlockSpec((features, features), lambda s: (s, 0)),
        ],
        out_specs=pl.BlockSpec((lines, features), lambda s: (0, s)),
        out_shape=jax.ShapeDtypeStruct((lines, hidden), bfloat),
        compiler_params=params(),
        cost_estimate=cost(2 * lines * features * hidden, 2 * lines * (features + hidden)),
        name="feed_upstream",
    )(db.reshape(lines, features), ws)


def feed_kernel(
    edge_ref, nb_ref, top_ref, bottom_ref, d_act_ref, we_ref, be_ref, ws_ref, taps_ref, bm_ref,
    branch_ref, e_ref, act_ref, d_hid_ref, small_ref,
    nb_wide, hidden, wide, d_wide,
):
    count, rows, columns, features = nb_ref.shape
    sub = columns // COLUMN_PARTS
    block = we_ref.shape[1]
    own = rows * columns
    tall = (rows + 4) * columns
    mid = (rows + 2) * columns

    @pl.when(pl.program_id(0) == 0)
    def _():
        for l in range(count):
            nb_wide[l * tall : l * tall + 2 * columns] = top_ref[l].reshape(2 * columns, features)
            nb_wide[l * tall + 2 * columns : (l + 1) * tall - 2 * columns] = nb_ref[l].reshape(
                own, features
            )
            nb_wide[(l + 1) * tall - 2 * columns : (l + 1) * tall] = bottom_ref[l].reshape(
                2 * columns, features
            )
        branch_ref[...] = jnp.zeros_like(branch_ref)
        e_ref[...] = jnp.zeros_like(e_ref)

    hidden[...] = (dot(nb_wide[...], we_ref[...]) + be_ref[...]).astype(bfloat)
    small_ref[...] = jnp.zeros_like(small_ref)

    c0 = math.sqrt(2.0 / math.pi)
    c1 = c0 * 0.044715

    @pl.loop(0, count * (block // LANES))
    def _(index):
        l = index // (block // LANES)
        at = pl.ds(pl.multiple_of((index % (block // LANES)) * LANES, LANES), LANES)
        taps = [taps_ref[t : t + 1, at] for t in range(9)]
        bias = bm_ref[:, at]
        for row in range(rows + 4):
            cells = hidden[pl.ds(pl.multiple_of(l * tall + row * columns, columns), columns), at]
            cells = cells.astype(single)
            if row < 2:
                cells = cells * edge_ref[0]
            if row >= rows + 2:
                cells = cells * edge_ref[1]
            put_wide(wide, row, cells.reshape(COLUMN_PARTS, sub, LANES))
        start = jnp.zeros((COLUMN_PARTS, sub, LANES), single) + bias
        for row in range(rows + 2):
            v = conv_row(wide, row, taps, start)
            cube = (v * v) * c1
            half = 0.5 * jnp.tanh(v * (cube + c0)) + 0.5
            gelu = v * half
            slope = half + gelu * (1.0 - half) * (6.0 * cube + 2.0 * c0)
            if 1 <= row <= rows:
                act_ref[
                    pl.ds(pl.multiple_of(l * own + (row - 1) * columns, columns), columns), at
                ] = gelu.reshape(columns, LANES).astype(bfloat)
            grad = d_act_ref[pl.ds(pl.multiple_of(l * mid + row * columns, columns), columns), at]
            grad = grad.astype(single).reshape(COLUMN_PARTS, sub, LANES) * slope
            put_wide(d_wide, row, grad.astype(bfloat).astype(single))
        sums = [jnp.zeros((sub, LANES), single) for _ in range(11)]
        for row in range(rows):
            d_in = conv_back_row(d_wide, row, taps).astype(bfloat)
            d_hid_ref[pl.ds(pl.multiple_of(l * own + row * columns, columns), columns), at] = (
                d_in.reshape(columns, LANES)
            )
            center = d_wide[row + 1, 1 : COLUMN_PARTS + 1]
            for i in range(3):
                for j in range(3):
                    sums[3 * i + j] += jnp.sum(
                        center * wide[row + 1 + i, j : j + COLUMN_PARTS], axis=0
                    )
            sums[9] += jnp.sum(center, axis=0)
            sums[10] += jnp.sum(d_in.astype(single), axis=0)
        for t in range(11):
            small_ref[t : t + 1, at] += jnp.sum(sums[t], axis=0, keepdims=True)

    branch_ref[...] += dot(act_ref[...], ws_ref[...])
    e_ref[...] += dot_nt(d_hid_ref[...], we_ref[...])


def feed_forward(edge, nb, top, bottom, d_act, we, be, taps, bm, ws):
    count, rows, columns, features = nb.shape
    hidden = we.shape[1]
    block = features
    steps = hidden // block
    tokens = count * rows * columns
    tall = count * (rows + 4) * columns
    mid = count * (rows + 2) * columns
    sub = columns // COLUMN_PARTS
    whole = lambda a: pl.BlockSpec(a.shape, lambda s: (0,) * a.ndim)
    column = lambda n: pl.BlockSpec((n, block), lambda s: (0, s))
    flat = pl.BlockSpec((tokens, features), lambda s: (0, 0))
    return pl.pallas_call(
        feed_kernel,
        grid=(steps,),
        in_specs=[
            pl.BlockSpec(memory_space=pltpu.SMEM),
            whole(nb), whole(top), whole(bottom),
            column(mid), column(features), column(1),
            pl.BlockSpec((block, features), lambda s: (s, 0)),
            column(16), column(1),
        ],
        out_specs=[flat, flat, column(tokens), column(tokens), column(16)],
        out_shape=[
            jax.ShapeDtypeStruct((tokens, features), single),
            jax.ShapeDtypeStruct((tokens, features), single),
            jax.ShapeDtypeStruct((tokens, hidden), bfloat),
            jax.ShapeDtypeStruct((tokens, hidden), bfloat),
            jax.ShapeDtypeStruct((16, hidden), single),
        ],
        scratch_shapes=[
            pltpu.VMEM((tall, features), bfloat),
            pltpu.VMEM((tall, block), bfloat),
            pltpu.VMEM((rows + 4, COLUMN_PARTS + 2, sub, LANES), single),
            pltpu.VMEM((rows + 2, COLUMN_PARTS + 2, sub, LANES), single),
        ],
        compiler_params=params(),
        cost_estimate=cost(
            2 * features * hidden * (tall + 2 * tokens),
            8 * tokens * features + 8 * features * hidden + 6 * tokens * hidden,
            mid * hidden,
        ),
        name="feed_forward",
    )(edge, nb, top, bottom, d_act, we, be, ws, taps, bm)


def feed_grads_kernel(act_ref, d_hid_ref, nb_ref, db_ref, gws_ref, gwe_ref, db_own):
    count, rows, columns, features = nb_ref.shape
    own = rows * columns

    @pl.when(pl.program_id(0) == 0)
    def _():
        for l in range(count):
            db_own[l * own : (l + 1) * own] = db_ref[l, 1 : rows + 1].reshape(own, features)

    gws_ref[...] = dot_tn(act_ref[...], db_own[...]).astype(bfloat)
    gwe_ref[0] = dot_tn(nb_ref[...].reshape(count * own, features), d_hid_ref[...]).astype(bfloat)


def feed_grads(act, d_hid, nb, db):
    count, rows, columns, features = nb.shape
    tokens, hidden = act.shape
    block = features
    steps = hidden // block
    whole = lambda a: pl.BlockSpec(a.shape, lambda s: (0,) * a.ndim)
    return pl.pallas_call(
        feed_grads_kernel,
        grid=(steps,),
        in_specs=[
            pl.BlockSpec((tokens, block), lambda s: (0, s)),
            pl.BlockSpec((tokens, block), lambda s: (0, s)),
            whole(nb), whole(db),
        ],
        out_specs=[
            pl.BlockSpec((block, features), lambda s: (s, 0)),
            pl.BlockSpec((1, features, block), lambda s: (s, 0, 0)),
        ],
        out_shape=[
            jax.ShapeDtypeStruct((hidden, features), bfloat),
            jax.ShapeDtypeStruct((steps, features, block), bfloat),
        ],
        scratch_shapes=[pltpu.VMEM((tokens, features), bfloat)],
        compiler_params=params(),
        cost_estimate=cost(4 * features * hidden * tokens, 8 * features * hidden + 4 * tokens * hidden),
        name="feed_grads",
    )(act, d_hid, nb, db)


def turn_kernel(parts, *refs):
    (
        branch_ref, e_ref, middle_ref, attended_ref, g_ref,
        gate_b_ref, scale_ref, gate_a_ref, bias_ref, weight_ref,
    ) = refs[:10]
    mixed_refs = refs[10 : 10 + parts]
    result_ref, d_middle_ref = refs[10 + parts : 12 + parts]
    d_mixed_refs = refs[12 + parts : 12 + 2 * parts]
    gw_ref, sums_ref, gw_sum, grouped = refs[12 + 2 * parts :]
    rows, columns, features = g_ref.shape[1:]
    sub = columns // COLUMN_PARTS
    quarter = rows * columns // 4
    back = column_order(columns, True)
    gate_b = gate_b_ref[0]
    scale = 1.0 + scale_ref[0]
    gate_a = gate_a_ref[0]

    def step(pair, sums):
        for a in range(2):
            row = pair * 2 + a
            at = pl.ds(pl.multiple_of(row * columns, columns), columns)
            branch = branch_ref[at] + bias_ref[...]
            middle = middle_ref[0, row]
            g = g_ref[0, row].astype(single)
            result = (middle + gate_b * branch).astype(bfloat)
            result_ref[0, row] = dot(back, result).astype(bfloat)
            normed, inverse = norm_parts(middle)
            e = e_ref[at]
            d_middle = g + norm_back(normed, inverse, e * scale)
            d_middle_ref[0, row] = d_middle
            low = (d_middle * gate_a).astype(bfloat)
            for j in range(COLUMN_PARTS):
                grouped[
                    2 * a + j % 2, pl.ds(pl.multiple_of((pair * 2 + j // 2) * sub, sub), sub)
                ] = low[j * sub : (j + 1) * sub]
            terms = (g * branch, e, e * normed, d_middle * attended_ref[0, row], low.astype(single))
            sums = tuple(
                s + jnp.sum(t.reshape(columns // 8, 8, features), axis=0) for s, t in zip(sums, terms)
            )
        return sums

    sums = lax.fori_loop(
        0, rows // 2, step, tuple(jnp.zeros((8, features), single) for _ in range(5))
    )
    for t in range(5):
        sums_ref[0, t : t + 1] = jnp.sum(sums[t], axis=0, keepdims=True)
    sums_ref[0, 5:8] = jnp.zeros((3, features), single)
    grad = grouped[...].reshape(4 * quarter, features)
    at = 0
    for mixed_ref, d_ref in zip(mixed_refs, d_mixed_refs):
        width = mixed_ref.shape[-1]
        piece = slice(at, at + width)
        d_ref[0] = dot_nt(grad, weight_ref[piece]).astype(bfloat).reshape(4, quarter, width)
        part = dot_tn(mixed_ref[0].reshape(4 * quarter, width), grad)

        @pl.when(pl.program_id(0) == 0)
        def _():
            gw_sum[piece] = part

        @pl.when(pl.program_id(0) > 0)
        def _():
            gw_sum[piece] += part

        at += width

    @pl.when(pl.program_id(0) == pl.num_programs(0) - 1)
    def _():
        gw_ref[...] = gw_sum[...].astype(bfloat)


def turn(branch, e, middle, attended, g, gate_b, scale, gate_a, bias, weight, mixed):
    count, rows, columns, features = g.shape
    quarter = rows * columns // 4
    own = rows * columns
    image = pl.BlockSpec((1, rows, columns, features), lambda l: (l, 0, 0, 0))
    flat = pl.BlockSpec((own, features), lambda l: (l, 0))
    vector = pl.BlockSpec((1, 1, features), lambda l: (l, 0, 0))
    groups = [pl.BlockSpec((1, 4, quarter, m.shape[-1]), lambda l: (l, 0, 0, 0)) for m in mixed]
    square = pl.BlockSpec((features, features), lambda l: (0, 0))
    return pl.pallas_call(
        partial(turn_kernel, len(mixed)),
        grid=(count,),
        in_specs=[flat, flat, image, image, image, vector, vector, vector]
        + [pl.BlockSpec((1, features), lambda l: (0, 0)), square]
        + groups,
        out_specs=[image, image] + groups + [square, pl.BlockSpec((1, 8, features), lambda l: (l, 0, 0))],
        out_shape=[
            jax.ShapeDtypeStruct(g.shape, bfloat),
            jax.ShapeDtypeStruct(g.shape, single),
        ]
        + [jax.ShapeDtypeStruct(m.shape, bfloat) for m in mixed]
        + [
            jax.ShapeDtypeStruct((features, features), bfloat),
            jax.ShapeDtypeStruct((count, 8, features), single),
        ],
        scratch_shapes=[
            pltpu.VMEM((features, features), single),
            pltpu.VMEM((4, quarter, features), bfloat),
        ],
        compiler_params=params(),
        cost_estimate=cost(4 * g.size * features, 26 * g.size),
        name="turn",
    )(branch, e, middle, attended, g, gate_b, scale, gate_a, bias, weight, *mixed)


def final_kernel(
    d_ref, top_ref, bottom_ref, normed_ref, x_ref, d_middle_ref, scale_ref, taps_ref,
    out_ref, taps_out_ref, sums_ref, wide, d_wide,
):
    rows, columns, features = x_ref.shape[1:]
    sub = columns // COLUMN_PARTS
    back = column_order(columns, True)
    scale = 1.0 + scale_ref[0]

    def piece(ref, a, start):
        parts = [
            ref[0, 2 * a + j % 2, pl.ds(pl.multiple_of(start + (j // 2) * sub, sub), sub)]
            for j in range(COLUMN_PARTS)
        ]
        return jnp.stack(parts, axis=0).astype(single)

    def halo(ref):
        parts = [
            ref[0, j % 2, pl.ds((j // 2) * sub, sub)] for j in range(COLUMN_PARTS)
        ]
        return jnp.stack(parts, axis=0).astype(single)

    put_wide(d_wide, 0, halo(top_ref))
    put_wide(d_wide, rows + 1, halo(bottom_ref))

    @pl.loop(0, rows // 2)
    def _(pair):
        for a in range(2):
            put_wide(d_wide, pair * 2 + a + 1, piece(d_ref, a, pair * 2 * sub))

    @pl.loop(0, rows + 2)
    def _(row):
        put_wide(wide, row, normed_ref[0, row].astype(single).reshape(COLUMN_PARTS, sub, features))

    @pl.when(pl.program_id(0) == 0)
    def _():
        taps_out_ref[...] = jnp.zeros_like(taps_out_ref)

    d_normed = wide
    for lane in range(0, features, LANES):
        at = pl.ds(lane, LANES)
        taps = [taps_ref[t : t + 1, at] for t in range(9)]

        def step(row, sums):
            total = None
            center = d_wide[row + 1, 1 : COLUMN_PARTS + 1, :, at]
            sums = list(sums)
            for i in range(3):
                for j in range(3):
                    term = taps[3 * i + j] * d_wide[row + 2 - i, 2 - j : 2 - j + COLUMN_PARTS, :, at]
                    total = term if total is None else total + term
                    sums[3 * i + j] = sums[3 * i + j] + jnp.sum(
                        center * wide[row + i, j : j + COLUMN_PARTS, :, at], axis=0
                    )
            sums[9] = sums[9] + jnp.sum(center, axis=0)
            d_normed[row, 1 : COLUMN_PARTS + 1, :, at] = total
            return tuple(sums)

        sums = lax.fori_loop(
            0, rows, step, tuple(jnp.zeros((sub, LANES), single) for _ in range(10))
        )
        for t in range(10):
            taps_out_ref[t : t + 1, at] += jnp.sum(sums[t], axis=0, keepdims=True)

    def last(row, sums):
        cells = d_normed[row, 1 : COLUMN_PARTS + 1].reshape(columns, features)
        normed, inverse = norm_parts(x_ref[0, row].astype(single))
        grad = d_middle_ref[0, row] + norm_back(normed, inverse, cells * scale)
        out_ref[0, row] = dot(back, grad.astype(bfloat)).astype(bfloat)
        return tuple(
            s + jnp.sum(t.reshape(columns // 8, 8, features), axis=0)
            for s, t in zip(sums, (cells, cells * normed))
        )

    sums = lax.fori_loop(0, rows, last, tuple(jnp.zeros((8, features), single) for _ in range(2)))
    for t in range(2):
        sums_ref[0, t : t + 1] = jnp.sum(sums[t], axis=0, keepdims=True)
    sums_ref[0, 2:8] = jnp.zeros((6, features), single)


def final(d_reduced, top, bottom, normed, kept, d_middle, scale, taps):
    count, rows, columns, features = kept.shape
    quarter = rows * columns // 4
    sub = columns // COLUMN_PARTS
    image = lambda r: pl.BlockSpec((1, r, columns, features), lambda l: (l, 0, 0, 0))
    vector = pl.BlockSpec((1, 1, features), lambda l: (l, 0, 0))
    side = pl.BlockSpec((1, 2, 2 * sub, features), lambda l: (l, 0, 0, 0))
    return pl.pallas_call(
        final_kernel,
        grid=(count,),
        in_specs=[
            pl.BlockSpec((1, 4, quarter, features), lambda l: (l, 0, 0, 0)),
            side, side, image(rows + 2), image(rows), image(rows), vector,
            pl.BlockSpec((16, features), lambda l: (0, 0)),
        ],
        out_specs=[
            image(rows),
            pl.BlockSpec((16, features), lambda l: (0, 0)),
            pl.BlockSpec((1, 8, features), lambda l: (l, 0, 0)),
        ],
        out_shape=[
            jax.ShapeDtypeStruct(kept.shape, bfloat),
            jax.ShapeDtypeStruct((16, features), single),
            jax.ShapeDtypeStruct((count, 8, features), single),
        ],
        scratch_shapes=[pltpu.VMEM((rows + 2, COLUMN_PARTS + 2, sub, features), single)] * 2,
        compiler_params=params(),
        cost_estimate=cost(kept.size * 180, kept.size * 12),
        name="final",
    )(d_reduced, top, bottom, normed, kept, d_middle, scale, taps)


def from_above(tail):
    count = lax.axis_size("strips")
    return lax.ppermute(tail, "strips", [(i, i + 1) for i in range(count - 1)])


def from_below(head):
    count = lax.axis_size("strips")
    return lax.ppermute(head, "strips", [(i + 1, i) for i in range(count - 1)])


def time_features(timesteps, halves):
    frequency = jnp.exp(-math.log(10000.0) * jnp.arange(halves, dtype=jnp.float32) / halves)
    phase = timesteps.astype(jnp.float32)[:, None] * frequency[None, :]
    return jnp.concatenate([jnp.cos(phase), jnp.sin(phase)], axis=1)


def thirds(value):
    high = value.astype(bfloat)
    rest = value - high.astype(single)
    middle = rest.astype(bfloat)
    low = (rest - middle.astype(single)).astype(bfloat)
    return jnp.concatenate([high, middle, low], axis=0)


def exact(value, weight, nt=False):
    n = value.shape[0]
    out = (dot_nt if nt else dot)(thirds(value), weight)
    return out[:n] + out[n : 2 * n] + out[2 * n :]


def silu(value):
    return value * (1.0 / (1.0 + jnp.exp(-value)))


def silu_slope(value):
    gate = 1.0 / (1.0 + jnp.exp(-value))
    return gate * (1.0 + value * (1.0 - gate))


def label_rows(labels, classes):
    return (lax.broadcasted_iota(jnp.int32, (labels.shape[0], classes), 1) == labels).astype(bfloat)


def condition(sinus, labels, wi_ref, bi_ref, wo_ref, bo_ref, table_ref):
    before = exact(sinus, wi_ref[...]) + bi_ref[...]
    inner = silu(before)
    onehot = label_rows(labels, table_ref.shape[1])
    cond = exact(inner, wo_ref[...]) + bo_ref[...] + dot_nt(onehot, table_ref[...])
    return before, inner, cond


def modulate_kernel(
    sinus_ref, label_ref, wi_ref, bi_ref, wo_ref, bo_ref, table_ref, ada_ref, ab_ref, out_ref, active
):
    @pl.when(pl.program_id(0) == 0)
    def _():
        cond = condition(
            sinus_ref[...], label_ref[...], wi_ref, bi_ref, wo_ref, bo_ref, table_ref
        )[2]
        active[...] = silu(cond)

    out_ref[0] = exact(active[...], ada_ref[...]) + ab_ref[...]


def modulate(sinus, labels, weights, ada, ada_bias):
    n = sinus.shape[0]
    features = ada.shape[0]
    whole = lambda a: pl.BlockSpec(a.shape, lambda s: (0,) * a.ndim)
    return pl.pallas_call(
        modulate_kernel,
        grid=(6,),
        in_specs=[whole(a) for a in (sinus, labels) + weights]
        + [
            pl.BlockSpec((features, features), lambda s: (0, s)),
            pl.BlockSpec((1, features), lambda s: (0, s)),
        ],
        out_specs=pl.BlockSpec((1, n, features), lambda s: (s, 0, 0)),
        out_shape=jax.ShapeDtypeStruct((6, n, features), single),
        scratch_shapes=[pltpu.VMEM((n, features), single)],
        compiler_params=params(),
        cost_estimate=cost(50 * n * ada.size, 2 * ada.size),
        name="modulate",
    )(sinus, labels, *weights, ada, ada_bias)


def own_rows(me_ref, value, size):
    width = value.shape[1]
    place = lax.broadcasted_iota(jnp.int32, (size, width), 1)
    line = lax.broadcasted_iota(jnp.int32, (size, width), 0)
    pick = (place == me_ref[0] * size + line).astype(single)
    return lax.dot_general(
        pick, value, (((1,), (1,)), ((), ())), precision=highest, preferred_element_type=single
    )


def exact_small(a, b):
    return lax.dot_general(
        a, b, (((1,), (0,)), ((), ())), precision=highest, preferred_element_type=single
    )


def strip_sum(ref, kinds, count, features):
    lines = []
    for item in range(ref.shape[0]):
        for l in range(count):
            at = l * kinds * features
            lines.append(jnp.sum(ref[item, :, at : at + kinds * features], axis=0, keepdims=True))
    return jnp.concatenate(lines, axis=0)


def early_kernel(
    count, me_ref, parts_ref, sinus_ref, label_ref, wi_ref, bi_ref, wo_ref, bo_ref, table_ref, ada_ref,
    before_ref, cond_ref, d_active_ref, ada_out_ref, d_mod_ref,
):
    features = ada_ref.shape[0]
    d_mod = strip_sum(parts_ref, 4, count, features)
    before, _, cond = condition(
        sinus_ref[...], label_ref[...], wi_ref, bi_ref, wo_ref, bo_ref, table_ref
    )
    before_ref[...] = before
    cond_ref[...] = cond
    d_active_ref[...] = exact(d_mod, ada_ref[:, 2 * features :], nt=True)
    size = ada_out_ref.shape[0]
    ada_out_ref[...] = exact_small(own_rows(me_ref, silu(cond), size), d_mod)
    d_mod_ref[...] = jnp.sum(d_mod, axis=0, keepdims=True)


def early_condition(me, parts, count, sinus, labels, weights, ada, size):
    n = sinus.shape[0]
    features = ada.shape[0]
    whole = lambda a: pl.BlockSpec(a.shape, lambda s: (0,) * a.ndim)
    shapes = [
        jax.ShapeDtypeStruct((n, features), single),
        jax.ShapeDtypeStruct((n, features), single),
        jax.ShapeDtypeStruct((n, features), single),
        jax.ShapeDtypeStruct((size, 4 * features), single),
        jax.ShapeDtypeStruct((1, 4 * features), single),
    ]
    return pl.pallas_call(
        partial(early_kernel, count),
        grid=(1,),
        in_specs=[pl.BlockSpec(memory_space=pltpu.SMEM)]
        + [whole(a) for a in (parts, sinus, labels) + weights + (ada,)],
        out_specs=[whole(a) for a in shapes],
        out_shape=shapes,
        compiler_params=params(),
        cost_estimate=cost(50 * n * ada.size, 2 * ada.size),
        name="early_condition",
    )(me, parts, sinus, labels, *weights, ada)


def late_kernel(
    count, me_ref, parts_ref, before_ref, cond_ref, d_active_ref, sinus_ref, label_ref,
    wo_ref, ada_ref,
    ada_out_ref, d_mod_ref, table_out_ref, wo_out_ref, wi_out_ref, d_cond_ref, d_before_ref,
):
    features = wo_ref.shape[0]
    before = before_ref[...]
    cond = cond_ref[...]
    d_mod = strip_sum(parts_ref, 2, count, features)
    d_active = d_active_ref[...] + exact(d_mod, ada_ref[...], nt=True)
    d_cond = d_active * silu_slope(cond)
    d_before = exact(d_cond, wo_ref[...], nt=True) * silu_slope(before)
    size = ada_out_ref.shape[0]
    ada_out_ref[...] = exact_small(own_rows(me_ref, silu(cond), size), d_mod)
    d_mod_ref[...] = jnp.sum(d_mod, axis=0, keepdims=True)
    onehot = label_rows(label_ref[...], table_out_ref.shape[1]).astype(single)
    table_out_ref[...] = exact_small(own_rows(me_ref, d_cond, size), onehot)
    wo_out_ref[...] = exact_small(own_rows(me_ref, silu(before), size), d_cond)
    wi_out_ref[...] = exact_small(
        own_rows(me_ref, sinus_ref[...], wi_out_ref.shape[0]), d_before
    )
    d_cond_ref[...] = jnp.sum(d_cond, axis=0, keepdims=True)
    d_before_ref[...] = jnp.sum(d_before, axis=0, keepdims=True)


def late_condition(me, parts, count, before, cond, d_active, sinus, labels, wo, ada, classes, devices):
    features = ada.shape[0]
    size = features // devices
    whole = lambda a: pl.BlockSpec(a.shape, lambda s: (0,) * a.ndim)
    shapes = [
        jax.ShapeDtypeStruct((size, 2 * features), single),
        jax.ShapeDtypeStruct((1, 2 * features), single),
        jax.ShapeDtypeStruct((size, classes), single),
        jax.ShapeDtypeStruct((size, features), single),
        jax.ShapeDtypeStruct((sinus.shape[1] // devices, features), single),
        jax.ShapeDtypeStruct((1, features), single),
        jax.ShapeDtypeStruct((1, features), single),
    ]
    return pl.pallas_call(
        partial(late_kernel, count),
        grid=(1,),
        in_specs=[pl.BlockSpec(memory_space=pltpu.SMEM)]
        + [whole(a) for a in (parts, before, cond, d_active, sinus, labels, wo)]
        + [pl.BlockSpec((features, 2 * features), lambda s: (0, 0))],
        out_specs=[whole(a) for a in shapes],
        out_shape=shapes,
        compiler_params=params(),
        cost_estimate=cost(20 * ada.size, ada.size),
        name="late_condition",
    )(me, parts, before, cond, d_active, sinus, labels, wo, ada)


def sum_cores(halves):
    strips = lax.axis_size("strips")
    core = lax.axis_index("strips") % 2
    got = lax.ppermute(halves(1 - core), "strips", [(i, i ^ 1) for i in range(strips)])
    return (halves(core).astype(single) + got.astype(single)).astype(bfloat)


def sum_axis(part, axis, size, place, step):
    pick = lambda k: lax.dynamic_index_in_dim(part, place ^ k, 0, keepdims=False)
    count = lax.axis_size(axis)
    got = [
        lax.ppermute(pick(k), axis, [(i, i ^ (k * step)) for i in range(count)])
        for k in range(1, size)
    ]
    total = pick(0).astype(single)
    for g in got:
        total = total + g.astype(single)
    return total


def sum_items(part):
    return sum_axis(part, "items", lax.axis_size("items"), lax.axis_index("items"), 1).astype(bfloat)


def sum_strips(part):
    strip = lax.axis_index("strips")
    return sum_axis(part, "strips", lax.axis_size("strips") // 2, strip // 2, 2)


def after(value, *others):
    return lax.optimization_barrier((value,) + others)[0]


def tap_rows(kernel):
    return jnp.pad(kernel.astype(single).T, ((0, 7), (0, 0)))


def per_device(
    latents,
    timesteps,
    labels,
    time_in_weight,
    time_in_bias,
    time_out_weight,
    time_out_bias,
    label_table,
    ada_weight,
    ada_bias,
    down_kernel,
    down_bias,
    input_weight,
    query_bias,
    value_bias,
    output_weight,
    output_bias,
    expand_weight,
    expand_bias,
    mixer_kernel,
    mixer_bias,
    shrink_weight,
    shrink_bias,
    cotangent,
):
    count, rows, columns, features = latents.shape
    strips = lax.axis_size("strips")
    items = lax.axis_size("items")
    devices = strips * items
    strip = lax.axis_index("strips")
    item = lax.axis_index("items")
    me = item * strips + strip
    sub = columns // COLUMN_PARTS
    quarter = rows * columns // 4
    groups = count * 4
    share = strips // groups
    width = features // share
    row_vector = lambda v: v.astype(single).reshape(1, -1)
    edge = jnp.stack([strip > 0, strip < strips - 1]).astype(single)

    lines = -(-count // 8) * 8
    weights = (
        time_in_weight, row_vector(time_in_bias), time_out_weight, row_vector(time_out_bias),
        label_table,
    )
    waves = time_in_weight.shape[0] // 2
    modulation = modulate(
        time_features(jnp.pad(timesteps, (0, lines - count)), waves),
        jnp.pad(labels, (0, lines - count))[:, None],
        weights,
        ada_weight,
        row_vector(ada_bias),
    )
    shift_a, scale_a, gate_a, shift_b, scale_b, gate_b = (
        modulation[i, :count, None, :] for i in range(6)
    )

    ends = jnp.concatenate([latents[:, -1:], cotangent[:, -1:]], axis=1)
    starts = jnp.concatenate([latents[:, :1], cotangent[:, :1]], axis=1)
    above = from_above(ends)
    below = from_below(starts)

    down_taps = tap_rows(down_kernel)
    grouped, normed_a, kept = front(
        edge, latents, above[:, :1], below[:, :1], scale_a, shift_a, down_taps, row_vector(down_bias)
    )

    def spread(array):
        flat = array.reshape(groups, quarter, array.shape[-1])
        if share > 1:
            flat = jnp.repeat(flat, share, axis=0)
        got = lax.all_to_all(flat, "strips", 0, 0, tiled=True)
        return got.reshape(strips * quarter, array.shape[-1])

    def collect(array):
        flat = array.reshape(strips, quarter, array.shape[-1])
        return lax.all_to_all(flat, "strips", 0, 0, tiled=True)

    group = spread(grouped)
    g_kept, d_branch, grad_shrink_bias = upstream_parts(
        cotangent, above[:, 1:], below[:, 1:], gate_b
    )

    head_at = (strip % share) * width
    def own_columns(array, axis):
        return array if share == 1 else lax.dynamic_slice_in_dim(array, head_at, width, axis=axis)

    own_weight = jnp.concatenate(
        [own_columns(input_weight[:, i * features : (i + 1) * features], 1) for i in range(3)], axis=1
    ) if share > 1 else input_weight
    own_bias = jnp.concatenate(
        [own_columns(row_vector(b), 1) for b in (query_bias, value_bias)], axis=1
    )
    piece = width // CHUNKS
    saved = []
    mixed = []
    d_act = feed_upstream(d_branch, shrink_weight)
    group, d_act = lax.optimization_barrier((group, d_act))
    for c in range(CHUNKS):
        saved.append(attend(group, own_weight, own_bias, c * piece, piece))
        mixed.append(collect(saved[c][3]))
    if share == 1:
        mixed = [m.reshape(count, 4, quarter, piece) for m in mixed]
    else:
        joined = jnp.concatenate(mixed, axis=-1).reshape(groups, share, quarter, width)
        joined = joined.transpose(0, 2, 1, 3).reshape(count, 4, quarter, features)
        mixed = [joined]

    attended, middle, normed_b = middle_part(
        mixed, output_weight, row_vector(output_bias), kept, gate_a, scale_b, shift_b
    )
    branch, e, act, d_hid, feed_small = feed_forward(
        edge,
        normed_b,
        from_above(normed_b[:, -2:]),
        from_below(normed_b[:, :2]),
        d_act,
        expand_weight,
        row_vector(expand_bias),
        tap_rows(mixer_kernel),
        row_vector(mixer_bias),
        shrink_weight,
    )
    turned = turn(
        branch, e, middle, attended, g_kept, gate_b, scale_b, gate_a, row_vector(shrink_bias),
        output_weight, mixed,
    )
    result, d_middle = turned[:2]
    d_mixed = turned[2:-2]
    grad_output, turn_sums = turned[-2:]

    hidden = expand_weight.shape[1]
    steps = hidden // features
    grad_shrink, grad_expand = feed_grads(act, d_hid, normed_b, d_branch)

    early = jnp.concatenate(
        [
            grad_shrink.reshape(devices, hidden // devices, features),
            grad_expand.reshape(steps, devices, features // devices, features)
            .transpose(1, 0, 2, 3)
            .reshape(devices, hidden // devices, features),
        ],
        axis=1,
    )
    early_sum = lax.psum_scatter(early, both, scatter_dimension=0, tiled=False).astype(single)

    if share == 1:
        d_mixed = [spread(d) for d in d_mixed]
    else:
        parts = d_mixed[0].reshape(groups, quarter, share, width).transpose(0, 2, 1, 3)
        got = lax.all_to_all(parts.reshape(strips, quarter, width), "strips", 0, 0, tiled=True)
        got = got.reshape(strips * quarter, width)
        d_mixed = [got[:, c * piece : (c + 1) * piece] for c in range(CHUNKS)]
    grads = []
    for c in range(CHUNKS):
        if c == 0:
            d_mixed[c], _ = lax.optimization_barrier((d_mixed[c], early))
        q, k, v, out, logs = saved[c]
        grads.append(attend_back(q, k, v, out, d_mixed[c], logs))
    size = features // devices
    narrow = jnp.stack([jnp.sum(turn_sums[:, 4], axis=0), jnp.sum(grad_shrink_bias[:, 0], axis=0)])
    to_all = jnp.concatenate(
        [
            turn_sums[:, 3], turn_sums[:, 1], turn_sums[:, 2], turn_sums[:, 0],
        ],
        axis=1,
    ).reshape(-1)
    to_all = jnp.concatenate([to_all, timesteps.astype(single), labels.astype(single)])
    fill = -(to_all.shape[0] + 11 * (hidden // devices) + 2 * size) % LANES
    early_small = jnp.concatenate(
        [
            jnp.broadcast_to(to_all, (devices, to_all.shape[0])),
            feed_small[:11].reshape(11, devices, -1).transpose(1, 0, 2).reshape(devices, -1),
            narrow.reshape(2, devices, -1).transpose(1, 0, 2).reshape(devices, -1),
            jnp.zeros((devices, fill), single),
        ],
        axis=1,
    )
    early_small = after(early_small, grads[0][0], *d_mixed)
    early_got = lax.all_to_all(early_small, both, 0, 0, tiled=True)

    parts = [g for chunk in grads for g in chunk]
    d_group = regroup(parts, own_weight)
    d_reduced = collect(d_group)
    if share > 1:
        d_reduced = jnp.sum(
            d_reduced.reshape(groups, share, quarter, features).astype(single), axis=1
        ).astype(bfloat)
    d_reduced = d_reduced.reshape(count, 4, quarter, features)
    late, d_sums = input_grad(after(group, d_group), grad_output, parts)
    d_query_sum = d_sums[0, :width]
    d_value_sum = d_sums[0, width:]
    if share > 1:
        zero = jnp.zeros((features, 3, features), bfloat)
        grad_input = lax.dynamic_update_slice(
            zero, late[:, : 3 * width].reshape(features, 3, width), (0, 0, head_at)
        ).reshape(features, 3 * features)
        late = jnp.concatenate([grad_input, grad_output], axis=1)
        flat = jnp.zeros((features,), single)
        d_query_sum = lax.dynamic_update_slice(flat, d_query_sum, (head_at,))
        d_value_sum = lax.dynamic_update_slice(flat, d_value_sum, (head_at,))
    late = late.reshape(items, strips // 2, 2, size, 4 * features)
    late_part = sum_cores(lambda core: lax.dynamic_index_in_dim(late, core, 2, keepdims=False))

    per_latent = count * 4 * features
    parts_early = early_got[:, :per_latent].reshape(items, strips, per_latent)
    first = early_got.reshape(items, strips, -1)[:, 0, per_latent : per_latent + 2 * count]
    all_times = first[:, :count].reshape(-1)
    all_labels = first[:, count:].reshape(-1, 1).astype(jnp.int32)
    sinus = time_features(all_times, waves)
    early_sums = jnp.sum(early_got[:, per_latent + 2 * count :], axis=0)
    cut = 11 * (hidden // devices)
    feed_sum = early_sums[:cut].reshape(11, -1)
    narrow_sum = early_sums[cut : cut + 2 * size].reshape(2, size)
    index = jnp.reshape(me, (1,)).astype(jnp.int32)
    before, cond, d_active, grad_ada_early, d_mod_early = early_condition(
        index, parts_early, count, sinus, all_labels, weights, ada_weight, size
    )

    d_reduced, before, late_part = lax.optimization_barrier((d_reduced, before, late_part))
    late_part = sum_items(late_part)
    grad_latents, down_small, final_sums = final(
        d_reduced,
        from_above(d_reduced[:, 2:, -2 * sub :]),
        from_below(d_reduced[:, :2, : 2 * sub]),
        normed_a,
        kept,
        d_middle,
        scale_a,
        down_taps,
    )

    late_narrow = jnp.concatenate([d_query_sum[None], d_value_sum[None], down_small[:10]], axis=0)
    to_all = final_sums[:, :2].reshape(-1)
    fill = -(to_all.shape[0] + 12 * size) % LANES
    late_small = jnp.concatenate(
        [
            jnp.broadcast_to(to_all, (devices, to_all.shape[0])),
            late_narrow.reshape(12, devices, size).transpose(1, 0, 2).reshape(devices, -1),
            jnp.zeros((devices, fill), single),
        ],
        axis=1,
    )
    late_small, late_part = lax.optimization_barrier((late_small, late_part))
    late_sum = sum_strips(late_part)
    late_got = lax.all_to_all(late_small, both, 0, 0, tiled=True)
    late_sums = jnp.sum(late_got[:, to_all.shape[0] :], axis=0)[: 12 * size].reshape(12, size)
    (
        grad_ada_late, d_mod_late, grad_table, grad_time_out, grad_time_in, d_cond, d_before,
    ) = late_condition(
        index,
        late_got[:, : to_all.shape[0]].reshape(items, strips, -1),
        count,
        before,
        cond,
        d_active,
        sinus,
        all_labels,
        time_out_weight,
        ada_weight,
        label_table.shape[1],
        devices,
    )

    def mine(array):
        part = array.shape[-1] // devices
        return lax.dynamic_slice_in_dim(array[0], me * part, part, axis=0)

    feed_rows = hidden // devices
    return (
        result,
        grad_latents,
        grad_time_in,
        mine(d_before),
        grad_time_out,
        mine(d_cond),
        grad_table,
        jnp.concatenate([grad_ada_late, grad_ada_early], axis=1),
        mine(jnp.concatenate([d_mod_late, d_mod_early], axis=1)),
        late_sums[2:11].T,
        late_sums[11],
        late_sum[:, : 3 * features],
        late_sums[0],
        late_sums[1],
        late_sum[:, 3 * features :],
        narrow_sum[0],
        early_sum[feed_rows:]
        .reshape(steps, features // devices, features)
        .transpose(1, 0, 2)
        .reshape(features // devices, hidden),
        feed_sum[10],
        feed_sum[:9].T,
        feed_sum[9],
        early_sum[:feed_rows],
        narrow_sum[1],
    )


def solution(mesh):
    image = P("items", "strips", None, None)
    split = P(both, None)
    line = P(both)
    return jax.shard_map(
        per_device,
        mesh=mesh,
        in_specs=(image, P("items"), P("items")) + (P(),) * 20 + (image,),
        out_specs=(
            image, image, split, line, split, line, split, split, line, split, line,
            split, line, line, split, line, split, line, split, line, split, line,
        ),
        check_vma=False,
    )
```

```python
from functools import partial
import math

import jax
import jax.numpy as jnp
from jax import lax
from jax.experimental import pallas as pl
from jax.experimental.pallas import tpu as pltpu
from jax.sharding import PartitionSpec as P

HEADS = 12
HEAD_DIM = 64
LANES = 128
COLUMN_PARTS = 4
CHUNKS = 2

highest = lax.Precision.HIGHEST
epsilon = 1e-06
bfloat = jnp.bfloat16
single = jnp.float32
both = ("items", "strips")


def params(mebibytes):
    return pltpu.CompilerParams(vmem_limit_bytes=mebibytes * 1024 * 1024)


def cost(flops, moved, exps=0):
    return pl.CostEstimate(flops=int(flops), bytes_accessed=int(moved), transcendentals=int(exps))


def dot(a, b):
    return lax.dot_general(a, b, (((1,), (0,)), ((), ())), preferred_element_type=single)


def dot_nt(a, b):
    return lax.dot_general(a, b, (((1,), (1,)), ((), ())), preferred_element_type=single)


def dot_tn(a, b):
    return lax.dot_general(a, b, (((0,), (0,)), ((), ())), preferred_element_type=single)


def column_order(columns, back):
    sub = columns // COLUMN_PARTS
    first = lax.broadcasted_iota(jnp.int32, (columns, columns), 0)
    second = lax.broadcasted_iota(jnp.int32, (columns, columns), 1)
    kept, column = (second, first) if back else (first, second)
    return (column == COLUMN_PARTS * (kept % sub) + kept // sub).astype(bfloat)


def norm_parts(value):
    center = value - jnp.mean(value, axis=-1, keepdims=True)
    inverse = lax.rsqrt(jnp.mean(center * center, axis=-1, keepdims=True) + epsilon)
    return center * inverse, inverse


def norm_back(normed, inverse, grad):
    return inverse * (
        grad
        - jnp.mean(grad, axis=-1, keepdims=True)
        - normed * jnp.mean(grad * normed, axis=-1, keepdims=True)
    )


def put_wide(ref, row, cells):
    sub = cells.shape[1]
    place = lax.broadcasted_iota(jnp.int32, cells.shape[1:], 0)
    last = cells[COLUMN_PARTS - 1].astype(single)
    first = cells[0].astype(single)
    ref[row, 1 : COLUMN_PARTS + 1] = cells
    ref[row, 0] = jnp.where(place == 0, 0.0, pltpu.roll(last, 1, 0)).astype(ref.dtype)
    ref[row, COLUMN_PARTS + 1] = jnp.where(
        place == sub - 1, 0.0, pltpu.roll(first, sub - 1, 0)
    ).astype(ref.dtype)


def put_part(ref, row, j, cells):
    sub = cells.shape[0]
    place = lax.broadcasted_iota(jnp.int32, cells.shape, 0)
    ref[row, j + 1] = cells
    if j == COLUMN_PARTS - 1:
        ref[row, 0] = jnp.where(place == 0, 0.0, pltpu.roll(cells, 1, 0))
    if j == 0:
        ref[row, COLUMN_PARTS + 1] = jnp.where(place == sub - 1, 0.0, pltpu.roll(cells, sub - 1, 0))


def conv_low(ref, row, taps):
    total = None
    for i in range(3):
        line = [taps[3 * i + j] * ref[row + i, j : j + COLUMN_PARTS] for j in range(3)]
        line = (line[0] + line[1]) + line[2]
        total = line if total is None else total + line
    return total


def conv_back_row(ref, row, taps):
    total = None
    for i in range(3):
        line = [
            taps[3 * i + j] * ref[row + 2 - i, 2 - j : 2 - j + COLUMN_PARTS] for j in range(3)
        ]
        line = (line[0] + line[1]) + line[2]
        total = line if total is None else total + line
    return total


def front_kernel(
    edge_ref, x_ref, top_ref, bottom_ref, scale_ref, shift_ref, taps_ref, bias_ref,
    grouped_ref, normed_ref, kept_ref, wide,
):
    rows, columns, features = x_ref.shape[1:]
    sub = columns // COLUMN_PARTS
    order = column_order(columns, False)
    scale = 1.0 + scale_ref[0]
    shift = shift_ref[0]

    def fill(row, raw, keep, kept_row=None):
        cells = dot(order, raw)
        if kept_row is not None:
            kept_ref[0, kept_row] = cells.astype(bfloat)
        for j in range(COLUMN_PARTS):
            line = slice(j * sub, (j + 1) * sub)
            normed = norm_parts(cells[line])[0] * scale + shift
            low = (normed if keep is None else normed * keep).astype(bfloat)
            normed_ref[0, row, line] = low
            put_part(wide, row, j, low.astype(single))

    fill(0, top_ref[0, 0], edge_ref[0])
    fill(rows + 1, bottom_ref[0, 0], edge_ref[1])

    for row in range(rows):
        fill(row + 1, x_ref[0, row], None, row)

    taps = [taps_ref[t : t + 1] for t in range(9)]
    bias = bias_ref[...]

    @pl.loop(0, rows // 2)
    def _(pair):
        for a in range(2):
            for lane in range(0, features, LANES):
                at = pl.ds(lane, LANES)
                total = jnp.zeros((COLUMN_PARTS, sub, LANES), single) + bias[:, lane : lane + LANES]
                for i in range(3):
                    for j in range(3):
                        total = total + taps[3 * i + j][:, lane : lane + LANES] * wide[
                            pair * 2 + a + i, j : j + COLUMN_PARTS, :, at
                        ]
                low = total.astype(bfloat)
                for j in range(COLUMN_PARTS):
                    grouped_ref[
                        0, 2 * a + j % 2, pl.ds(pl.multiple_of((pair * 2 + j // 2) * sub, sub), sub), at
                    ] = low[j]


def front(edge, latents, top, bottom, scale, shift, taps, bias):
    count, rows, columns, features = latents.shape
    quarter = rows * columns // 4
    sub = columns // COLUMN_PARTS
    image = lambda r: pl.BlockSpec((1, r, columns, features), lambda l: (l, 0, 0, 0))
    vector = pl.BlockSpec((1, 1, features), lambda l: (l, 0, 0))
    return pl.pallas_call(
        front_kernel,
        grid=(count,),
        in_specs=[
            pl.BlockSpec(memory_space=pltpu.SMEM),
            image(rows), image(1), image(1), vector, vector,
            pl.BlockSpec((16, features), lambda l: (0, 0)),
            pl.BlockSpec((1, features), lambda l: (0, 0)),
        ],
        out_specs=[
            pl.BlockSpec((1, 4, quarter, features), lambda l: (l, 0, 0, 0)),
            image(rows + 2), image(rows),
        ],
        out_shape=[
            jax.ShapeDtypeStruct((count, 4, quarter, features), bfloat),
            jax.ShapeDtypeStruct((count, rows + 2, columns, features), bfloat),
            jax.ShapeDtypeStruct((count, rows, columns, features), bfloat),
        ],
        scratch_shapes=[pltpu.VMEM((rows + 2, COLUMN_PARTS + 2, sub, features), single)],
        compiler_params=params(18),
        cost_estimate=cost(count * rows * columns * features * 150, count * rows * columns * features * 8),
        name="front",
    )(edge, latents, top, bottom, scale, shift, taps, bias)


def upstream_kernel(g_ref, top_ref, bottom_ref, gate_ref, kept_ref, branch_ref, bias_ref):
    rows, columns, features = g_ref.shape[1:]
    order = column_order(columns, False)
    gate = gate_ref[0]

    def low(raw):
        cells = dot(order, raw)
        return cells, (cells * gate).astype(bfloat)

    branch_ref[0, 0] = low(top_ref[0, 0])[1]
    branch_ref[0, rows + 1] = low(bottom_ref[0, 0])[1]

    def step(row, total):
        cells, grad = low(g_ref[0, row])
        kept_ref[0, row] = cells.astype(bfloat)
        branch_ref[0, row + 1] = grad
        return total + jnp.sum(grad.astype(single), axis=0, keepdims=True)

    total = jnp.zeros((1, features), single)
    for row in range(rows):
        total = step(row, total)
    bias_ref[0] = total


def upstream_parts(cotangent, top, bottom, gate):
    count, rows, columns, features = cotangent.shape
    image = lambda r: pl.BlockSpec((1, r, columns, features), lambda l: (l, 0, 0, 0))
    vector = pl.BlockSpec((1, 1, features), lambda l: (l, 0, 0))
    return pl.pallas_call(
        upstream_kernel,
        grid=(count,),
        in_specs=[image(rows), image(1), image(1), vector],
        out_specs=[image(rows), image(rows + 2), vector],
        out_shape=[
            jax.ShapeDtypeStruct((count, rows, columns, features), bfloat),
            jax.ShapeDtypeStruct((count, rows + 2, columns, features), bfloat),
            jax.ShapeDtypeStruct((count, 1, features), single),
        ],
        compiler_params=params(14),
        cost_estimate=cost(count * rows * columns * features * 130, count * rows * columns * features * 6),
        name="upstream",
    )(cotangent, top, bottom, gate)


QUERY_STEP = 1024
QUERY_STEP_BACK = 256


def attend_kernel(
    x_ref, wq_ref, wk_ref, wv_ref, bq_ref, bv_ref, q_ref, k_ref, v_ref, mixed_ref, log_ref
):
    tokens = x_ref.shape[0]
    base = math.log2(math.e) / math.sqrt(HEAD_DIM)
    x = x_ref[...]
    q_ref[...] = (dot(x, wq_ref[...]) + bq_ref[...]).astype(bfloat)
    k_ref[...] = dot(x, wk_ref[...]).astype(bfloat)
    v_ref[...] = (dot(x, wv_ref[...]) + bv_ref[...]).astype(bfloat)
    keys = k_ref[...]
    values = v_ref[...].T
    lane = lax.broadcasted_iota(jnp.int32, (QUERY_STEP, LANES), 1)
    for at in range(0, tokens, QUERY_STEP):
        part = q_ref[at : at + QUERY_STEP]
        outs = []
        for head in range(LANES // HEAD_DIM):
            own = jnp.where(lane // HEAD_DIM == head, part, jnp.zeros_like(part))
            scores = dot_nt(keys, own)
            peak = jnp.max(scores, axis=0, keepdims=True) * base
            soft = jnp.exp2(scores * base - peak)
            total = jnp.sum(soft, axis=0, keepdims=True)
            log_ref[0, head : head + 1, at : at + QUERY_STEP] = peak + jnp.log2(total)
            out = dot(values[head * HEAD_DIM : (head + 1) * HEAD_DIM], soft.astype(bfloat))
            outs.append(out * (1.0 / total))
        mixed_ref[at : at + QUERY_STEP] = jnp.concatenate(outs, axis=0).T.astype(bfloat)


def attend(x, weights, biases, first, width):
    tokens, features = x.shape
    pairs = width // LANES
    start = first // LANES
    stride = weights.shape[1] // 3 // LANES
    weight = lambda i: pl.BlockSpec((features, LANES), lambda h: (0, i * stride + start + h))
    bias = lambda i: pl.BlockSpec((1, LANES), lambda h: (0, i * stride + start + h))
    column = pl.BlockSpec((tokens, LANES), lambda h: (0, h))
    lows = jax.ShapeDtypeStruct((tokens, width), bfloat)
    return pl.pallas_call(
        attend_kernel,
        grid=(pairs,),
        in_specs=[pl.BlockSpec((tokens, features), lambda h: (0, 0))]
        + [weight(0), weight(1), weight(2), bias(0), bias(1)],
        out_specs=[column] * 4 + [pl.BlockSpec((1, 2, tokens), lambda h: (h, 0, 0))],
        out_shape=[lows] * 4 + [jax.ShapeDtypeStruct((pairs, 2, tokens), single)],
        compiler_params=params(60),
        cost_estimate=cost(
            6 * tokens * features * width + 16 * tokens * tokens * width,
            2 * tokens * features + 8 * tokens * width + 6 * features * width,
            2 * pairs * tokens * tokens,
        ),
        name="attend",
    )(x, weights, weights, weights, biases, biases)


def attend_back_kernel(
    q_ref, k_ref, v_ref, mixed_ref, grad_ref, log_ref, dq_ref, dk_ref, dv_ref, dk_sum, dv_sum
):
    tokens = q_ref.shape[0]
    scale = 1.0 / math.sqrt(HEAD_DIM)
    base = math.log2(math.e) * scale
    keys = k_ref[...]
    values = v_ref[...]
    keys_turned = keys.T
    lane = lax.broadcasted_iota(jnp.int32, (QUERY_STEP_BACK, LANES), 1)
    for at in range(0, tokens, QUERY_STEP_BACK):
        rows = slice(at, at + QUERY_STEP_BACK)
        part = q_ref[rows]
        grad = grad_ref[rows]
        shares = (grad.astype(single) * mixed_ref[rows].astype(single)).T
        outs = []
        for head in range(LANES // HEAD_DIM):
            mine = lane // HEAD_DIM == head
            own = jnp.where(mine, part, jnp.zeros_like(part))
            own_grad = jnp.where(mine, grad, jnp.zeros_like(grad))
            share = jnp.sum(
                shares[head * HEAD_DIM : (head + 1) * HEAD_DIM], axis=0, keepdims=True
            )
            soft = jnp.exp2(dot_nt(keys, own) * base - log_ref[0, head : head + 1, rows])
            d_scores = (soft * (dot_nt(values, own_grad) - share)).astype(bfloat)
            dv_part = dot(soft.astype(bfloat), own_grad)
            dk_part = dot(d_scores, own)
            if at == 0 and head == 0:
                dv_sum[...] = dv_part
                dk_sum[...] = dk_part
            else:
                dv_sum[...] += dv_part
                dk_sum[...] += dk_part
            outs.append(dot(keys_turned[head * HEAD_DIM : (head + 1) * HEAD_DIM], d_scores))
        dq_ref[rows] = (jnp.concatenate(outs, axis=0) * scale).T.astype(bfloat)
    dk_ref[...] = (dk_sum[...] * scale).astype(bfloat)
    dv_ref[...] = dv_sum[...].astype(bfloat)


def attend_back(q, k, v, mixed, grad, logs):
    tokens, width = q.shape
    pairs = width // LANES
    column = pl.BlockSpec((tokens, LANES), lambda h: (0, h))
    lows = jax.ShapeDtypeStruct((tokens, width), bfloat)
    return pl.pallas_call(
        attend_back_kernel,
        grid=(pairs,),
        in_specs=[column] * 5 + [pl.BlockSpec((1, 2, tokens), lambda h: (h, 0, 0))],
        out_specs=[column] * 3,
        out_shape=[lows] * 3,
        scratch_shapes=[pltpu.VMEM((tokens, LANES), single)] * 2,
        compiler_params=params(60),
        cost_estimate=cost(
            40 * tokens * tokens * width, 16 * tokens * width, 2 * pairs * tokens * tokens
        ),
        name="attend_back",
    )(q, k, v, mixed, grad, logs)


def regroup_kernel(*refs):
    parts, weight_ref, out_ref = refs[:-2], refs[-2], refs[-1]
    count = len(parts) // 3
    piece = parts[0].shape[1]
    third = weight_ref.shape[1] // 3
    total = None
    for c in range(count):
        for i in range(3):
            at = i * third + c * piece
            term = dot_nt(parts[3 * c + i][...], weight_ref[:, at : at + piece])
            total = term if total is None else total + term
    out_ref[...] = total.astype(bfloat)


def regroup(parts, weight):
    tokens, piece = parts[0].shape
    features = weight.shape[0]
    step = min(256, tokens)
    return pl.pallas_call(
        regroup_kernel,
        grid=(tokens // step,),
        in_specs=[pl.BlockSpec((step, piece), lambda t: (t, 0))] * len(parts)
        + [pl.BlockSpec(weight.shape, lambda t: (0, 0))],
        out_specs=pl.BlockSpec((step, features), lambda t: (t, 0)),
        out_shape=jax.ShapeDtypeStruct((tokens, features), bfloat),
        compiler_params=params(60),
        cost_estimate=cost(2 * tokens * features * weight.shape[1], 2 * tokens * features * 4),
        name="regroup",
    )(*parts, weight)


def input_grad_kernel(*refs):
    x_ref, other_ref = refs[0], refs[1]
    parts = refs[2:-2]
    out_ref, sums_ref = refs[-2:]
    count = len(parts) // 3
    tokens, piece = parts[0].shape
    third = count * piece
    turned = x_ref[...].T
    for c in range(count):
        for i in range(3):
            at = i * third + c * piece
            out_ref[:, at : at + piece] = dot(turned, parts[3 * c + i][...]).astype(bfloat)
    out_ref[:, 3 * third :] = other_ref[...]

    @pl.when(pl.program_id(0) == 0)
    def _():
        ones = jnp.ones((16, tokens), bfloat)
        for c in range(count):
            for i in (0, 2):
                total = dot(ones, parts[3 * c + i][...])
                sums_ref[:, i // 2 * third + c * piece : i // 2 * third + (c + 1) * piece] = total[:8]


def input_grad(x, other, parts):
    tokens, features = x.shape
    piece = parts[0].shape[1]
    third = piece * len(parts) // 3
    step = 256
    return pl.pallas_call(
        input_grad_kernel,
        grid=(features // step,),
        in_specs=[
            pl.BlockSpec((tokens, step), lambda t: (0, t)),
            pl.BlockSpec((step, other.shape[1]), lambda t: (t, 0)),
        ]
        + [pl.BlockSpec((tokens, piece), lambda t: (0, 0))] * len(parts),
        out_specs=[
            pl.BlockSpec((step, 3 * third + other.shape[1]), lambda t: (t, 0)),
            pl.BlockSpec((8, 2 * third), lambda t: (0, 0)),
        ],
        out_shape=[
            jax.ShapeDtypeStruct((features, 3 * third + other.shape[1]), bfloat),
            jax.ShapeDtypeStruct((8, 2 * third), single),
        ],
        compiler_params=params(60),
        cost_estimate=cost(6 * tokens * features * third, 2 * tokens * features * 5),
        name="input_grad",
    )(x, other, *parts)


def middle_kernel(
    parts, *refs
):
    mixed_refs = refs[:parts]
    weight_ref, bias_ref, x_ref, gate_ref, scale_ref, shift_ref = refs[parts : parts + 6]
    attended_ref, middle_ref, normed_ref, first_ref, last_ref, grouped = refs[parts + 6 :]
    rows, columns, features = x_ref.shape[1:]
    sub = columns // COLUMN_PARTS
    quarter = rows * columns // 4
    total = bias_ref[...]
    at = 0
    for ref in mixed_refs:
        width = ref.shape[-1]
        total = total + dot(ref[0].reshape(4 * quarter, width), weight_ref[at : at + width])
        at += width
    grouped[...] = total.reshape(4, quarter, features)
    gate = gate_ref[0]
    scale = 1.0 + scale_ref[0]
    shift = shift_ref[0]

    for pair in range(rows // 2):
        for a in range(2):
            row = pair * 2 + a
            for j in range(COLUMN_PARTS):
                line = slice(j * sub, (j + 1) * sub)
                cells = grouped[
                    2 * a + j % 2, pl.ds((pair * 2 + j // 2) * sub, sub)
                ]
                attended_ref[0, row, line] = cells
                middle = x_ref[0, row, line].astype(single) + gate * cells
                middle_ref[0, row, line] = middle
                low = (norm_parts(middle)[0] * scale + shift).astype(bfloat)
                normed_ref[0, row, line] = low
                if row < 2:
                    first_ref[0, row, line] = low
                if row >= rows - 2:
                    last_ref[0, row - rows + 2, line] = low


def middle_part(mixed, weight, bias, kept, gate, scale, shift):
    count, rows, columns, features = kept.shape
    quarter = rows * columns // 4
    image = pl.BlockSpec((1, rows, columns, features), lambda l: (l, 0, 0, 0))
    vector = pl.BlockSpec((1, 1, features), lambda l: (l, 0, 0))
    return pl.pallas_call(
        partial(middle_kernel, len(mixed)),
        grid=(count,),
        in_specs=[
            pl.BlockSpec((1, 4, quarter, m.shape[-1]), lambda l: (l, 0, 0, 0)) for m in mixed
        ]
        + [
            pl.BlockSpec((features, features), lambda l: (0, 0)),
            pl.BlockSpec((1, features), lambda l: (0, 0)),
            image, vector, vector, vector,
        ],
        out_specs=[image] * 3
        + [pl.BlockSpec((1, 2, columns, features), lambda l: (l, 0, 0, 0))] * 2,
        out_shape=[
            jax.ShapeDtypeStruct(kept.shape, single),
            jax.ShapeDtypeStruct(kept.shape, single),
            jax.ShapeDtypeStruct(kept.shape, bfloat),
        ]
        + [jax.ShapeDtypeStruct((count, 2, columns, features), bfloat)] * 2,
        scratch_shapes=[pltpu.VMEM((4, quarter, features), single)],
        compiler_params=params(60),
        cost_estimate=cost(2 * kept.size * features, 14 * kept.size),
        name="middle",
    )(*mixed, weight, bias, kept, gate, scale, shift)


def feed_upstream_kernel(db_ref, ws_ref, out_ref):
    out_ref[...] = dot_nt(db_ref[...], ws_ref[...]).astype(bfloat)


def feed_upstream(db, ws):
    count, tall, columns, features = db.shape
    hidden = ws.shape[0]
    lines = count * tall * columns
    return pl.pallas_call(
        feed_upstream_kernel,
        grid=(hidden // features,),
        in_specs=[
            pl.BlockSpec((lines, features), lambda s: (0, 0)),
            pl.BlockSpec((features, features), lambda s: (s, 0)),
        ],
        out_specs=pl.BlockSpec((lines, features), lambda s: (0, s)),
        out_shape=jax.ShapeDtypeStruct((lines, hidden), bfloat),
        compiler_params=params(60),
        cost_estimate=cost(2 * lines * features * hidden, 2 * lines * (features + hidden)),
        name="feed_upstream",
    )(db.reshape(lines, features), ws)


def feed_kernel(
    edge_ref, nb_ref, top_ref, bottom_ref, d_act_ref, we_ref, be_ref, taps_ref, bm_ref,
    act_ref, d_hid_ref, small_ref,
    nb_wide, hidden, wide, d_wide,
):
    count, rows, columns, features = nb_ref.shape
    sub = columns // COLUMN_PARTS
    block = we_ref.shape[1]
    own = rows * columns
    tall = (rows + 4) * columns
    mid = (rows + 2) * columns

    @pl.when(pl.program_id(0) == 0)
    def _():
        for l in range(count):
            nb_wide[l * tall : l * tall + 2 * columns] = top_ref[l].reshape(2 * columns, features)
            nb_wide[l * tall + 2 * columns : (l + 1) * tall - 2 * columns] = nb_ref[l].reshape(
                own, features
            )
            nb_wide[(l + 1) * tall - 2 * columns : (l + 1) * tall] = bottom_ref[l].reshape(
                2 * columns, features
            )

    hidden[...] = (dot(nb_wide[...], we_ref[...]) + be_ref[...]).astype(bfloat)
    small_ref[...] = jnp.zeros_like(small_ref)

    c0 = math.sqrt(2.0 / math.pi)
    c1 = c0 * 0.044715

    @pl.loop(0, count * (block // LANES))
    def _(index):
        l = index // (block // LANES)
        at = pl.ds(pl.multiple_of((index % (block // LANES)) * LANES, LANES), LANES)
        taps = [taps_ref[t : t + 1, at] for t in range(9)]
        bias = bm_ref[:, at]
        for row in range(rows + 4):
            cells = hidden[pl.ds(pl.multiple_of(l * tall + row * columns, columns), columns), at]
            if row < 2:
                cells = cells * edge_ref[0].astype(bfloat)
            if row >= rows + 2:
                cells = cells * edge_ref[1].astype(bfloat)
            put_wide(wide, row, cells.reshape(COLUMN_PARTS, sub, LANES))
        taps = [(t + jnp.zeros((sub, LANES), single)).astype(bfloat) for t in taps]
        for row in range(rows + 2):
            v = conv_low(wide, row, taps).astype(single) + bias
            cube = (v * v) * c1
            half = 0.5 * jnp.tanh(v * (cube + c0)) + 0.5
            gelu = v * half
            slope = half + gelu * (1.0 - half) * (6.0 * cube + 2.0 * c0)
            if 1 <= row <= rows:
                act_ref[
                    pl.ds(pl.multiple_of(l * own + (row - 1) * columns, columns), columns), at
                ] = gelu.reshape(columns, LANES).astype(bfloat)
            grad = d_act_ref[pl.ds(pl.multiple_of(l * mid + row * columns, columns), columns), at]
            grad = grad.astype(single).reshape(COLUMN_PARTS, sub, LANES) * slope
            put_wide(d_wide, row, grad.astype(bfloat))
        sums = [jnp.zeros((sub, LANES), single) for _ in range(11)]
        for row in range(rows):
            d_in = conv_back_row(d_wide, row, taps).astype(bfloat)
            d_hid_ref[pl.ds(pl.multiple_of(l * own + row * columns, columns), columns), at] = (
                d_in.reshape(columns, LANES)
            )
            center = d_wide[row + 1, 1 : COLUMN_PARTS + 1]
            for i in range(3):
                for j in range(3):
                    term = center * wide[row + 1 + i, j : j + COLUMN_PARTS]
                    term = (term[0] + term[1]) + (term[2] + term[3])
                    sums[3 * i + j] += term.astype(single)
            sums[9] += jnp.sum(center.astype(single), axis=0)
            sums[10] += jnp.sum(d_in.astype(single), axis=0)
        for t in range(11):
            small_ref[t : t + 1, at] += jnp.sum(sums[t], axis=0, keepdims=True)


def feed_forward(edge, nb, top, bottom, d_act, we, be, taps, bm):
    count, rows, columns, features = nb.shape
    hidden = we.shape[1]
    block = features
    steps = hidden // block
    tokens = count * rows * columns
    tall = count * (rows + 4) * columns
    mid = count * (rows + 2) * columns
    sub = columns // COLUMN_PARTS
    whole = lambda a: pl.BlockSpec(a.shape, lambda s: (0,) * a.ndim)
    column = lambda n: pl.BlockSpec((n, block), lambda s: (0, s))
    return pl.pallas_call(
        feed_kernel,
        grid=(steps,),
        in_specs=[
            pl.BlockSpec(memory_space=pltpu.SMEM),
            whole(nb), whole(top), whole(bottom),
            column(mid), column(features), column(1), column(16), column(1),
        ],
        out_specs=[column(tokens), column(tokens), column(16)],
        out_shape=[
            jax.ShapeDtypeStruct((tokens, hidden), bfloat),
            jax.ShapeDtypeStruct((tokens, hidden), bfloat),
            jax.ShapeDtypeStruct((16, hidden), single),
        ],
        scratch_shapes=[
            pltpu.VMEM((tall, features), bfloat),
            pltpu.VMEM((tall, block), bfloat),
            pltpu.VMEM((rows + 4, COLUMN_PARTS + 2, sub, LANES), bfloat),
            pltpu.VMEM((rows + 2, COLUMN_PARTS + 2, sub, LANES), bfloat),
        ],
        compiler_params=params(60),
        cost_estimate=cost(
            2 * features * hidden * tall,
            8 * tokens * features + 4 * features * hidden + 6 * tokens * hidden,
            mid * hidden,
        ),
        name="feed_forward",
    )(edge, nb, top, bottom, d_act, we, be, taps, bm)


def feed_grads_kernel(
    act_ref, d_hid_ref, nb_ref, db_ref, out_ref, db_own, shrink_s, expand_s, shrink_sem, expand_sem
):
    count, rows, columns, features = nb_ref.shape
    own = rows * columns
    step = pl.program_id(0)
    steps = pl.num_programs(0)
    some, slots, unit = shrink_s.shape[:3]

    @pl.when(step == 0)
    def _():
        for l in range(count):
            db_own[l * own : (l + 1) * own] = db_ref[l, 1 : rows + 1].reshape(own, features)

    def copies(s):
        return (
            pltpu.make_async_copy(
                shrink_s, out_ref.at[pl.ds(s * some, some), pl.ds(0, slots)], shrink_sem
            ),
            pltpu.make_async_copy(expand_s, out_ref.at[:, slots + s], expand_sem),
        )

    shrink = dot_tn(act_ref[...], db_own[...])
    expand = dot_tn(nb_ref[...].reshape(count * own, features), d_hid_ref[...])

    @pl.when(step > 0)
    def _():
        for c in copies(step - 1):
            c.wait()

    shrink_s[...] = shrink.reshape(shrink_s.shape).astype(bfloat)
    expand_s[...] = expand.reshape(expand_s.shape).astype(bfloat)
    for c in copies(step):
        c.start()

    @pl.when(step == steps - 1)
    def _():
        for c in copies(step):
            c.wait()


def feed_grads(act, d_hid, nb, db, devices):
    count, rows, columns, features = nb.shape
    tokens, hidden = act.shape
    block = features
    steps = hidden // block
    unit = features // devices
    if unit % 8:
        shrink = dot_tn(act, db[:, 1:-1].reshape(tokens, features))
        expand = dot_tn(nb.reshape(tokens, features), d_hid)
        return jnp.concatenate(
            [
                shrink.reshape(devices, steps, unit, features),
                expand.reshape(devices, unit, steps, features).transpose(0, 2, 1, 3),
            ],
            axis=1,
        ).astype(bfloat)
    whole = lambda a: pl.BlockSpec(a.shape, lambda s: (0,) * a.ndim)
    return pl.pallas_call(
        feed_grads_kernel,
        grid=(steps,),
        in_specs=[
            pl.BlockSpec((tokens, block), lambda s: (0, s)),
            pl.BlockSpec((tokens, block), lambda s: (0, s)),
            whole(nb), whole(db),
        ],
        out_specs=pl.BlockSpec(memory_space=pl.ANY),
        out_shape=jax.ShapeDtypeStruct((devices, 2 * steps, unit, features), bfloat),
        scratch_shapes=[
            pltpu.VMEM((tokens, features), bfloat),
            pltpu.VMEM((devices // steps, steps, unit, features), bfloat),
            pltpu.VMEM((devices, unit, features), bfloat),
            pltpu.SemaphoreType.DMA,
            pltpu.SemaphoreType.DMA,
        ],
        compiler_params=params(60),
        cost_estimate=cost(4 * features * hidden * tokens, 8 * features * hidden + 4 * tokens * hidden),
        name="feed_grads",
    )(act, d_hid, nb, db)


TURN_ROWS = 4


def turn_kernel(parts, *refs):
    (
        act_ref, d_hid_ref, middle_ref, attended_ref, g_ref,
        gate_b_ref, scale_ref, gate_a_ref, bias_ref, weight_ref, ws_ref, we_ref,
    ) = refs[:12]
    mixed_refs = refs[12 : 12 + parts]
    result_ref, d_middle_ref = refs[12 + parts : 14 + parts]
    d_mixed_refs = refs[14 + parts : 14 + 2 * parts]
    gw_ref, sums_ref, gw_sum, grouped, branch_s, e_s, sums = refs[14 + 2 * parts :]
    rows, columns, features = g_ref.shape[1:]
    sub = columns // COLUMN_PARTS
    quarter = rows * columns // 4
    back = column_order(columns, True)
    gate_b = gate_b_ref[0]
    scale = 1.0 + scale_ref[0]
    gate_a = gate_a_ref[0]
    first = (pl.program_id(0) == 0) & (pl.program_id(1) == 0)
    last = (pl.program_id(0) == pl.num_programs(0) - 1) & (
        pl.program_id(1) == pl.num_programs(1) - 1
    )

    branch_s[...] = dot(act_ref[...], ws_ref[...]) + bias_ref[...]
    e_s[...] = dot_nt(d_hid_ref[...], we_ref[...])

    @pl.when(pl.program_id(1) == 0)
    def _():
        sums[...] = jnp.zeros_like(sums)

    for pair in range(rows // 2):
        for a in range(2):
            row = pair * 2 + a
            lows = []
            for j in range(COLUMN_PARTS):
                line = slice(j * sub, (j + 1) * sub)
                at = pl.ds(row * columns + j * sub, sub)
                branch = branch_s[at]
                middle = middle_ref[0, row, line]
                g = g_ref[0, row, line].astype(single)
                lows.append((middle + gate_b * branch).astype(bfloat))
                normed, inverse = norm_parts(middle)
                e = e_s[at]
                d_middle = g + norm_back(normed, inverse, e * scale)
                d_middle_ref[0, row, line] = d_middle
                low = (d_middle * gate_a).astype(bfloat)
                grouped[
                    2 * a + j % 2, pl.ds((pair * 2 + j // 2) * sub, sub)
                ] = low
                terms = (
                    g * branch, e, e * normed, d_middle * attended_ref[0, row, line], low.astype(single)
                )
                for t, term in enumerate(terms):
                    sums[t] += jnp.sum(term.reshape(sub // 8, 8, features), axis=0)
            result_ref[0, row] = dot(back, jnp.concatenate(lows, axis=0)).astype(bfloat)

    for t in range(5):
        sums_ref[0, t : t + 1] = jnp.sum(sums[t], axis=0, keepdims=True)
    sums_ref[0, 5:8] = jnp.zeros((3, features), single)
    grad = grouped[...].reshape(4 * quarter, features)
    at = 0
    for mixed_ref, d_ref in zip(mixed_refs, d_mixed_refs):
        width = mixed_ref.shape[-1]
        piece = slice(at, at + width)
        d_ref[0] = dot_nt(grad, weight_ref[piece]).astype(bfloat).reshape(4, quarter, width)
        part = dot_tn(mixed_ref[0].reshape(4 * quarter, width), grad)

        @pl.when(first)
        def _():
            gw_sum[piece] = part

        @pl.when(jnp.logical_not(first))
        def _():
            gw_sum[piece] += part

        at += width

    @pl.when(last)
    def _():
        gw_ref[...] = gw_sum[...].astype(bfloat)


def turn(
    act, d_hid, middle, attended, g, gate_b, scale, gate_a, bias, weight, shrink, expand, mixed
):
    count, rows, columns, features = g.shape
    hidden = act.shape[1]
    step = min(TURN_ROWS, rows)
    steps = rows // step
    quarter = step * columns // 4
    image = pl.BlockSpec((1, step, columns, features), lambda l, r: (l, r, 0, 0))
    flat = pl.BlockSpec((step * columns, hidden), lambda l, r: (l * steps + r, 0))
    vector = pl.BlockSpec((1, 1, features), lambda l, r: (l, 0, 0))
    groups = [
        pl.BlockSpec((1, 4, quarter, m.shape[-1]), lambda l, r: (l, 0, r, 0)) for m in mixed
    ]
    whole = lambda a: pl.BlockSpec(a.shape, lambda l, r: (0,) * a.ndim)
    square = pl.BlockSpec((features, features), lambda l, r: (0, 0))
    return pl.pallas_call(
        partial(turn_kernel, len(mixed)),
        grid=(count, steps),
        in_specs=[flat, flat, image, image, image, vector, vector, vector]
        + [whole(bias), square, whole(shrink), whole(expand)]
        + groups,
        out_specs=[image, image]
        + groups
        + [square, pl.BlockSpec((1, 8, features), lambda l, r: (l, 0, 0))],
        out_shape=[
            jax.ShapeDtypeStruct(g.shape, bfloat),
            jax.ShapeDtypeStruct(g.shape, single),
        ]
        + [jax.ShapeDtypeStruct(m.shape, bfloat) for m in mixed]
        + [
            jax.ShapeDtypeStruct((features, features), bfloat),
            jax.ShapeDtypeStruct((count, 8, features), single),
        ],
        scratch_shapes=[
            pltpu.VMEM((features, features), single),
            pltpu.VMEM((4, quarter, features), bfloat),
            pltpu.VMEM((step * columns, features), single),
            pltpu.VMEM((step * columns, features), single),
            pltpu.VMEM((5, 8, features), single),
        ],
        compiler_params=params(60),
        cost_estimate=cost(4 * g.size * (features + hidden), 20 * g.size + 4 * act.size),
        name="turn",
    )(act, d_hid, middle, attended, g, gate_b, scale, gate_a, bias, weight, shrink, expand, *mixed)


def final_kernel(
    d_ref, top_ref, bottom_ref, normed_ref, x_ref, d_middle_ref, scale_ref, taps_ref,
    out_ref, taps_out_ref, sums_ref, wide, d_wide,
):
    rows, columns, features = x_ref.shape[1:]
    sub = columns // COLUMN_PARTS
    back = column_order(columns, True)
    scale = 1.0 + scale_ref[0]

    def piece(ref, a, start):
        parts = [
            ref[0, 2 * a + j % 2, pl.ds(pl.multiple_of(start + (j // 2) * sub, sub), sub)]
            for j in range(COLUMN_PARTS)
        ]
        return jnp.stack(parts, axis=0).astype(single)

    def halo(ref):
        parts = [
            ref[0, j % 2, pl.ds((j // 2) * sub, sub)] for j in range(COLUMN_PARTS)
        ]
        return jnp.stack(parts, axis=0).astype(single)

    put_wide(d_wide, 0, halo(top_ref))
    put_wide(d_wide, rows + 1, halo(bottom_ref))

    @pl.loop(0, rows // 2)
    def _(pair):
        for a in range(2):
            put_wide(d_wide, pair * 2 + a + 1, piece(d_ref, a, pair * 2 * sub))

    @pl.loop(0, rows + 2)
    def _(row):
        for j in range(COLUMN_PARTS):
            put_part(wide, row, j, normed_ref[0, row, j * sub : (j + 1) * sub].astype(single))

    @pl.when(pl.program_id(0) == 0)
    def _():
        taps_out_ref[...] = jnp.zeros_like(taps_out_ref)

    d_normed = wide
    for lane in range(0, features, LANES):
        at = pl.ds(lane, LANES)
        taps = [taps_ref[t : t + 1, at] for t in range(9)]

        def step(row, sums):
            total = None
            center = d_wide[row + 1, 1 : COLUMN_PARTS + 1, :, at]
            sums = list(sums)
            for i in range(3):
                for j in range(3):
                    term = taps[3 * i + j] * d_wide[row + 2 - i, 2 - j : 2 - j + COLUMN_PARTS, :, at]
                    total = term if total is None else total + term
                    sums[3 * i + j] = sums[3 * i + j] + jnp.sum(
                        center * wide[row + i, j : j + COLUMN_PARTS, :, at], axis=0
                    )
            sums[9] = sums[9] + jnp.sum(center, axis=0)
            d_normed[row, 1 : COLUMN_PARTS + 1, :, at] = total
            return tuple(sums)

        sums = lax.fori_loop(
            0, rows, step, tuple(jnp.zeros((sub, LANES), single) for _ in range(10))
        )
        for t in range(10):
            taps_out_ref[t : t + 1, at] += jnp.sum(sums[t], axis=0, keepdims=True)

    def last(row, sums):
        lows = []
        for j in range(COLUMN_PARTS):
            line = slice(j * sub, (j + 1) * sub)
            cells = d_normed[row, j + 1]
            normed, inverse = norm_parts(x_ref[0, row, line].astype(single))
            grad = d_middle_ref[0, row, line] + norm_back(normed, inverse, cells * scale)
            lows.append(grad.astype(bfloat))
            sums = tuple(
                s + jnp.sum(t.reshape(sub // 8, 8, features), axis=0)
                for s, t in zip(sums, (cells, cells * normed))
            )
        out_ref[0, row] = dot(back, jnp.concatenate(lows, axis=0)).astype(bfloat)
        return sums

    sums = tuple(jnp.zeros((8, features), single) for _ in range(2))
    for row in range(rows):
        sums = last(row, sums)
    for t in range(2):
        sums_ref[0, t : t + 1] = jnp.sum(sums[t], axis=0, keepdims=True)
    sums_ref[0, 2:8] = jnp.zeros((6, features), single)


def final(d_reduced, top, bottom, normed, kept, d_middle, scale, taps):
    count, rows, columns, features = kept.shape
    quarter = rows * columns // 4
    sub = columns // COLUMN_PARTS
    image = lambda r: pl.BlockSpec((1, r, columns, features), lambda l: (l, 0, 0, 0))
    vector = pl.BlockSpec((1, 1, features), lambda l: (l, 0, 0))
    side = pl.BlockSpec((1, 2, 2 * sub, features), lambda l: (l, 0, 0, 0))
    return pl.pallas_call(
        final_kernel,
        grid=(count,),
        in_specs=[
            pl.BlockSpec((1, 4, quarter, features), lambda l: (l, 0, 0, 0)),
            side, side, image(rows + 2), image(rows), image(rows), vector,
            pl.BlockSpec((16, features), lambda l: (0, 0)),
        ],
        out_specs=[
            image(rows),
            pl.BlockSpec((16, features), lambda l: (0, 0)),
            pl.BlockSpec((1, 8, features), lambda l: (l, 0, 0)),
        ],
        out_shape=[
            jax.ShapeDtypeStruct(kept.shape, bfloat),
            jax.ShapeDtypeStruct((16, features), single),
            jax.ShapeDtypeStruct((count, 8, features), single),
        ],
        scratch_shapes=[pltpu.VMEM((rows + 2, COLUMN_PARTS + 2, sub, features), single)] * 2,
        compiler_params=params(60),
        cost_estimate=cost(kept.size * 180, kept.size * 12),
        name="final",
    )(d_reduced, top, bottom, normed, kept, d_middle, scale, taps)


def from_above(tail):
    count = lax.axis_size("strips")
    return lax.ppermute(tail, "strips", [(i, i + 1) for i in range(count - 1)])


def from_below(head):
    count = lax.axis_size("strips")
    return lax.ppermute(head, "strips", [(i + 1, i) for i in range(count - 1)])


def time_features(timesteps, halves):
    frequency = jnp.exp(-math.log(10000.0) * jnp.arange(halves, dtype=jnp.float32) / halves)
    phase = timesteps.astype(jnp.float32)[:, None] * frequency[None, :]
    return jnp.concatenate([jnp.cos(phase), jnp.sin(phase)], axis=1)


def thirds(value):
    high = value.astype(bfloat)
    rest = value - high.astype(single)
    middle = rest.astype(bfloat)
    low = (rest - middle.astype(single)).astype(bfloat)
    return jnp.concatenate([high, middle, low], axis=0)


def exact(value, weight, nt=False):
    n = value.shape[0]
    out = (dot_nt if nt else dot)(thirds(value), weight)
    return out[:n] + out[n : 2 * n] + out[2 * n :]


def silu(value):
    return value * (1.0 / (1.0 + jnp.exp(-value)))


def silu_slope(value):
    gate = 1.0 / (1.0 + jnp.exp(-value))
    return gate * (1.0 + value * (1.0 - gate))


def label_rows(labels, classes):
    return (lax.broadcasted_iota(jnp.int32, (labels.shape[0], classes), 1) == labels).astype(bfloat)


def condition(sinus, labels, wi_ref, bi_ref, wo_ref, bo_ref, table_ref):
    before = exact(sinus, wi_ref[...]) + bi_ref[...]
    inner = silu(before)
    onehot = label_rows(labels, table_ref.shape[1])
    cond = exact(inner, wo_ref[...]) + bo_ref[...] + dot_nt(onehot, table_ref[...])
    return before, inner, cond


def modulate_kernel(
    sinus_ref, label_ref, wi_ref, bi_ref, wo_ref, bo_ref, table_ref, ada_ref, ab_ref, out_ref, active
):
    @pl.when(pl.program_id(0) == 0)
    def _():
        cond = condition(
            sinus_ref[...], label_ref[...], wi_ref, bi_ref, wo_ref, bo_ref, table_ref
        )[2]
        active[...] = silu(cond)

    out_ref[0] = exact(active[...], ada_ref[...]) + ab_ref[...]


def modulate(sinus, labels, weights, ada, ada_bias):
    n = sinus.shape[0]
    features = ada.shape[0]
    whole = lambda a: pl.BlockSpec(a.shape, lambda s: (0,) * a.ndim)
    return pl.pallas_call(
        modulate_kernel,
        grid=(6,),
        in_specs=[whole(a) for a in (sinus, labels) + weights]
        + [
            pl.BlockSpec((features, features), lambda s: (0, s)),
            pl.BlockSpec((1, features), lambda s: (0, s)),
        ],
        out_specs=pl.BlockSpec((1, n, features), lambda s: (s, 0, 0)),
        out_shape=jax.ShapeDtypeStruct((6, n, features), single),
        scratch_shapes=[pltpu.VMEM((n, features), single)],
        compiler_params=params(16),
        cost_estimate=cost(50 * n * ada.size, 2 * ada.size),
        name="modulate",
    )(sinus, labels, *weights, ada, ada_bias)


def own_rows(me_ref, value, size):
    width = value.shape[1]
    place = lax.broadcasted_iota(jnp.int32, (size, width), 1)
    line = lax.broadcasted_iota(jnp.int32, (size, width), 0)
    pick = (place == me_ref[0] * size + line).astype(single)
    return lax.dot_general(
        pick, value, (((1,), (1,)), ((), ())), precision=highest, preferred_element_type=single
    )


def exact_small(a, b):
    return lax.dot_general(
        a, b, (((1,), (0,)), ((), ())), precision=highest, preferred_element_type=single
    )


def strip_sum(ref, kinds, count, features):
    lines = []
    for item in range(ref.shape[0]):
        for l in range(count):
            at = l * kinds * features
            lines.append(jnp.sum(
                    ref[item, :, at : at + kinds * features].astype(single), axis=0, keepdims=True
                ))
    return jnp.concatenate(lines, axis=0)


def early_kernel(
    count, me_ref, parts_ref, sinus_ref, label_ref, wi_ref, bi_ref, wo_ref, bo_ref, table_ref, ada_ref,
    before_ref, cond_ref, d_active_ref, ada_out_ref, d_mod_ref,
):
    features = ada_ref.shape[0]
    d_mod = strip_sum(parts_ref, 4, count, features)
    before, _, cond = condition(
        sinus_ref[...], label_ref[...], wi_ref, bi_ref, wo_ref, bo_ref, table_ref
    )
    before_ref[...] = before
    cond_ref[...] = cond
    d_active_ref[...] = exact(d_mod, ada_ref[:, 2 * features :], nt=True)
    size = ada_out_ref.shape[0]
    ada_out_ref[...] = exact_small(own_rows(me_ref, silu(cond), size), d_mod)
    d_mod_ref[...] = jnp.sum(d_mod, axis=0, keepdims=True)


def early_condition(me, parts, count, sinus, labels, weights, ada, size):
    n = sinus.shape[0]
    features = ada.shape[0]
    whole = lambda a: pl.BlockSpec(a.shape, lambda s: (0,) * a.ndim)
    shapes = [
        jax.ShapeDtypeStruct((n, features), single),
        jax.ShapeDtypeStruct((n, features), single),
        jax.ShapeDtypeStruct((n, features), single),
        jax.ShapeDtypeStruct((size, 4 * features), single),
        jax.ShapeDtypeStruct((1, 4 * features), single),
    ]
    return pl.pallas_call(
        partial(early_kernel, count),
        grid=(1,),
        in_specs=[pl.BlockSpec(memory_space=pltpu.SMEM)]
        + [whole(a) for a in (parts, sinus, labels) + weights + (ada,)],
        out_specs=[whole(a) for a in shapes],
        out_shape=shapes,
        compiler_params=params(28),
        cost_estimate=cost(50 * n * ada.size, 2 * ada.size),
        name="early_condition",
    )(me, parts, sinus, labels, *weights, ada)


def late_kernel(
    count, me_ref, parts_ref, before_ref, cond_ref, d_active_ref, ada_early_ref, d_mod_early_ref,
    sinus_ref, label_ref, wo_ref, ada_ref,
    ada_out_ref, d_mod_ref, table_out_ref, wo_out_ref, wi_out_ref, d_cond_ref, d_before_ref,
):
    features = wo_ref.shape[0]
    before = before_ref[...]
    cond = cond_ref[...]
    d_mod = strip_sum(parts_ref, 2, count, features)
    d_active = d_active_ref[...] + exact(d_mod, ada_ref[...], nt=True)
    d_cond = d_active * silu_slope(cond)
    d_before = exact(d_cond, wo_ref[...], nt=True) * silu_slope(before)
    size = ada_out_ref.shape[0]
    ada_out_ref[:, : 2 * features] = exact_small(own_rows(me_ref, silu(cond), size), d_mod)
    ada_out_ref[:, 2 * features :] = ada_early_ref[...]
    d_mod_ref[:, : 2 * features] = jnp.sum(d_mod, axis=0, keepdims=True)
    d_mod_ref[:, 2 * features :] = d_mod_early_ref[...]
    onehot = label_rows(label_ref[...], table_out_ref.shape[1]).astype(single)
    table_out_ref[...] = exact_small(own_rows(me_ref, d_cond, size), onehot)
    wo_out_ref[...] = exact_small(own_rows(me_ref, silu(before), size), d_cond)
    wi_out_ref[...] = exact_small(
        own_rows(me_ref, sinus_ref[...], wi_out_ref.shape[0]), d_before
    )
    d_cond_ref[...] = jnp.sum(d_cond, axis=0, keepdims=True)
    d_before_ref[...] = jnp.sum(d_before, axis=0, keepdims=True)


def late_condition(
    me, parts, count, before, cond, d_active, ada_early, d_mod_early, sinus, labels, wo, ada, classes,
    devices,
):
    features = ada.shape[0]
    size = features // devices
    whole = lambda a: pl.BlockSpec(a.shape, lambda s: (0,) * a.ndim)
    shapes = [
        jax.ShapeDtypeStruct((size, 6 * features), single),
        jax.ShapeDtypeStruct((1, 6 * features), single),
        jax.ShapeDtypeStruct((size, classes), single),
        jax.ShapeDtypeStruct((size, features), single),
        jax.ShapeDtypeStruct((sinus.shape[1] // devices, features), single),
        jax.ShapeDtypeStruct((1, features), single),
        jax.ShapeDtypeStruct((1, features), single),
    ]
    return pl.pallas_call(
        partial(late_kernel, count),
        grid=(1,),
        in_specs=[pl.BlockSpec(memory_space=pltpu.SMEM)]
        + [
            whole(a)
            for a in (parts, before, cond, d_active, ada_early, d_mod_early, sinus, labels, wo)
        ]
        + [pl.BlockSpec((features, 2 * features), lambda s: (0, 0))],
        out_specs=[whole(a) for a in shapes],
        out_shape=shapes,
        compiler_params=params(16),
        cost_estimate=cost(20 * ada.size, ada.size),
        name="late_condition",
    )(me, parts, before, cond, d_active, ada_early, d_mod_early, sinus, labels, wo, ada)


def sum_cores(keep, give):
    strips = lax.axis_size("strips")
    got = lax.ppermute(give, "strips", [(i, i ^ 1) for i in range(strips)])
    return (keep.astype(single) + got.astype(single)).astype(bfloat)


def sum_axis(part, axis, size, place, step):
    pick = lambda k: lax.dynamic_index_in_dim(part, place ^ k, 0, keepdims=False)
    count = lax.axis_size(axis)
    got = [
        lax.ppermute(pick(k), axis, [(i, i ^ (k * step)) for i in range(count)])
        for k in range(1, size)
    ]
    total = pick(0).astype(single)
    for g in got:
        total = total + g.astype(single)
    return total


def sum_items(part):
    return sum_axis(part, "items", lax.axis_size("items"), lax.axis_index("items"), 1).astype(bfloat)


def sum_strips(part):
    strip = lax.axis_index("strips")
    return sum_axis(part, "strips", lax.axis_size("strips") // 2, strip // 2, 2)


def after(value, *others):
    return lax.optimization_barrier((value,) + others)[0]


def tap_rows(kernel):
    return jnp.pad(kernel.astype(single).T, ((0, 7), (0, 0)))


def per_device(
    latents,
    timesteps,
    labels,
    time_in_weight,
    time_in_bias,
    time_out_weight,
    time_out_bias,
    label_table,
    ada_weight,
    ada_bias,
    down_kernel,
    down_bias,
    input_weight,
    query_bias,
    value_bias,
    output_weight,
    output_bias,
    expand_weight,
    expand_bias,
    mixer_kernel,
    mixer_bias,
    shrink_weight,
    shrink_bias,
    cotangent,
):
    count, rows, columns, features = latents.shape
    strips = lax.axis_size("strips")
    items = lax.axis_size("items")
    devices = strips * items
    strip = lax.axis_index("strips")
    item = lax.axis_index("items")
    me = item * strips + strip
    sub = columns // COLUMN_PARTS
    quarter = rows * columns // 4
    groups = count * 4
    share = strips // groups
    width = features // share
    row_vector = lambda v: v.astype(single).reshape(1, -1)
    edge = jnp.stack([strip > 0, strip < strips - 1]).astype(single)

    lines = -(-count // 8) * 8
    weights = (
        time_in_weight, row_vector(time_in_bias), time_out_weight, row_vector(time_out_bias),
        label_table,
    )
    waves = time_in_weight.shape[0] // 2
    modulation = modulate(
        time_features(jnp.pad(timesteps, (0, lines - count)), waves),
        jnp.pad(labels, (0, lines - count))[:, None],
        weights,
        ada_weight,
        row_vector(ada_bias),
    )
    shift_a, scale_a, gate_a, shift_b, scale_b, gate_b = (
        modulation[i, :count, None, :] for i in range(6)
    )

    ends = jnp.concatenate([latents[:, -1:], cotangent[:, -1:]], axis=1)
    starts = jnp.concatenate([latents[:, :1], cotangent[:, :1]], axis=1)
    above = from_above(ends)
    below = from_below(starts)

    down_taps = tap_rows(down_kernel)
    grouped, normed_a, kept = front(
        edge, latents, above[:, :1], below[:, :1], scale_a, shift_a, down_taps, row_vector(down_bias)
    )

    def spread(array):
        flat = array.reshape(groups, quarter, array.shape[-1])
        if share > 1:
            flat = jnp.repeat(flat, share, axis=0)
        got = lax.all_to_all(flat, "strips", 0, 0, tiled=True)
        return got.reshape(strips * quarter, array.shape[-1])

    def collect(array):
        flat = array.reshape(strips, quarter, array.shape[-1])
        return lax.all_to_all(flat, "strips", 0, 0, tiled=True)

    group = spread(grouped)
    g_kept, d_branch, grad_shrink_bias = upstream_parts(
        cotangent, above[:, 1:], below[:, 1:], gate_b
    )

    head_at = (strip % share) * width
    def own_columns(array, axis):
        return array if share == 1 else lax.dynamic_slice_in_dim(array, head_at, width, axis=axis)

    own_weight = jnp.concatenate(
        [own_columns(input_weight[:, i * features : (i + 1) * features], 1) for i in range(3)], axis=1
    ) if share > 1 else input_weight
    own_bias = jnp.concatenate(
        [own_columns(row_vector(b), 1) for b in (query_bias, value_bias)], axis=1
    )
    piece = width // CHUNKS
    saved = []
    mixed = []
    d_act = feed_upstream(d_branch, shrink_weight)
    group, d_act, expand_line, mixer_taps, mixer_line, output_line, shrink_line = (
        lax.optimization_barrier(
            (
                group,
                d_act,
                row_vector(expand_bias),
                tap_rows(mixer_kernel),
                row_vector(mixer_bias),
                row_vector(output_bias),
                row_vector(shrink_bias),
            )
        )
    )
    for c in range(CHUNKS):
        saved.append(attend(group, own_weight, own_bias, c * piece, piece))
        mixed.append(collect(saved[c][3]))
    if share == 1:
        mixed = [m.reshape(count, 4, quarter, piece) for m in mixed]
    else:
        joined = jnp.concatenate(mixed, axis=-1).reshape(groups, share, quarter, width)
        joined = joined.transpose(0, 2, 1, 3).reshape(count, 4, quarter, features)
        mixed = [joined]

    attended, middle, normed_b, first_rows, last_rows = middle_part(
        mixed, output_weight, output_line, kept, gate_a, scale_b, shift_b
    )
    act, d_hid, feed_small = feed_forward(
        edge,
        normed_b,
        from_above(last_rows),
        from_below(first_rows),
        d_act,
        expand_weight,
        expand_line,
        mixer_taps,
        mixer_line,
    )
    turned = turn(
        act, d_hid, middle, attended, g_kept, gate_b, scale_b, gate_a, shrink_line,
        output_weight, shrink_weight, expand_weight, mixed,
    )
    result, d_middle = turned[:2]
    d_mixed = turned[2:-2]
    grad_output, turn_sums = turned[-2:]

    hidden = expand_weight.shape[1]
    steps = hidden // features
    early = feed_grads(act, d_hid, normed_b, d_branch, devices)
    early_sum = lax.psum_scatter(early, both, scatter_dimension=0, tiled=False).astype(single)

    if share == 1:
        d_mixed = [spread(d) for d in d_mixed]
    else:
        parts = d_mixed[0].reshape(groups, quarter, share, width).transpose(0, 2, 1, 3)
        got = lax.all_to_all(parts.reshape(strips, quarter, width), "strips", 0, 0, tiled=True)
        got = got.reshape(strips * quarter, width)
        d_mixed = [got[:, c * piece : (c + 1) * piece] for c in range(CHUNKS)]
    grads = []
    for c in range(CHUNKS):
        if c == 0:
            d_mixed[c], _ = lax.optimization_barrier((d_mixed[c], early))
        q, k, v, out, logs = saved[c]
        grads.append(attend_back(q, k, v, out, d_mixed[c], logs))
    size = features // devices
    narrow = jnp.stack([jnp.sum(turn_sums[:, 4], axis=0), jnp.sum(grad_shrink_bias[:, 0], axis=0)])
    to_all = jnp.concatenate(
        [
            turn_sums[:, 3], turn_sums[:, 1], turn_sums[:, 2], turn_sums[:, 0],
        ],
        axis=1,
    ).reshape(-1)
    whole_numbers = jnp.concatenate([timesteps // 32, timesteps % 32, labels // 32, labels % 32])
    to_all = jnp.concatenate([to_all, whole_numbers.astype(single)])
    fill = -(to_all.shape[0] + 11 * (hidden // devices) + 2 * size) % LANES
    early_small = jnp.concatenate(
        [
            jnp.broadcast_to(to_all, (devices, to_all.shape[0])),
            feed_small[:11].reshape(11, devices, -1).transpose(1, 0, 2).reshape(devices, -1),
            narrow.reshape(2, devices, -1).transpose(1, 0, 2).reshape(devices, -1),
            jnp.zeros((devices, fill), single),
        ],
        axis=1,
    ).astype(bfloat)
    early_small = after(early_small, grads[0][0], *d_mixed)
    early_got = lax.all_to_all(early_small, both, 0, 0, tiled=True)

    parts = [g for chunk in grads for g in chunk]
    d_group = regroup(parts, own_weight)
    d_reduced = collect(d_group)
    if share > 1:
        d_reduced = jnp.sum(
            d_reduced.reshape(groups, share, quarter, features).astype(single), axis=1
        ).astype(bfloat)
    d_reduced = d_reduced.reshape(count, 4, quarter, features)
    late, d_sums = input_grad(after(group, d_group), grad_output, parts)
    d_query_sum = d_sums[0, :width]
    d_value_sum = d_sums[0, width:]
    if share > 1:
        zero = jnp.zeros((features, 3, features), bfloat)
        grad_input = lax.dynamic_update_slice(
            zero, late[:, : 3 * width].reshape(features, 3, width), (0, 0, head_at)
        ).reshape(features, 3 * features)
        late = jnp.concatenate([grad_input, grad_output], axis=1)
        flat = jnp.zeros((features,), single)
        d_query_sum = lax.dynamic_update_slice(flat, d_query_sum, (head_at,))
        d_value_sum = lax.dynamic_update_slice(flat, d_value_sum, (head_at,))
    late = late.reshape(items, strips // 2, 2, size, 4 * features)
    core = strip % 2
    keep = lax.dynamic_index_in_dim(late, core, 2, keepdims=False)
    give = lax.dynamic_index_in_dim(late, 1 - core, 2, keepdims=False)

    per_latent = count * 4 * features
    parts_early = early_got[:, :per_latent].reshape(items, strips, per_latent)
    first = early_got.reshape(items, strips, -1)[:, 0, per_latent : per_latent + 4 * count]
    first = first.astype(single).reshape(items, 4, count)
    all_times = (first[:, 0] * 32.0 + first[:, 1]).reshape(-1)
    all_labels = (first[:, 2] * 32.0 + first[:, 3]).reshape(-1, 1).astype(jnp.int32)
    sinus = time_features(all_times, waves)
    early_sums = jnp.sum(early_got[:, per_latent + 4 * count :].astype(single), axis=0)
    cut = 11 * (hidden // devices)
    feed_sum = early_sums[:cut].reshape(11, -1)
    narrow_sum = early_sums[cut : cut + 2 * size].reshape(2, size)
    index = jnp.reshape(me, (1,)).astype(jnp.int32)
    before, cond, d_active, grad_ada_early, d_mod_early = early_condition(
        index, parts_early, count, sinus, all_labels, weights, ada_weight, size
    )

    d_reduced, before, keep, give = lax.optimization_barrier((d_reduced, before, keep, give))
    late_part = sum_items(sum_cores(keep, give))
    grad_latents, down_small, final_sums = final(
        d_reduced,
        from_above(d_reduced[:, 2:, -2 * sub :]),
        from_below(d_reduced[:, :2, : 2 * sub]),
        normed_a,
        kept,
        d_middle,
        scale_a,
        down_taps,
    )

    late_narrow = jnp.concatenate([d_query_sum[None], d_value_sum[None], down_small[:10]], axis=0)
    to_all = final_sums[:, :2].reshape(-1)
    fill = -(to_all.shape[0] + 12 * size) % LANES
    late_small = jnp.concatenate(
        [
            jnp.broadcast_to(to_all, (devices, to_all.shape[0])),
            late_narrow.reshape(12, devices, size).transpose(1, 0, 2).reshape(devices, -1),
            jnp.zeros((devices, fill), single),
        ],
        axis=1,
    ).astype(bfloat)
    late_got = lax.all_to_all(late_small, both, 0, 0, tiled=True)
    late_got, late_part = lax.optimization_barrier((late_got, late_part))
    late_sum = sum_strips(late_part)
    late_sums = jnp.sum(late_got[:, to_all.shape[0] :].astype(single), axis=0)[: 12 * size].reshape(12, size)
    (
        grad_ada, d_mod, grad_table, grad_time_out, grad_time_in, d_cond, d_before,
    ) = late_condition(
        index,
        late_got[:, : to_all.shape[0]].reshape(items, strips, -1),
        count,
        before,
        cond,
        d_active,
        grad_ada_early,
        d_mod_early,
        sinus,
        all_labels,
        time_out_weight,
        ada_weight,
        label_table.shape[1],
        devices,
    )

    def mine(array):
        part = array.shape[-1] // devices
        return lax.dynamic_slice_in_dim(array[0], me * part, part, axis=0)

    return (
        result,
        grad_latents,
        grad_time_in,
        mine(d_before),
        grad_time_out,
        mine(d_cond),
        grad_table,
        grad_ada,
        mine(d_mod),
        late_sums[2:11].T,
        late_sums[11],
        late_sum[:, : 3 * features],
        late_sums[0],
        late_sums[1],
        late_sum[:, 3 * features :],
        narrow_sum[0],
        early_sum[steps:].transpose(1, 0, 2).reshape(size, hidden),
        feed_sum[10],
        feed_sum[:9].T,
        feed_sum[9],
        early_sum[:steps].reshape(hidden // devices, features),
        narrow_sum[1],
    )


def solution(mesh):
    image = P("items", "strips", None, None)
    split = P(both, None)
    line = P(both)
    return jax.shard_map(
        per_device,
        mesh=mesh,
        in_specs=(image, P("items"), P("items")) + (P(),) * 20 + (image,),
        out_specs=(
            image, image, split, line, split, line, split, split, line, split, line,
            split, line, line, split, line, split, line, split, line, split, line,
        ),
        check_vma=False,
    )
```

```python
from functools import partial
import math

import jax
import jax.numpy as jnp
from jax import lax
from jax.experimental import pallas as pl
from jax.experimental.pallas import tpu as pltpu
from jax.sharding import PartitionSpec as P

HEADS = 12
HEAD_DIM = 64
LANES = 128
COLUMN_PARTS = 4
CHUNKS = 2

highest = lax.Precision.HIGHEST
epsilon = 1e-06
bfloat = jnp.bfloat16
single = jnp.float32
both = ("items", "strips")


def params(mebibytes):
    return pltpu.CompilerParams(vmem_limit_bytes=mebibytes * 1024 * 1024)


def cost(flops, moved, exps=0):
    return pl.CostEstimate(flops=int(flops), bytes_accessed=int(moved), transcendentals=int(exps))


def dot(a, b):
    return lax.dot_general(a, b, (((1,), (0,)), ((), ())), preferred_element_type=single)


def dot_nt(a, b):
    return lax.dot_general(a, b, (((1,), (1,)), ((), ())), preferred_element_type=single)


def dot_tn(a, b):
    return lax.dot_general(a, b, (((0,), (0,)), ((), ())), preferred_element_type=single)


def column_order(columns, back):
    sub = columns // COLUMN_PARTS
    first = lax.broadcasted_iota(jnp.int32, (columns, columns), 0)
    second = lax.broadcasted_iota(jnp.int32, (columns, columns), 1)
    kept, column = (second, first) if back else (first, second)
    return (column == COLUMN_PARTS * (kept % sub) + kept // sub).astype(bfloat)


def norm_parts(value):
    center = value - jnp.mean(value, axis=-1, keepdims=True)
    inverse = lax.rsqrt(jnp.mean(center * center, axis=-1, keepdims=True) + epsilon)
    return center * inverse, inverse


def norm_back(normed, inverse, grad):
    return inverse * (
        grad
        - jnp.mean(grad, axis=-1, keepdims=True)
        - normed * jnp.mean(grad * normed, axis=-1, keepdims=True)
    )


def put_wide(ref, row, cells):
    sub = cells.shape[1]
    place = lax.broadcasted_iota(jnp.int32, cells.shape[1:], 0)
    last = cells[COLUMN_PARTS - 1].astype(single)
    first = cells[0].astype(single)
    ref[row, 1 : COLUMN_PARTS + 1] = cells
    ref[row, 0] = jnp.where(place == 0, 0.0, pltpu.roll(last, 1, 0)).astype(ref.dtype)
    ref[row, COLUMN_PARTS + 1] = jnp.where(
        place == sub - 1, 0.0, pltpu.roll(first, sub - 1, 0)
    ).astype(ref.dtype)


def put_part(ref, row, j, cells):
    sub = cells.shape[0]
    place = lax.broadcasted_iota(jnp.int32, cells.shape, 0)
    ref[row, j + 1] = cells
    if j == COLUMN_PARTS - 1:
        ref[row, 0] = jnp.where(place == 0, 0.0, pltpu.roll(cells, 1, 0))
    if j == 0:
        ref[row, COLUMN_PARTS + 1] = jnp.where(place == sub - 1, 0.0, pltpu.roll(cells, sub - 1, 0))


def conv_low(ref, row, taps):
    total = None
    for i in range(3):
        line = [taps[3 * i + j] * ref[row + i, j : j + COLUMN_PARTS] for j in range(3)]
        line = (line[0] + line[1]) + line[2]
        total = line if total is None else total + line
    return total


def conv_back_row(ref, row, taps):
    total = None
    for i in range(3):
        line = [
            taps[3 * i + j] * ref[row + 2 - i, 2 - j : 2 - j + COLUMN_PARTS] for j in range(3)
        ]
        line = (line[0] + line[1]) + line[2]
        total = line if total is None else total + line
    return total


def front_kernel(
    edge_ref, x_ref, top_ref, bottom_ref, scale_ref, shift_ref, taps_ref, bias_ref,
    grouped_ref, normed_ref, kept_ref, wide,
):
    rows, columns, features = x_ref.shape[1:]
    sub = columns // COLUMN_PARTS
    order = column_order(columns, False)
    scale = 1.0 + scale_ref[0]
    shift = shift_ref[0]

    def fill(row, raw, keep, kept_row=None):
        cells = dot(order, raw)
        if kept_row is not None:
            kept_ref[0, kept_row] = cells.astype(bfloat)
        for j in range(COLUMN_PARTS):
            line = slice(j * sub, (j + 1) * sub)
            normed = norm_parts(cells[line])[0] * scale + shift
            low = (normed if keep is None else normed * keep).astype(bfloat)
            normed_ref[0, row, line] = low
            put_part(wide, row, j, low.astype(single))

    fill(0, top_ref[0, 0], edge_ref[0])
    fill(rows + 1, bottom_ref[0, 0], edge_ref[1])

    for row in range(rows):
        fill(row + 1, x_ref[0, row], None, row)

    taps = [taps_ref[t : t + 1] for t in range(9)]
    bias = bias_ref[...]

    @pl.loop(0, rows // 2)
    def _(pair):
        for a in range(2):
            for lane in range(0, features, LANES):
                at = pl.ds(lane, LANES)
                total = jnp.zeros((COLUMN_PARTS, sub, LANES), single) + bias[:, lane : lane + LANES]
                for i in range(3):
                    for j in range(3):
                        total = total + taps[3 * i + j][:, lane : lane + LANES] * wide[
                            pair * 2 + a + i, j : j + COLUMN_PARTS, :, at
                        ]
                low = total.astype(bfloat)
                for j in range(COLUMN_PARTS):
                    grouped_ref[
                        0, 2 * a + j % 2, pl.ds(pl.multiple_of((pair * 2 + j // 2) * sub, sub), sub), at
                    ] = low[j]


def front(edge, latents, top, bottom, scale, shift, taps, bias):
    count, rows, columns, features = latents.shape
    quarter = rows * columns // 4
    sub = columns // COLUMN_PARTS
    image = lambda r: pl.BlockSpec((1, r, columns, features), lambda l: (l, 0, 0, 0))
    vector = pl.BlockSpec((1, 1, features), lambda l: (l, 0, 0))
    return pl.pallas_call(
        front_kernel,
        grid=(count,),
        in_specs=[
            pl.BlockSpec(memory_space=pltpu.SMEM),
            image(rows), image(1), image(1), vector, vector,
            pl.BlockSpec((16, features), lambda l: (0, 0)),
            pl.BlockSpec((1, features), lambda l: (0, 0)),
        ],
        out_specs=[
            pl.BlockSpec((1, 4, quarter, features), lambda l: (l, 0, 0, 0)),
            image(rows + 2), image(rows),
        ],
        out_shape=[
            jax.ShapeDtypeStruct((count, 4, quarter, features), bfloat),
            jax.ShapeDtypeStruct((count, rows + 2, columns, features), bfloat),
            jax.ShapeDtypeStruct((count, rows, columns, features), bfloat),
        ],
        scratch_shapes=[pltpu.VMEM((rows + 2, COLUMN_PARTS + 2, sub, features), single)],
        compiler_params=params(18),
        cost_estimate=cost(count * rows * columns * features * 150, count * rows * columns * features * 8),
        name="front",
    )(edge, latents, top, bottom, scale, shift, taps, bias)


def upstream_kernel(g_ref, top_ref, bottom_ref, gate_ref, kept_ref, branch_ref, bias_ref):
    rows, columns, features = g_ref.shape[1:]
    order = column_order(columns, False)
    gate = gate_ref[0]

    def low(raw):
        cells = dot(order, raw)
        return cells, (cells * gate).astype(bfloat)

    branch_ref[0, 0] = low(top_ref[0, 0])[1]
    branch_ref[0, rows + 1] = low(bottom_ref[0, 0])[1]

    def step(row, total):
        cells, grad = low(g_ref[0, row])
        kept_ref[0, row] = cells.astype(bfloat)
        branch_ref[0, row + 1] = grad
        return total + jnp.sum(grad.astype(single), axis=0, keepdims=True)

    total = jnp.zeros((1, features), single)
    for row in range(rows):
        total = step(row, total)
    bias_ref[0] = total


def upstream_parts(cotangent, top, bottom, gate):
    count, rows, columns, features = cotangent.shape
    image = lambda r: pl.BlockSpec((1, r, columns, features), lambda l: (l, 0, 0, 0))
    vector = pl.BlockSpec((1, 1, features), lambda l: (l, 0, 0))
    return pl.pallas_call(
        upstream_kernel,
        grid=(count,),
        in_specs=[image(rows), image(1), image(1), vector],
        out_specs=[image(rows), image(rows + 2), vector],
        out_shape=[
            jax.ShapeDtypeStruct((count, rows, columns, features), bfloat),
            jax.ShapeDtypeStruct((count, rows + 2, columns, features), bfloat),
            jax.ShapeDtypeStruct((count, 1, features), single),
        ],
        compiler_params=params(14),
        cost_estimate=cost(count * rows * columns * features * 130, count * rows * columns * features * 6),
        name="upstream",
    )(cotangent, top, bottom, gate)


QUERY_STEP = 1024
QUERY_STEP_BACK = 256


def attend_kernel(
    x_ref, wq_ref, wk_ref, wv_ref, bq_ref, bv_ref, q_ref, k_ref, v_ref, mixed_ref, log_ref
):
    tokens = x_ref.shape[0]
    base = math.log2(math.e) / math.sqrt(HEAD_DIM)
    x = x_ref[...]
    q_ref[...] = (dot(x, wq_ref[...]) + bq_ref[...]).astype(bfloat)
    k_ref[...] = dot(x, wk_ref[...]).astype(bfloat)
    v_ref[...] = (dot(x, wv_ref[...]) + bv_ref[...]).astype(bfloat)
    keys = k_ref[...]
    values = v_ref[...].T
    lane = lax.broadcasted_iota(jnp.int32, (QUERY_STEP, LANES), 1)
    for at in range(0, tokens, QUERY_STEP):
        part = q_ref[at : at + QUERY_STEP]
        outs = []
        for head in range(LANES // HEAD_DIM):
            own = jnp.where(lane // HEAD_DIM == head, part, jnp.zeros_like(part))
            scores = dot_nt(keys, own)
            peak = jnp.max(scores, axis=0, keepdims=True) * base
            soft = jnp.exp2(scores * base - peak)
            total = jnp.sum(soft, axis=0, keepdims=True)
            log_ref[0, head : head + 1, at : at + QUERY_STEP] = peak + jnp.log2(total)
            out = dot(values[head * HEAD_DIM : (head + 1) * HEAD_DIM], soft.astype(bfloat))
            outs.append(out * (1.0 / total))
        mixed_ref[at : at + QUERY_STEP] = jnp.concatenate(outs, axis=0).T.astype(bfloat)


def attend(x, weights, biases, first, width):
    tokens, features = x.shape
    pairs = width // LANES
    start = first // LANES
    stride = weights.shape[1] // 3 // LANES
    weight = lambda i: pl.BlockSpec((features, LANES), lambda h: (0, i * stride + start + h))
    bias = lambda i: pl.BlockSpec((1, LANES), lambda h: (0, i * stride + start + h))
    column = pl.BlockSpec((tokens, LANES), lambda h: (0, h))
    lows = jax.ShapeDtypeStruct((tokens, width), bfloat)
    return pl.pallas_call(
        attend_kernel,
        grid=(pairs,),
        in_specs=[pl.BlockSpec((tokens, features), lambda h: (0, 0))]
        + [weight(0), weight(1), weight(2), bias(0), bias(1)],
        out_specs=[column] * 4 + [pl.BlockSpec((1, 2, tokens), lambda h: (h, 0, 0))],
        out_shape=[lows] * 4 + [jax.ShapeDtypeStruct((pairs, 2, tokens), single)],
        compiler_params=params(60),
        cost_estimate=cost(
            6 * tokens * features * width + 16 * tokens * tokens * width,
            2 * tokens * features + 8 * tokens * width + 6 * features * width,
            2 * pairs * tokens * tokens,
        ),
        name="attend",
    )(x, weights, weights, weights, biases, biases)


def attend_back_kernel(
    q_ref, k_ref, v_ref, mixed_ref, grad_ref, log_ref, dq_ref, dk_ref, dv_ref, dk_sum, dv_sum
):
    tokens = q_ref.shape[0]
    scale = 1.0 / math.sqrt(HEAD_DIM)
    base = math.log2(math.e) * scale
    keys = k_ref[...]
    values = v_ref[...]
    keys_turned = keys.T
    lane = lax.broadcasted_iota(jnp.int32, (QUERY_STEP_BACK, LANES), 1)
    for at in range(0, tokens, QUERY_STEP_BACK):
        rows = slice(at, at + QUERY_STEP_BACK)
        part = q_ref[rows]
        grad = grad_ref[rows]
        shares = (grad.astype(single) * mixed_ref[rows].astype(single)).T
        outs = []
        for head in range(LANES // HEAD_DIM):
            mine = lane // HEAD_DIM == head
            own = jnp.where(mine, part, jnp.zeros_like(part))
            own_grad = jnp.where(mine, grad, jnp.zeros_like(grad))
            share = jnp.sum(
                shares[head * HEAD_DIM : (head + 1) * HEAD_DIM], axis=0, keepdims=True
            )
            soft = jnp.exp2(dot_nt(keys, own) * base - log_ref[0, head : head + 1, rows])
            d_scores = (soft * (dot_nt(values, own_grad) - share)).astype(bfloat)
            dv_part = dot(soft.astype(bfloat), own_grad)
            dk_part = dot(d_scores, own)
            if at == 0 and head == 0:
                dv_sum[...] = dv_part
                dk_sum[...] = dk_part
            else:
                dv_sum[...] += dv_part
                dk_sum[...] += dk_part
            outs.append(dot(keys_turned[head * HEAD_DIM : (head + 1) * HEAD_DIM], d_scores))
        dq_ref[rows] = (jnp.concatenate(outs, axis=0) * scale).T.astype(bfloat)
    dk_ref[...] = (dk_sum[...] * scale).astype(bfloat)
    dv_ref[...] = dv_sum[...].astype(bfloat)


def attend_back(q, k, v, mixed, grad, logs):
    tokens, width = q.shape
    pairs = width // LANES
    column = pl.BlockSpec((tokens, LANES), lambda h: (0, h))
    lows = jax.ShapeDtypeStruct((tokens, width), bfloat)
    return pl.pallas_call(
        attend_back_kernel,
        grid=(pairs,),
        in_specs=[column] * 5 + [pl.BlockSpec((1, 2, tokens), lambda h: (h, 0, 0))],
        out_specs=[column] * 3,
        out_shape=[lows] * 3,
        scratch_shapes=[pltpu.VMEM((tokens, LANES), single)] * 2,
        compiler_params=params(60),
        cost_estimate=cost(
            40 * tokens * tokens * width, 16 * tokens * width, 2 * pairs * tokens * tokens
        ),
        name="attend_back",
    )(q, k, v, mixed, grad, logs)


def regroup_kernel(*refs):
    parts, weight_ref, out_ref = refs[:-2], refs[-2], refs[-1]
    count = len(parts) // 3
    piece = parts[0].shape[1]
    third = weight_ref.shape[1] // 3
    total = None
    for c in range(count):
        for i in range(3):
            at = i * third + c * piece
            term = dot_nt(parts[3 * c + i][...], weight_ref[:, at : at + piece])
            total = term if total is None else total + term
    out_ref[...] = total.astype(bfloat)


def regroup(parts, weight):
    tokens, piece = parts[0].shape
    features = weight.shape[0]
    step = min(256, tokens)
    return pl.pallas_call(
        regroup_kernel,
        grid=(tokens // step,),
        in_specs=[pl.BlockSpec((step, piece), lambda t: (t, 0))] * len(parts)
        + [pl.BlockSpec(weight.shape, lambda t: (0, 0))],
        out_specs=pl.BlockSpec((step, features), lambda t: (t, 0)),
        out_shape=jax.ShapeDtypeStruct((tokens, features), bfloat),
        compiler_params=params(60),
        cost_estimate=cost(2 * tokens * features * weight.shape[1], 2 * tokens * features * 4),
        name="regroup",
    )(*parts, weight)


def input_grad_kernel(*refs):
    x_ref, other_ref = refs[0], refs[1]
    parts = refs[2:-2]
    out_ref, sums_ref = refs[-2:]
    count = len(parts) // 3
    tokens, piece = parts[0].shape
    third = count * piece
    turned = x_ref[...].T
    for c in range(count):
        for i in range(3):
            at = i * third + c * piece
            out_ref[:, at : at + piece] = dot(turned, parts[3 * c + i][...]).astype(bfloat)
    out_ref[:, 3 * third :] = other_ref[...]

    @pl.when(pl.program_id(0) == 0)
    def _():
        ones = jnp.ones((16, tokens), bfloat)
        for c in range(count):
            for i in (0, 2):
                total = dot(ones, parts[3 * c + i][...])
                sums_ref[:, i // 2 * third + c * piece : i // 2 * third + (c + 1) * piece] = total[:8]


def input_grad(x, other, parts):
    tokens, features = x.shape
    piece = parts[0].shape[1]
    third = piece * len(parts) // 3
    step = 256
    return pl.pallas_call(
        input_grad_kernel,
        grid=(features // step,),
        in_specs=[
            pl.BlockSpec((tokens, step), lambda t: (0, t)),
            pl.BlockSpec((step, other.shape[1]), lambda t: (t, 0)),
        ]
        + [pl.BlockSpec((tokens, piece), lambda t: (0, 0))] * len(parts),
        out_specs=[
            pl.BlockSpec((step, 3 * third + other.shape[1]), lambda t: (t, 0)),
            pl.BlockSpec((8, 2 * third), lambda t: (0, 0)),
        ],
        out_shape=[
            jax.ShapeDtypeStruct((features, 3 * third + other.shape[1]), bfloat),
            jax.ShapeDtypeStruct((8, 2 * third), single),
        ],
        compiler_params=params(60),
        cost_estimate=cost(6 * tokens * features * third, 2 * tokens * features * 5),
        name="input_grad",
    )(x, other, *parts)


def middle_kernel(
    parts, *refs
):
    mixed_refs = refs[:parts]
    weight_ref, bias_ref, x_ref, gate_ref, scale_ref, shift_ref = refs[parts : parts + 6]
    attended_ref, middle_ref, normed_ref, first_ref, last_ref, grouped = refs[parts + 6 :]
    rows, columns, features = x_ref.shape[1:]
    sub = columns // COLUMN_PARTS
    quarter = rows * columns // 4
    total = bias_ref[...]
    at = 0
    for ref in mixed_refs:
        width = ref.shape[-1]
        total = total + dot(ref[0].reshape(4 * quarter, width), weight_ref[at : at + width])
        at += width
    grouped[...] = total.reshape(4, quarter, features)
    gate = gate_ref[0]
    scale = 1.0 + scale_ref[0]
    shift = shift_ref[0]

    for pair in range(rows // 2):
        for a in range(2):
            row = pair * 2 + a
            for j in range(COLUMN_PARTS):
                line = slice(j * sub, (j + 1) * sub)
                cells = grouped[
                    2 * a + j % 2, pl.ds((pair * 2 + j // 2) * sub, sub)
                ]
                attended_ref[0, row, line] = cells
                middle = x_ref[0, row, line].astype(single) + gate * cells
                middle_ref[0, row, line] = middle
                low = (norm_parts(middle)[0] * scale + shift).astype(bfloat)
                normed_ref[0, row, line] = low
                if row < 2:
                    first_ref[0, row, line] = low
                if row >= rows - 2:
                    last_ref[0, row - rows + 2, line] = low


def middle_part(mixed, weight, bias, kept, gate, scale, shift):
    count, rows, columns, features = kept.shape
    quarter = rows * columns // 4
    image = pl.BlockSpec((1, rows, columns, features), lambda l: (l, 0, 0, 0))
    vector = pl.BlockSpec((1, 1, features), lambda l: (l, 0, 0))
    return pl.pallas_call(
        partial(middle_kernel, len(mixed)),
        grid=(count,),
        in_specs=[
            pl.BlockSpec((1, 4, quarter, m.shape[-1]), lambda l: (l, 0, 0, 0)) for m in mixed
        ]
        + [
            pl.BlockSpec((features, features), lambda l: (0, 0)),
            pl.BlockSpec((1, features), lambda l: (0, 0)),
            image, vector, vector, vector,
        ],
        out_specs=[image] * 3
        + [pl.BlockSpec((1, 2, columns, features), lambda l: (l, 0, 0, 0))] * 2,
        out_shape=[
            jax.ShapeDtypeStruct(kept.shape, single),
            jax.ShapeDtypeStruct(kept.shape, single),
            jax.ShapeDtypeStruct(kept.shape, bfloat),
        ]
        + [jax.ShapeDtypeStruct((count, 2, columns, features), bfloat)] * 2,
        scratch_shapes=[pltpu.VMEM((4, quarter, features), single)],
        compiler_params=params(60),
        cost_estimate=cost(2 * kept.size * features, 14 * kept.size),
        name="middle",
    )(*mixed, weight, bias, kept, gate, scale, shift)


def feed_upstream_kernel(db_ref, ws_ref, out_ref):
    out_ref[...] = dot_nt(db_ref[...], ws_ref[...]).astype(bfloat)


def feed_upstream(db, ws):
    count, tall, columns, features = db.shape
    hidden = ws.shape[0]
    lines = count * tall * columns
    return pl.pallas_call(
        feed_upstream_kernel,
        grid=(hidden // features,),
        in_specs=[
            pl.BlockSpec((lines, features), lambda s: (0, 0)),
            pl.BlockSpec((features, features), lambda s: (s, 0)),
        ],
        out_specs=pl.BlockSpec((lines, features), lambda s: (0, s)),
        out_shape=jax.ShapeDtypeStruct((lines, hidden), bfloat),
        compiler_params=params(60),
        cost_estimate=cost(2 * lines * features * hidden, 2 * lines * (features + hidden)),
        name="feed_upstream",
    )(db.reshape(lines, features), ws)


TURN_ROWS = 4


def feed_turn_kernel(parts, feeds, turns, *refs):
    (
        edge_ref, nb_ref, top_ref, bottom_ref, d_act_ref, we_ref, be_ref, taps_ref, bm_ref,
        middle_ref, attended_ref, g_ref, gate_b_ref, scale_ref, gate_a_ref, shrink_ref,
        ws_hbm, we_hbm, wo_hbm,
    ) = refs[:19]
    mixed_refs = refs[19 : 19 + parts]
    small_ref, act_hbm, d_hid_hbm, result_ref, d_middle_ref = refs[19 + parts : 24 + parts]
    d_mixed_refs = refs[24 + parts : 24 + 2 * parts]
    (
        gw_ref, sums_ref,
        nb_wide, hidden, wide, d_wide, act_s, d_hid_s, ws, we, wo, gw_sum, grouped, branch_s, e_s, sums,
        weight_sem, act_sem, d_hid_sem,
    ) = refs[24 + 2 * parts :]
    step = pl.program_id(0)
    columns, features = nb_ref.shape[2:]
    sub = columns // COLUMN_PARTS
    weights = (
        pltpu.make_async_copy(ws_hbm, ws, weight_sem.at[0]),
        pltpu.make_async_copy(we_hbm, we, weight_sem.at[1]),
        pltpu.make_async_copy(wo_hbm, wo, weight_sem.at[2]),
    )

    def out_copies(n):
        at = pl.ds(pl.multiple_of(n * features, features), features)
        return (
            pltpu.make_async_copy(act_s.at[:, at], act_hbm.at[:, at], act_sem.at[n]),
            pltpu.make_async_copy(d_hid_s.at[:, at], d_hid_hbm.at[:, at], d_hid_sem.at[n]),
        )

    @pl.when(step == 0)
    def _():
        count, rows = nb_ref.shape[:2]
        own = rows * columns
        tall = (rows + 4) * columns
        for c in weights:
            c.start()
        for l in range(count):
            nb_wide[l * tall : l * tall + 2 * columns] = top_ref[l].reshape(2 * columns, features)
            nb_wide[l * tall + 2 * columns : (l + 1) * tall - 2 * columns] = nb_ref[l].reshape(
                own, features
            )
            nb_wide[(l + 1) * tall - 2 * columns : (l + 1) * tall] = bottom_ref[l].reshape(
                2 * columns, features
            )

    @pl.when(step < feeds)
    def _():
        feed_step(
            step, edge_ref, d_act_ref, we_ref, be_ref, taps_ref, bm_ref, small_ref,
            nb_wide, hidden, wide, d_wide, act_s, d_hid_s, nb_ref.shape,
        )
        for c in out_copies(step):
            c.start()

    @pl.when(step == feeds)
    def _():
        for c in weights:
            c.wait()

    @pl.when(step >= feeds)
    def _():
        turn_step(
            step, feeds, turns, middle_ref, attended_ref, g_ref, gate_b_ref, scale_ref, gate_a_ref,
            shrink_ref, mixed_refs, result_ref, d_middle_ref, d_mixed_refs, gw_ref, sums_ref,
            act_s, d_hid_s, ws, we, wo, gw_sum, grouped, branch_s, e_s, sums,
        )

    @pl.when(step == pl.num_programs(0) - 1)
    def _():
        for n in range(feeds):
            for c in out_copies(n):
                c.wait()


def feed_step(
    step, edge_ref, d_act_ref, we_ref, be_ref, taps_ref, bm_ref, small_ref,
    nb_wide, hidden, wide, d_wide, act_s, d_hid_s, shape,
):
    count, rows, columns, features = shape
    sub = columns // COLUMN_PARTS
    block = we_ref.shape[1]
    own = rows * columns
    tall = (rows + 4) * columns
    mid = (rows + 2) * columns
    hidden[...] = (dot(nb_wide[...], we_ref[...]) + be_ref[...]).astype(bfloat)
    small_ref[...] = jnp.zeros_like(small_ref)

    c0 = math.sqrt(2.0 / math.pi)
    c1 = c0 * 0.044715

    @pl.loop(0, count * (block // LANES))
    def _(index):
        l = index // (block // LANES)
        at = pl.ds(pl.multiple_of((index % (block // LANES)) * LANES, LANES), LANES)
        out = pl.ds(
            pl.multiple_of(step * block + index % (block // LANES) * LANES, LANES), LANES
        )
        taps = [taps_ref[t : t + 1, at] for t in range(9)]
        bias = bm_ref[:, at]
        for row in range(rows + 4):
            cells = hidden[pl.ds(pl.multiple_of(l * tall + row * columns, columns), columns), at]
            if row < 2:
                cells = cells * edge_ref[0].astype(bfloat)
            if row >= rows + 2:
                cells = cells * edge_ref[1].astype(bfloat)
            put_wide(wide, row, cells.reshape(COLUMN_PARTS, sub, LANES))
        taps = [(t + jnp.zeros((sub, LANES), single)).astype(bfloat) for t in taps]
        for row in range(rows + 2):
            v = conv_low(wide, row, taps).astype(single) + bias
            cube = (v * v) * c1
            half = 0.5 * jnp.tanh(v * (cube + c0)) + 0.5
            gelu = v * half
            slope = half + gelu * (1.0 - half) * (6.0 * cube + 2.0 * c0)
            if 1 <= row <= rows:
                act_s[
                    pl.ds(pl.multiple_of(l * own + (row - 1) * columns, columns), columns), out
                ] = gelu.reshape(columns, LANES).astype(bfloat)
            grad = d_act_ref[pl.ds(pl.multiple_of(l * mid + row * columns, columns), columns), at]
            grad = grad.astype(single).reshape(COLUMN_PARTS, sub, LANES) * slope
            put_wide(d_wide, row, grad.astype(bfloat))
        sums = [jnp.zeros((sub, LANES), single) for _ in range(11)]
        for row in range(rows):
            d_in = conv_back_row(d_wide, row, taps).astype(bfloat)
            d_hid_s[pl.ds(pl.multiple_of(l * own + row * columns, columns), columns), out] = (
                d_in.reshape(columns, LANES)
            )
            center = d_wide[row + 1, 1 : COLUMN_PARTS + 1]
            for i in range(3):
                for j in range(3):
                    term = center * wide[row + 1 + i, j : j + COLUMN_PARTS]
                    term = (term[0] + term[1]) + (term[2] + term[3])
                    sums[3 * i + j] += term.astype(single)
            sums[9] += jnp.sum(center.astype(single), axis=0)
            sums[10] += jnp.sum(d_in.astype(single), axis=0)
        for t in range(11):
            small_ref[t : t + 1, at] += jnp.sum(sums[t], axis=0, keepdims=True)


def turn_step(
    step, feeds, turns, middle_ref, attended_ref, g_ref, gate_b_ref, scale_ref, gate_a_ref,
    shrink_ref, mixed_refs, result_ref, d_middle_ref, d_mixed_refs, gw_ref, sums_ref,
    act_s, d_hid_s, ws, we, wo, gw_sum, grouped, branch_s, e_s, sums,
):
    columns, features = g_ref.shape[2:]
    sub = columns // COLUMN_PARTS
    rows = g_ref.shape[1]
    quarter = rows * columns // 4
    back = column_order(columns, True)
    gate_b = gate_b_ref[0]
    scale = 1.0 + scale_ref[0]
    gate_a = gate_a_ref[0]
    piece_of = step - feeds
    lines = pl.ds(pl.multiple_of(piece_of * rows * columns, rows * columns), rows * columns)

    branch_s[...] = dot(act_s[lines], ws[...]) + shrink_ref[...]
    e_s[...] = dot_nt(d_hid_s[lines], we[...])

    @pl.when(piece_of % turns == 0)
    def _():
        sums[...] = jnp.zeros_like(sums)

    for pair in range(rows // 2):
        for a in range(2):
            row = pair * 2 + a
            lows = []
            for j in range(COLUMN_PARTS):
                line = slice(j * sub, (j + 1) * sub)
                at = pl.ds(row * columns + j * sub, sub)
                branch = branch_s[at]
                middle = middle_ref[0, row, line]
                g = g_ref[0, row, line].astype(single)
                lows.append((middle + gate_b * branch).astype(bfloat))
                normed, inverse = norm_parts(middle)
                e = e_s[at]
                d_middle = g + norm_back(normed, inverse, e * scale)
                d_middle_ref[0, row, line] = d_middle
                low = (d_middle * gate_a).astype(bfloat)
                grouped[
                    2 * a + j % 2, pl.ds((pair * 2 + j // 2) * sub, sub)
                ] = low
                terms = (
                    g * branch, e, e * normed, d_middle * attended_ref[0, row, line], low.astype(single)
                )
                for t, term in enumerate(terms):
                    sums[t] += jnp.sum(term.reshape(sub // 8, 8, features), axis=0)
            result_ref[0, row] = dot(back, jnp.concatenate(lows, axis=0)).astype(bfloat)

    for t in range(5):
        sums_ref[0, t : t + 1] = jnp.sum(sums[t], axis=0, keepdims=True)
    sums_ref[0, 5:8] = jnp.zeros((3, features), single)
    grad = grouped[...].reshape(4 * quarter, features)
    at = 0
    for mixed_ref, d_ref in zip(mixed_refs, d_mixed_refs):
        width = mixed_ref.shape[-1]
        piece = slice(at, at + width)
        d_ref[0] = dot_nt(grad, wo[piece]).astype(bfloat).reshape(4, quarter, width)
        part = dot_tn(mixed_ref[0].reshape(4 * quarter, width), grad)

        @pl.when(piece_of == 0)
        def _():
            gw_sum[piece] = part

        @pl.when(piece_of > 0)
        def _():
            gw_sum[piece] += part

        at += width

    @pl.when(step == pl.num_programs(0) - 1)
    def _():
        gw_ref[...] = gw_sum[...].astype(bfloat)


def feed_turn(
    edge, nb, top, bottom, d_act, we, be, taps, bm, ws, middle, attended, g, gate_b, scale, gate_a,
    shrink_bias, wo, mixed,
):
    count, rows, columns, features = nb.shape
    hidden = we.shape[1]
    block = features
    feeds = hidden // block
    tokens = count * rows * columns
    tall = count * (rows + 4) * columns
    mid = count * (rows + 2) * columns
    sub = columns // COLUMN_PARTS
    some = min(TURN_ROWS, rows)
    turns = rows // some
    quarter = some * columns // 4
    whole = lambda a: pl.BlockSpec(a.shape, lambda s: (0,) * a.ndim)
    feed = lambda s: jnp.minimum(s, feeds - 1)
    place = lambda s: jnp.maximum(s - feeds, 0)
    column = lambda n: pl.BlockSpec((n, block), lambda s: (0, feed(s)))
    image = pl.BlockSpec(
        (1, some, columns, features), lambda s: (place(s) // turns, place(s) % turns, 0, 0)
    )
    vector = pl.BlockSpec((1, 1, features), lambda s: (place(s) // turns, 0, 0))
    groups = [
        pl.BlockSpec(
            (1, 4, quarter, m.shape[-1]), lambda s: (place(s) // turns, 0, place(s) % turns, 0)
        )
        for m in mixed
    ]
    hbm = pl.BlockSpec(memory_space=pl.ANY)
    return pl.pallas_call(
        partial(feed_turn_kernel, len(mixed), feeds, turns),
        grid=(feeds + count * turns,),
        in_specs=[
            pl.BlockSpec(memory_space=pltpu.SMEM),
            whole(nb), whole(top), whole(bottom),
            column(mid), column(features), column(1), column(16), column(1),
            image, image, image, vector, vector, vector, whole(shrink_bias), hbm, hbm, hbm,
        ]
        + groups,
        out_specs=[column(16), hbm, hbm, image, image]
        + groups
        + [
            pl.BlockSpec((features, features), lambda s: (0, 0)),
            pl.BlockSpec((1, 8, features), lambda s: (place(s) // turns, 0, 0)),
        ],
        out_shape=[
            jax.ShapeDtypeStruct((16, hidden), single),
            jax.ShapeDtypeStruct((tokens, hidden), bfloat),
            jax.ShapeDtypeStruct((tokens, hidden), bfloat),
            jax.ShapeDtypeStruct(g.shape, bfloat),
            jax.ShapeDtypeStruct(g.shape, single),
        ]
        + [jax.ShapeDtypeStruct(m.shape, bfloat) for m in mixed]
        + [
            jax.ShapeDtypeStruct((features, features), bfloat),
            jax.ShapeDtypeStruct((count, 8, features), single),
        ],
        scratch_shapes=[
            pltpu.VMEM((tall, features), bfloat),
            pltpu.VMEM((tall, block), bfloat),
            pltpu.VMEM((rows + 4, COLUMN_PARTS + 2, sub, LANES), bfloat),
            pltpu.VMEM((rows + 2, COLUMN_PARTS + 2, sub, LANES), bfloat),
            pltpu.VMEM((tokens, hidden), bfloat),
            pltpu.VMEM((tokens, hidden), bfloat),
            pltpu.VMEM((hidden, features), bfloat),
            pltpu.VMEM((features, hidden), bfloat),
            pltpu.VMEM((features, features), bfloat),
            pltpu.VMEM((features, features), single),
            pltpu.VMEM((4, quarter, features), bfloat),
            pltpu.VMEM((some * columns, features), single),
            pltpu.VMEM((some * columns, features), single),
            pltpu.VMEM((5, 8, features), single),
            pltpu.SemaphoreType.DMA((3,)),
            pltpu.SemaphoreType.DMA((feeds,)),
            pltpu.SemaphoreType.DMA((feeds,)),
        ],
        compiler_params=params(62),
        cost_estimate=cost(
            2 * features * hidden * (tall + 2 * tokens) + 4 * g.size * features,
            30 * g.size + 8 * features * hidden + 6 * tokens * hidden,
            mid * hidden,
        ),
        name="feed_turn",
    )(
        edge, nb, top, bottom, d_act, we, be, taps, bm, middle, attended, g, gate_b, scale, gate_a,
        shrink_bias, ws, we, wo, *mixed,
    )


def feed_grads_kernel(
    act_ref, d_hid_ref, nb_ref, db_ref, out_ref, db_own, shrink_s, expand_s, shrink_sem, expand_sem
):
    count, rows, columns, features = nb_ref.shape
    own = rows * columns
    step = pl.program_id(0)
    steps = pl.num_programs(0)
    some, slots, unit = shrink_s.shape[:3]

    @pl.when(step == 0)
    def _():
        for l in range(count):
            db_own[l * own : (l + 1) * own] = db_ref[l, 1 : rows + 1].reshape(own, features)

    def copies(s):
        return (
            pltpu.make_async_copy(
                shrink_s, out_ref.at[pl.ds(s * some, some), pl.ds(0, slots)], shrink_sem
            ),
            pltpu.make_async_copy(expand_s, out_ref.at[:, slots + s], expand_sem),
        )

    shrink = dot_tn(act_ref[...], db_own[...])
    expand = dot_tn(nb_ref[...].reshape(count * own, features), d_hid_ref[...])

    @pl.when(step > 0)
    def _():
        for c in copies(step - 1):
            c.wait()

    shrink_s[...] = shrink.reshape(shrink_s.shape).astype(bfloat)
    expand_s[...] = expand.reshape(expand_s.shape).astype(bfloat)
    for c in copies(step):
        c.start()

    @pl.when(step == steps - 1)
    def _():
        for c in copies(step):
            c.wait()


def feed_grads(act, d_hid, nb, db, devices):
    count, rows, columns, features = nb.shape
    tokens, hidden = act.shape
    block = features
    steps = hidden // block
    unit = features // devices
    if unit % 8:
        shrink = dot_tn(act, db[:, 1:-1].reshape(tokens, features))
        expand = dot_tn(nb.reshape(tokens, features), d_hid)
        return jnp.concatenate(
            [
                shrink.reshape(devices, steps, unit, features),
                expand.reshape(devices, unit, steps, features).transpose(0, 2, 1, 3),
            ],
            axis=1,
        ).astype(bfloat)
    whole = lambda a: pl.BlockSpec(a.shape, lambda s: (0,) * a.ndim)
    return pl.pallas_call(
        feed_grads_kernel,
        grid=(steps,),
        in_specs=[
            pl.BlockSpec((tokens, block), lambda s: (0, s)),
            pl.BlockSpec((tokens, block), lambda s: (0, s)),
            whole(nb), whole(db),
        ],
        out_specs=pl.BlockSpec(memory_space=pl.ANY),
        out_shape=jax.ShapeDtypeStruct((devices, 2 * steps, unit, features), bfloat),
        scratch_shapes=[
            pltpu.VMEM((tokens, features), bfloat),
            pltpu.VMEM((devices // steps, steps, unit, features), bfloat),
            pltpu.VMEM((devices, unit, features), bfloat),
            pltpu.SemaphoreType.DMA,
            pltpu.SemaphoreType.DMA,
        ],
        compiler_params=params(60),
        cost_estimate=cost(4 * features * hidden * tokens, 8 * features * hidden + 4 * tokens * hidden),
        name="feed_grads",
    )(act, d_hid, nb, db)


def final_kernel(
    d_ref, top_ref, bottom_ref, normed_ref, x_ref, d_middle_ref, scale_ref, taps_ref,
    out_ref, taps_out_ref, sums_ref, wide, d_wide,
):
    rows, columns, features = x_ref.shape[1:]
    sub = columns // COLUMN_PARTS
    back = column_order(columns, True)
    scale = 1.0 + scale_ref[0]

    def piece(ref, a, start):
        parts = [
            ref[0, 2 * a + j % 2, pl.ds(pl.multiple_of(start + (j // 2) * sub, sub), sub)]
            for j in range(COLUMN_PARTS)
        ]
        return jnp.stack(parts, axis=0).astype(single)

    def halo(ref):
        parts = [
            ref[0, j % 2, pl.ds((j // 2) * sub, sub)] for j in range(COLUMN_PARTS)
        ]
        return jnp.stack(parts, axis=0).astype(single)

    put_wide(d_wide, 0, halo(top_ref))
    put_wide(d_wide, rows + 1, halo(bottom_ref))

    @pl.loop(0, rows // 2)
    def _(pair):
        for a in range(2):
            put_wide(d_wide, pair * 2 + a + 1, piece(d_ref, a, pair * 2 * sub))

    @pl.loop(0, rows + 2)
    def _(row):
        for j in range(COLUMN_PARTS):
            put_part(wide, row, j, normed_ref[0, row, j * sub : (j + 1) * sub].astype(single))

    @pl.when(pl.program_id(0) == 0)
    def _():
        taps_out_ref[...] = jnp.zeros_like(taps_out_ref)

    d_normed = wide
    for lane in range(0, features, LANES):
        at = pl.ds(lane, LANES)
        taps = [taps_ref[t : t + 1, at] for t in range(9)]

        def step(row, sums):
            total = None
            center = d_wide[row + 1, 1 : COLUMN_PARTS + 1, :, at]
            sums = list(sums)
            for i in range(3):
                for j in range(3):
                    term = taps[3 * i + j] * d_wide[row + 2 - i, 2 - j : 2 - j + COLUMN_PARTS, :, at]
                    total = term if total is None else total + term
                    sums[3 * i + j] = sums[3 * i + j] + jnp.sum(
                        center * wide[row + i, j : j + COLUMN_PARTS, :, at], axis=0
                    )
            sums[9] = sums[9] + jnp.sum(center, axis=0)
            d_normed[row, 1 : COLUMN_PARTS + 1, :, at] = total
            return tuple(sums)

        sums = lax.fori_loop(
            0, rows, step, tuple(jnp.zeros((sub, LANES), single) for _ in range(10))
        )
        for t in range(10):
            taps_out_ref[t : t + 1, at] += jnp.sum(sums[t], axis=0, keepdims=True)

    def last(row, sums):
        lows = []
        for j in range(COLUMN_PARTS):
            line = slice(j * sub, (j + 1) * sub)
            cells = d_normed[row, j + 1]
            normed, inverse = norm_parts(x_ref[0, row, line].astype(single))
            grad = d_middle_ref[0, row, line] + norm_back(normed, inverse, cells * scale)
            lows.append(grad.astype(bfloat))
            sums = tuple(
                s + jnp.sum(t.reshape(sub // 8, 8, features), axis=0)
                for s, t in zip(sums, (cells, cells * normed))
            )
        out_ref[0, row] = dot(back, jnp.concatenate(lows, axis=0)).astype(bfloat)
        return sums

    sums = tuple(jnp.zeros((8, features), single) for _ in range(2))
    for row in range(rows):
        sums = last(row, sums)
    for t in range(2):
        sums_ref[0, t : t + 1] = jnp.sum(sums[t], axis=0, keepdims=True)
    sums_ref[0, 2:8] = jnp.zeros((6, features), single)


def final(d_reduced, top, bottom, normed, kept, d_middle, scale, taps):
    count, rows, columns, features = kept.shape
    quarter = rows * columns // 4
    sub = columns // COLUMN_PARTS
    image = lambda r: pl.BlockSpec((1, r, columns, features), lambda l: (l, 0, 0, 0))
    vector = pl.BlockSpec((1, 1, features), lambda l: (l, 0, 0))
    side = pl.BlockSpec((1, 2, 2 * sub, features), lambda l: (l, 0, 0, 0))
    return pl.pallas_call(
        final_kernel,
        grid=(count,),
        in_specs=[
            pl.BlockSpec((1, 4, quarter, features), lambda l: (l, 0, 0, 0)),
            side, side, image(rows + 2), image(rows), image(rows), vector,
            pl.BlockSpec((16, features), lambda l: (0, 0)),
        ],
        out_specs=[
            image(rows),
            pl.BlockSpec((16, features), lambda l: (0, 0)),
            pl.BlockSpec((1, 8, features), lambda l: (l, 0, 0)),
        ],
        out_shape=[
            jax.ShapeDtypeStruct(kept.shape, bfloat),
            jax.ShapeDtypeStruct((16, features), single),
            jax.ShapeDtypeStruct((count, 8, features), single),
        ],
        scratch_shapes=[pltpu.VMEM((rows + 2, COLUMN_PARTS + 2, sub, features), single)] * 2,
        compiler_params=params(60),
        cost_estimate=cost(kept.size * 180, kept.size * 12),
        name="final",
    )(d_reduced, top, bottom, normed, kept, d_middle, scale, taps)


def from_above(tail):
    count = lax.axis_size("strips")
    return lax.ppermute(tail, "strips", [(i, i + 1) for i in range(count - 1)])


def from_below(head):
    count = lax.axis_size("strips")
    return lax.ppermute(head, "strips", [(i + 1, i) for i in range(count - 1)])


def time_features(timesteps, halves):
    frequency = jnp.exp(-math.log(10000.0) * jnp.arange(halves, dtype=jnp.float32) / halves)
    phase = timesteps.astype(jnp.float32)[:, None] * frequency[None, :]
    return jnp.concatenate([jnp.cos(phase), jnp.sin(phase)], axis=1)


def thirds(value):
    high = value.astype(bfloat)
    rest = value - high.astype(single)
    middle = rest.astype(bfloat)
    low = (rest - middle.astype(single)).astype(bfloat)
    return jnp.concatenate([high, middle, low], axis=0)


def exact(value, weight, nt=False):
    n = value.shape[0]
    out = (dot_nt if nt else dot)(thirds(value), weight)
    return out[:n] + out[n : 2 * n] + out[2 * n :]


def silu(value):
    return value * (1.0 / (1.0 + jnp.exp(-value)))


def silu_slope(value):
    gate = 1.0 / (1.0 + jnp.exp(-value))
    return gate * (1.0 + value * (1.0 - gate))


def label_rows(labels, classes):
    return (lax.broadcasted_iota(jnp.int32, (labels.shape[0], classes), 1) == labels).astype(bfloat)


def condition(sinus, labels, wi_ref, bi_ref, wo_ref, bo_ref, table_ref):
    before = exact(sinus, wi_ref[...]) + bi_ref[...]
    inner = silu(before)
    onehot = label_rows(labels, table_ref.shape[1])
    cond = exact(inner, wo_ref[...]) + bo_ref[...] + dot_nt(onehot, table_ref[...])
    return before, inner, cond


def modulate_kernel(
    sinus_ref, label_ref, wi_ref, bi_ref, wo_ref, bo_ref, table_ref, ada_ref, ab_ref, out_ref, active
):
    @pl.when(pl.program_id(0) == 0)
    def _():
        cond = condition(
            sinus_ref[...], label_ref[...], wi_ref, bi_ref, wo_ref, bo_ref, table_ref
        )[2]
        active[...] = silu(cond)

    out_ref[0] = exact(active[...], ada_ref[...]) + ab_ref[...]


def modulate(sinus, labels, weights, ada, ada_bias):
    n = sinus.shape[0]
    features = ada.shape[0]
    whole = lambda a: pl.BlockSpec(a.shape, lambda s: (0,) * a.ndim)
    return pl.pallas_call(
        modulate_kernel,
        grid=(6,),
        in_specs=[whole(a) for a in (sinus, labels) + weights]
        + [
            pl.BlockSpec((features, features), lambda s: (0, s)),
            pl.BlockSpec((1, features), lambda s: (0, s)),
        ],
        out_specs=pl.BlockSpec((1, n, features), lambda s: (s, 0, 0)),
        out_shape=jax.ShapeDtypeStruct((6, n, features), single),
        scratch_shapes=[pltpu.VMEM((n, features), single)],
        compiler_params=params(16),
        cost_estimate=cost(50 * n * ada.size, 2 * ada.size),
        name="modulate",
    )(sinus, labels, *weights, ada, ada_bias)


def own_rows(me_ref, value, size):
    width = value.shape[1]
    place = lax.broadcasted_iota(jnp.int32, (size, width), 1)
    line = lax.broadcasted_iota(jnp.int32, (size, width), 0)
    pick = (place == me_ref[0] * size + line).astype(single)
    return lax.dot_general(
        pick, value, (((1,), (1,)), ((), ())), precision=highest, preferred_element_type=single
    )


def exact_small(a, b):
    return lax.dot_general(
        a, b, (((1,), (0,)), ((), ())), precision=highest, preferred_element_type=single
    )


def strip_sum(ref, kinds, count, features):
    lines = []
    for item in range(ref.shape[0]):
        for l in range(count):
            at = l * kinds * features
            lines.append(jnp.sum(
                    ref[item, :, at : at + kinds * features].astype(single), axis=0, keepdims=True
                ))
    return jnp.concatenate(lines, axis=0)


def early_kernel(
    count, me_ref, parts_ref, sinus_ref, label_ref, wi_ref, bi_ref, wo_ref, bo_ref, table_ref, ada_ref,
    before_ref, cond_ref, d_active_ref, ada_out_ref, d_mod_ref,
):
    features = ada_ref.shape[0]
    d_mod = strip_sum(parts_ref, 4, count, features)
    before, _, cond = condition(
        sinus_ref[...], label_ref[...], wi_ref, bi_ref, wo_ref, bo_ref, table_ref
    )
    before_ref[...] = before
    cond_ref[...] = cond
    d_active_ref[...] = exact(d_mod, ada_ref[:, 2 * features :], nt=True)
    size = ada_out_ref.shape[0]
    ada_out_ref[...] = exact_small(own_rows(me_ref, silu(cond), size), d_mod)
    d_mod_ref[...] = jnp.sum(d_mod, axis=0, keepdims=True)


def early_condition(me, parts, count, sinus, labels, weights, ada, size):
    n = sinus.shape[0]
    features = ada.shape[0]
    whole = lambda a: pl.BlockSpec(a.shape, lambda s: (0,) * a.ndim)
    shapes = [
        jax.ShapeDtypeStruct((n, features), single),
        jax.ShapeDtypeStruct((n, features), single),
        jax.ShapeDtypeStruct((n, features), single),
        jax.ShapeDtypeStruct((size, 4 * features), single),
        jax.ShapeDtypeStruct((1, 4 * features), single),
    ]
    return pl.pallas_call(
        partial(early_kernel, count),
        grid=(1,),
        in_specs=[pl.BlockSpec(memory_space=pltpu.SMEM)]
        + [whole(a) for a in (parts, sinus, labels) + weights + (ada,)],
        out_specs=[whole(a) for a in shapes],
        out_shape=shapes,
        compiler_params=params(28),
        cost_estimate=cost(50 * n * ada.size, 2 * ada.size),
        name="early_condition",
    )(me, parts, sinus, labels, *weights, ada)


def late_kernel(
    count, me_ref, parts_ref, before_ref, cond_ref, d_active_ref, ada_early_ref, d_mod_early_ref,
    sinus_ref, label_ref, wo_ref, ada_ref,
    ada_out_ref, d_mod_ref, table_out_ref, wo_out_ref, wi_out_ref, d_cond_ref, d_before_ref,
):
    features = wo_ref.shape[0]
    before = before_ref[...]
    cond = cond_ref[...]
    d_mod = strip_sum(parts_ref, 2, count, features)
    d_active = d_active_ref[...] + exact(d_mod, ada_ref[...], nt=True)
    d_cond = d_active * silu_slope(cond)
    d_before = exact(d_cond, wo_ref[...], nt=True) * silu_slope(before)
    size = ada_out_ref.shape[0]
    ada_out_ref[:, : 2 * features] = exact_small(own_rows(me_ref, silu(cond), size), d_mod)
    ada_out_ref[:, 2 * features :] = ada_early_ref[...]
    d_mod_ref[:, : 2 * features] = jnp.sum(d_mod, axis=0, keepdims=True)
    d_mod_ref[:, 2 * features :] = d_mod_early_ref[...]
    onehot = label_rows(label_ref[...], table_out_ref.shape[1]).astype(single)
    table_out_ref[...] = exact_small(own_rows(me_ref, d_cond, size), onehot)
    wo_out_ref[...] = exact_small(own_rows(me_ref, silu(before), size), d_cond)
    wi_out_ref[...] = exact_small(
        own_rows(me_ref, sinus_ref[...], wi_out_ref.shape[0]), d_before
    )
    d_cond_ref[...] = jnp.sum(d_cond, axis=0, keepdims=True)
    d_before_ref[...] = jnp.sum(d_before, axis=0, keepdims=True)


def late_condition(
    me, parts, count, before, cond, d_active, ada_early, d_mod_early, sinus, labels, wo, ada, classes,
    devices,
):
    features = ada.shape[0]
    size = features // devices
    whole = lambda a: pl.BlockSpec(a.shape, lambda s: (0,) * a.ndim)
    shapes = [
        jax.ShapeDtypeStruct((size, 6 * features), single),
        jax.ShapeDtypeStruct((1, 6 * features), single),
        jax.ShapeDtypeStruct((size, classes), single),
        jax.ShapeDtypeStruct((size, features), single),
        jax.ShapeDtypeStruct((sinus.shape[1] // devices, features), single),
        jax.ShapeDtypeStruct((1, features), single),
        jax.ShapeDtypeStruct((1, features), single),
    ]
    return pl.pallas_call(
        partial(late_kernel, count),
        grid=(1,),
        in_specs=[pl.BlockSpec(memory_space=pltpu.SMEM)]
        + [
            whole(a)
            for a in (parts, before, cond, d_active, ada_early, d_mod_early, sinus, labels, wo)
        ]
        + [pl.BlockSpec((features, 2 * features), lambda s: (0, 0))],
        out_specs=[whole(a) for a in shapes],
        out_shape=shapes,
        compiler_params=params(16),
        cost_estimate=cost(20 * ada.size, ada.size),
        name="late_condition",
    )(me, parts, before, cond, d_active, ada_early, d_mod_early, sinus, labels, wo, ada)


def sum_cores(keep, give):
    strips = lax.axis_size("strips")
    got = lax.ppermute(give, "strips", [(i, i ^ 1) for i in range(strips)])
    return (keep.astype(single) + got.astype(single)).astype(bfloat)


def sum_axis(part, axis, size, place, step):
    pick = lambda k: lax.dynamic_index_in_dim(part, place ^ k, 0, keepdims=False)
    count = lax.axis_size(axis)
    got = [
        lax.ppermute(pick(k), axis, [(i, i ^ (k * step)) for i in range(count)])
        for k in range(1, size)
    ]
    total = pick(0).astype(single)
    for g in got:
        total = total + g.astype(single)
    return total


def sum_items(part):
    return sum_axis(part, "items", lax.axis_size("items"), lax.axis_index("items"), 1).astype(bfloat)


def sum_strips(part):
    strip = lax.axis_index("strips")
    return sum_axis(part, "strips", lax.axis_size("strips") // 2, strip // 2, 2)


def after(value, *others):
    return lax.optimization_barrier((value,) + others)[0]


def tap_rows(kernel):
    return jnp.pad(kernel.astype(single).T, ((0, 7), (0, 0)))


def per_device(
    latents,
    timesteps,
    labels,
    time_in_weight,
    time_in_bias,
    time_out_weight,
    time_out_bias,
    label_table,
    ada_weight,
    ada_bias,
    down_kernel,
    down_bias,
    input_weight,
    query_bias,
    value_bias,
    output_weight,
    output_bias,
    expand_weight,
    expand_bias,
    mixer_kernel,
    mixer_bias,
    shrink_weight,
    shrink_bias,
    cotangent,
):
    count, rows, columns, features = latents.shape
    strips = lax.axis_size("strips")
    items = lax.axis_size("items")
    devices = strips * items
    strip = lax.axis_index("strips")
    item = lax.axis_index("items")
    me = item * strips + strip
    sub = columns // COLUMN_PARTS
    quarter = rows * columns // 4
    groups = count * 4
    share = strips // groups
    width = features // share
    row_vector = lambda v: v.astype(single).reshape(1, -1)
    edge = jnp.stack([strip > 0, strip < strips - 1]).astype(single)

    lines = -(-count // 8) * 8
    weights = (
        time_in_weight, row_vector(time_in_bias), time_out_weight, row_vector(time_out_bias),
        label_table,
    )
    waves = time_in_weight.shape[0] // 2
    modulation = modulate(
        time_features(jnp.pad(timesteps, (0, lines - count)), waves),
        jnp.pad(labels, (0, lines - count))[:, None],
        weights,
        ada_weight,
        row_vector(ada_bias),
    )
    shift_a, scale_a, gate_a, shift_b, scale_b, gate_b = (
        modulation[i, :count, None, :] for i in range(6)
    )

    ends = jnp.concatenate([latents[:, -1:], cotangent[:, -1:]], axis=1)
    starts = jnp.concatenate([latents[:, :1], cotangent[:, :1]], axis=1)
    above = from_above(ends)
    below = from_below(starts)

    down_taps = tap_rows(down_kernel)
    grouped, normed_a, kept = front(
        edge, latents, above[:, :1], below[:, :1], scale_a, shift_a, down_taps, row_vector(down_bias)
    )

    def spread(array):
        flat = array.reshape(groups, quarter, array.shape[-1])
        if share > 1:
            flat = jnp.repeat(flat, share, axis=0)
        got = lax.all_to_all(flat, "strips", 0, 0, tiled=True)
        return got.reshape(strips * quarter, array.shape[-1])

    def collect(array):
        flat = array.reshape(strips, quarter, array.shape[-1])
        return lax.all_to_all(flat, "strips", 0, 0, tiled=True)

    group = spread(grouped)
    g_kept, d_branch, grad_shrink_bias = upstream_parts(
        cotangent, above[:, 1:], below[:, 1:], gate_b
    )

    head_at = (strip % share) * width
    def own_columns(array, axis):
        return array if share == 1 else lax.dynamic_slice_in_dim(array, head_at, width, axis=axis)

    own_weight = jnp.concatenate(
        [own_columns(input_weight[:, i * features : (i + 1) * features], 1) for i in range(3)], axis=1
    ) if share > 1 else input_weight
    own_bias = jnp.concatenate(
        [own_columns(row_vector(b), 1) for b in (query_bias, value_bias)], axis=1
    )
    piece = width // CHUNKS
    saved = []
    mixed = []
    d_act = feed_upstream(d_branch, shrink_weight)
    group, d_act, expand_line, mixer_taps, mixer_line, output_line, shrink_line = (
        lax.optimization_barrier(
            (
                group,
                d_act,
                row_vector(expand_bias),
                tap_rows(mixer_kernel),
                row_vector(mixer_bias),
                row_vector(output_bias),
                row_vector(shrink_bias),
            )
        )
    )
    for c in range(CHUNKS):
        saved.append(attend(group, own_weight, own_bias, c * piece, piece))
        mixed.append(collect(saved[c][3]))
    if share == 1:
        mixed = [m.reshape(count, 4, quarter, piece) for m in mixed]
    else:
        joined = jnp.concatenate(mixed, axis=-1).reshape(groups, share, quarter, width)
        joined = joined.transpose(0, 2, 1, 3).reshape(count, 4, quarter, features)
        mixed = [joined]

    attended, middle, normed_b, first_rows, last_rows = middle_part(
        mixed, output_weight, output_line, kept, gate_a, scale_b, shift_b
    )
    feed_small, act, d_hid, *turned = feed_turn(
        edge,
        normed_b,
        from_above(last_rows),
        from_below(first_rows),
        d_act,
        expand_weight,
        expand_line,
        mixer_taps,
        mixer_line,
        shrink_weight,
        middle,
        attended,
        g_kept,
        gate_b,
        scale_b,
        gate_a,
        shrink_line,
        output_weight,
        mixed,
    )
    result, d_middle = turned[:2]
    d_mixed = turned[2:-2]
    grad_output, turn_sums = turned[-2:]

    hidden = expand_weight.shape[1]
    steps = hidden // features
    early = feed_grads(act, d_hid, normed_b, d_branch, devices)
    early_sum = lax.psum_scatter(early, both, scatter_dimension=0, tiled=False).astype(single)

    if share == 1:
        d_mixed = [spread(d) for d in d_mixed]
    else:
        parts = d_mixed[0].reshape(groups, quarter, share, width).transpose(0, 2, 1, 3)
        got = lax.all_to_all(parts.reshape(strips, quarter, width), "strips", 0, 0, tiled=True)
        got = got.reshape(strips * quarter, width)
        d_mixed = [got[:, c * piece : (c + 1) * piece] for c in range(CHUNKS)]
    grads = []
    for c in range(CHUNKS):
        if c == 0:
            d_mixed[c], _ = lax.optimization_barrier((d_mixed[c], early))
        q, k, v, out, logs = saved[c]
        grads.append(attend_back(q, k, v, out, d_mixed[c], logs))
    size = features // devices
    narrow = jnp.stack([jnp.sum(turn_sums[:, 4], axis=0), jnp.sum(grad_shrink_bias[:, 0], axis=0)])
    to_all = jnp.concatenate(
        [
            turn_sums[:, 3], turn_sums[:, 1], turn_sums[:, 2], turn_sums[:, 0],
        ],
        axis=1,
    ).reshape(-1)
    whole_numbers = jnp.concatenate([timesteps // 32, timesteps % 32, labels // 32, labels % 32])
    to_all = jnp.concatenate([to_all, whole_numbers.astype(single)])
    fill = -(to_all.shape[0] + 11 * (hidden // devices) + 2 * size) % LANES
    early_small = jnp.concatenate(
        [
            jnp.broadcast_to(to_all, (devices, to_all.shape[0])),
            feed_small[:11].reshape(11, devices, -1).transpose(1, 0, 2).reshape(devices, -1),
            narrow.reshape(2, devices, -1).transpose(1, 0, 2).reshape(devices, -1),
            jnp.zeros((devices, fill), single),
        ],
        axis=1,
    ).astype(bfloat)
    early_small = after(early_small, grads[0][0], *d_mixed)
    early_got = lax.all_to_all(early_small, both, 0, 0, tiled=True)

    parts = [g for chunk in grads for g in chunk]
    d_group = regroup(parts, own_weight)
    d_reduced = collect(d_group)
    if share > 1:
        d_reduced = jnp.sum(
            d_reduced.reshape(groups, share, quarter, features).astype(single), axis=1
        ).astype(bfloat)
    d_reduced = d_reduced.reshape(count, 4, quarter, features)
    late, d_sums = input_grad(after(group, d_group), grad_output, parts)
    d_query_sum = d_sums[0, :width]
    d_value_sum = d_sums[0, width:]
    if share > 1:
        zero = jnp.zeros((features, 3, features), bfloat)
        grad_input = lax.dynamic_update_slice(
            zero, late[:, : 3 * width].reshape(features, 3, width), (0, 0, head_at)
        ).reshape(features, 3 * features)
        late = jnp.concatenate([grad_input, grad_output], axis=1)
        flat = jnp.zeros((features,), single)
        d_query_sum = lax.dynamic_update_slice(flat, d_query_sum, (head_at,))
        d_value_sum = lax.dynamic_update_slice(flat, d_value_sum, (head_at,))
    late = late.reshape(items, strips // 2, 2, size, 4 * features)
    core = strip % 2
    keep = lax.dynamic_index_in_dim(late, core, 2, keepdims=False)
    give = lax.dynamic_index_in_dim(late, 1 - core, 2, keepdims=False)

    per_latent = count * 4 * features
    parts_early = early_got[:, :per_latent].reshape(items, strips, per_latent)
    first = early_got.reshape(items, strips, -1)[:, 0, per_latent : per_latent + 4 * count]
    first = first.astype(single).reshape(items, 4, count)
    all_times = (first[:, 0] * 32.0 + first[:, 1]).reshape(-1)
    all_labels = (first[:, 2] * 32.0 + first[:, 3]).reshape(-1, 1).astype(jnp.int32)
    sinus = time_features(all_times, waves)
    early_sums = jnp.sum(early_got[:, per_latent + 4 * count :].astype(single), axis=0)
    cut = 11 * (hidden // devices)
    feed_sum = early_sums[:cut].reshape(11, -1)
    narrow_sum = early_sums[cut : cut + 2 * size].reshape(2, size)
    index = jnp.reshape(me, (1,)).astype(jnp.int32)
    before, cond, d_active, grad_ada_early, d_mod_early = early_condition(
        index, parts_early, count, sinus, all_labels, weights, ada_weight, size
    )

    d_reduced, before, keep, give = lax.optimization_barrier((d_reduced, before, keep, give))
    late_part = sum_items(sum_cores(keep, give))
    grad_latents, down_small, final_sums = final(
        d_reduced,
        from_above(d_reduced[:, 2:, -2 * sub :]),
        from_below(d_reduced[:, :2, : 2 * sub]),
        normed_a,
        kept,
        d_middle,
        scale_a,
        down_taps,
    )

    late_narrow = jnp.concatenate([d_query_sum[None], d_value_sum[None], down_small[:10]], axis=0)
    to_all = final_sums[:, :2].reshape(-1)
    fill = -(to_all.shape[0] + 12 * size) % LANES
    late_small = jnp.concatenate(
        [
            jnp.broadcast_to(to_all, (devices, to_all.shape[0])),
            late_narrow.reshape(12, devices, size).transpose(1, 0, 2).reshape(devices, -1),
            jnp.zeros((devices, fill), single),
        ],
        axis=1,
    ).astype(bfloat)
    late_got = lax.all_to_all(late_small, both, 0, 0, tiled=True)
    late_got, late_part = lax.optimization_barrier((late_got, late_part))
    late_sum = sum_strips(late_part)
    late_sums = jnp.sum(late_got[:, to_all.shape[0] :].astype(single), axis=0)[: 12 * size].reshape(12, size)
    (
        grad_ada, d_mod, grad_table, grad_time_out, grad_time_in, d_cond, d_before,
    ) = late_condition(
        index,
        late_got[:, : to_all.shape[0]].reshape(items, strips, -1),
        count,
        before,
        cond,
        d_active,
        grad_ada_early,
        d_mod_early,
        sinus,
        all_labels,
        time_out_weight,
        ada_weight,
        label_table.shape[1],
        devices,
    )

    def mine(array):
        part = array.shape[-1] // devices
        return lax.dynamic_slice_in_dim(array[0], me * part, part, axis=0)

    return (
        result,
        grad_latents,
        grad_time_in,
        mine(d_before),
        grad_time_out,
        mine(d_cond),
        grad_table,
        grad_ada,
        mine(d_mod),
        late_sums[2:11].T,
        late_sums[11],
        late_sum[:, : 3 * features],
        late_sums[0],
        late_sums[1],
        late_sum[:, 3 * features :],
        narrow_sum[0],
        early_sum[steps:].transpose(1, 0, 2).reshape(size, hidden),
        feed_sum[10],
        feed_sum[:9].T,
        feed_sum[9],
        early_sum[:steps].reshape(hidden // devices, features),
        narrow_sum[1],
    )


def solution(mesh):
    image = P("items", "strips", None, None)
    split = P(both, None)
    line = P(both)
    return jax.shard_map(
        per_device,
        mesh=mesh,
        in_specs=(image, P("items"), P("items")) + (P(),) * 20 + (image,),
        out_specs=(
            image, image, split, line, split, line, split, split, line, split, line,
            split, line, line, split, line, split, line, split, line, split, line,
        ),
        check_vma=False,
    )
```

```python
from functools import partial
import math

import jax
import jax.numpy as jnp
from jax import lax
from jax.experimental import pallas as pl
from jax.experimental.pallas import tpu as pltpu
from jax.sharding import PartitionSpec as P

HEADS = 12
HEAD_DIM = 64
LANES = 128
COLUMN_PARTS = 4
CHUNKS = (2, 3, 1)

highest = lax.Precision.HIGHEST
epsilon = 1e-06
bfloat = jnp.bfloat16
single = jnp.float32
both = ("items", "strips")


def params(mebibytes):
    return pltpu.CompilerParams(vmem_limit_bytes=mebibytes * 1024 * 1024)


def cost(flops, moved, exps=0):
    return pl.CostEstimate(flops=int(flops), bytes_accessed=int(moved), transcendentals=int(exps))


def dot(a, b):
    return lax.dot_general(a, b, (((1,), (0,)), ((), ())), preferred_element_type=single)


def dot_nt(a, b):
    return lax.dot_general(a, b, (((1,), (1,)), ((), ())), preferred_element_type=single)


def dot_tn(a, b):
    return lax.dot_general(a, b, (((0,), (0,)), ((), ())), preferred_element_type=single)


def column_order(columns, back):
    sub = columns // COLUMN_PARTS
    first = lax.broadcasted_iota(jnp.int32, (columns, columns), 0)
    second = lax.broadcasted_iota(jnp.int32, (columns, columns), 1)
    kept, column = (second, first) if back else (first, second)
    return (column == COLUMN_PARTS * (kept % sub) + kept // sub).astype(bfloat)


def norm_parts(value):
    center = value - jnp.mean(value, axis=-1, keepdims=True)
    inverse = lax.rsqrt(jnp.mean(center * center, axis=-1, keepdims=True) + epsilon)
    return center * inverse, inverse


def norm_back(normed, inverse, grad):
    return inverse * (
        grad
        - jnp.mean(grad, axis=-1, keepdims=True)
        - normed * jnp.mean(grad * normed, axis=-1, keepdims=True)
    )


def put_wide(ref, row, cells):
    sub = cells.shape[1]
    place = lax.broadcasted_iota(jnp.int32, cells.shape[1:], 0)
    last = cells[COLUMN_PARTS - 1].astype(single)
    first = cells[0].astype(single)
    ref[row, 1 : COLUMN_PARTS + 1] = cells
    ref[row, 0] = jnp.where(place == 0, 0.0, pltpu.roll(last, 1, 0)).astype(ref.dtype)
    ref[row, COLUMN_PARTS + 1] = jnp.where(
        place == sub - 1, 0.0, pltpu.roll(first, sub - 1, 0)
    ).astype(ref.dtype)


def put_part(ref, row, j, cells):
    sub = cells.shape[0]
    place = lax.broadcasted_iota(jnp.int32, cells.shape, 0)
    ref[row, j + 1] = cells
    if j == COLUMN_PARTS - 1:
        ref[row, 0] = jnp.where(place == 0, 0.0, pltpu.roll(cells, 1, 0))
    if j == 0:
        ref[row, COLUMN_PARTS + 1] = jnp.where(place == sub - 1, 0.0, pltpu.roll(cells, sub - 1, 0))


def conv_low(ref, row, taps):
    total = None
    for i in range(3):
        line = [taps[3 * i + j] * ref[row + i, j : j + COLUMN_PARTS] for j in range(3)]
        line = (line[0] + line[1]) + line[2]
        total = line if total is None else total + line
    return total


def conv_back_row(ref, row, taps):
    total = None
    for i in range(3):
        line = [
            taps[3 * i + j] * ref[row + 2 - i, 2 - j : 2 - j + COLUMN_PARTS] for j in range(3)
        ]
        line = (line[0] + line[1]) + line[2]
        total = line if total is None else total + line
    return total


def front_kernel(
    edge_ref, x_ref, top_ref, bottom_ref, scale_ref, shift_ref, taps_ref, bias_ref,
    grouped_ref, normed_ref, kept_ref, wide,
):
    rows, columns, features = x_ref.shape[1:]
    sub = columns // COLUMN_PARTS
    order = column_order(columns, False)
    scale = 1.0 + scale_ref[0]
    shift = shift_ref[0]

    def fill(row, raw, keep, kept_row=None):
        cells = dot(order, raw)
        if kept_row is not None:
            kept_ref[0, kept_row] = cells.astype(bfloat)
        for j in range(COLUMN_PARTS):
            line = slice(j * sub, (j + 1) * sub)
            normed = norm_parts(cells[line])[0] * scale + shift
            low = (normed if keep is None else normed * keep).astype(bfloat)
            normed_ref[0, row, line] = low
            put_part(wide, row, j, low.astype(single))

    fill(0, top_ref[0, 0], edge_ref[0])
    fill(rows + 1, bottom_ref[0, 0], edge_ref[1])

    for row in range(rows):
        fill(row + 1, x_ref[0, row], None, row)

    taps = [taps_ref[t : t + 1] for t in range(9)]
    bias = bias_ref[...]

    @pl.loop(0, rows // 2)
    def _(pair):
        for a in range(2):
            for lane in range(0, features, LANES):
                at = pl.ds(lane, LANES)
                total = jnp.zeros((COLUMN_PARTS, sub, LANES), single) + bias[:, lane : lane + LANES]
                for i in range(3):
                    for j in range(3):
                        total = total + taps[3 * i + j][:, lane : lane + LANES] * wide[
                            pair * 2 + a + i, j : j + COLUMN_PARTS, :, at
                        ]
                low = total.astype(bfloat)
                for j in range(COLUMN_PARTS):
                    grouped_ref[
                        0, 2 * a + j % 2, pl.ds(pl.multiple_of((pair * 2 + j // 2) * sub, sub), sub), at
                    ] = low[j]


def front(edge, latents, top, bottom, scale, shift, taps, bias):
    count, rows, columns, features = latents.shape
    quarter = rows * columns // 4
    sub = columns // COLUMN_PARTS
    image = lambda r: pl.BlockSpec((1, r, columns, features), lambda l: (l, 0, 0, 0))
    vector = pl.BlockSpec((1, 1, features), lambda l: (l, 0, 0))
    return pl.pallas_call(
        front_kernel,
        grid=(count,),
        in_specs=[
            pl.BlockSpec(memory_space=pltpu.SMEM),
            image(rows), image(1), image(1), vector, vector,
            pl.BlockSpec((16, features), lambda l: (0, 0)),
            pl.BlockSpec((1, features), lambda l: (0, 0)),
        ],
        out_specs=[
            pl.BlockSpec((1, 4, quarter, features), lambda l: (l, 0, 0, 0)),
            image(rows + 2), image(rows),
        ],
        out_shape=[
            jax.ShapeDtypeStruct((count, 4, quarter, features), bfloat),
            jax.ShapeDtypeStruct((count, rows + 2, columns, features), bfloat),
            jax.ShapeDtypeStruct((count, rows, columns, features), bfloat),
        ],
        scratch_shapes=[pltpu.VMEM((rows + 2, COLUMN_PARTS + 2, sub, features), single)],
        compiler_params=params(18),
        cost_estimate=cost(count * rows * columns * features * 150, count * rows * columns * features * 8),
        name="front",
    )(edge, latents, top, bottom, scale, shift, taps, bias)


def upstream_kernel(g_ref, top_ref, bottom_ref, gate_ref, kept_ref, branch_ref, bias_ref):
    rows, columns, features = g_ref.shape[1:]
    order = column_order(columns, False)
    gate = gate_ref[0]

    def low(raw):
        cells = dot(order, raw)
        return cells, (cells * gate).astype(bfloat)

    branch_ref[0, 0] = low(top_ref[0, 0])[1]
    branch_ref[0, rows + 1] = low(bottom_ref[0, 0])[1]

    def step(row, total):
        cells, grad = low(g_ref[0, row])
        kept_ref[0, row] = cells.astype(bfloat)
        branch_ref[0, row + 1] = grad
        return total + jnp.sum(grad.astype(single), axis=0, keepdims=True)

    total = jnp.zeros((1, features), single)
    for row in range(rows):
        total = step(row, total)
    bias_ref[0] = total


def upstream_parts(cotangent, top, bottom, gate):
    count, rows, columns, features = cotangent.shape
    image = lambda r: pl.BlockSpec((1, r, columns, features), lambda l: (l, 0, 0, 0))
    vector = pl.BlockSpec((1, 1, features), lambda l: (l, 0, 0))
    return pl.pallas_call(
        upstream_kernel,
        grid=(count,),
        in_specs=[image(rows), image(1), image(1), vector],
        out_specs=[image(rows), image(rows + 2), vector],
        out_shape=[
            jax.ShapeDtypeStruct((count, rows, columns, features), bfloat),
            jax.ShapeDtypeStruct((count, rows + 2, columns, features), bfloat),
            jax.ShapeDtypeStruct((count, 1, features), single),
        ],
        compiler_params=params(14),
        cost_estimate=cost(count * rows * columns * features * 130, count * rows * columns * features * 6),
        name="upstream",
    )(cotangent, top, bottom, gate)


QUERY_STEP = 1024
QUERY_STEP_BACK = 256


def attend_kernel(
    x_ref, wq_ref, wk_ref, wv_ref, bq_ref, bv_ref, q_ref, k_ref, v_ref, mixed_ref, log_ref
):
    tokens = x_ref.shape[0]
    base = math.log2(math.e) / math.sqrt(HEAD_DIM)

    @pl.when(pl.program_id(0) == 0)
    def _():
        x = x_ref[...]
        q_ref[...] = (dot(x, wq_ref[...]) + bq_ref[...]).astype(bfloat)
        k_ref[...] = dot(x, wk_ref[...]).astype(bfloat)
        v_ref[...] = (dot(x, wv_ref[...]) + bv_ref[...]).astype(bfloat)

    pair = pl.ds(pl.multiple_of(pl.program_id(0) * LANES, LANES), LANES)
    keys = k_ref[:, pair]
    values = v_ref[:, pair].T
    lane = lax.broadcasted_iota(jnp.int32, (QUERY_STEP, LANES), 1)
    for at in range(0, tokens, QUERY_STEP):
        part = q_ref[at : at + QUERY_STEP, pair]
        outs = []
        for head in range(LANES // HEAD_DIM):
            own = jnp.where(lane // HEAD_DIM == head, part, jnp.zeros_like(part))
            scores = dot_nt(keys, own)
            peak = jnp.max(scores, axis=0, keepdims=True) * base
            soft = jnp.exp2(scores * base - peak)
            total = jnp.sum(soft, axis=0, keepdims=True)
            log_ref[0, head : head + 1, at : at + QUERY_STEP] = peak + jnp.log2(total)
            out = dot(values[head * HEAD_DIM : (head + 1) * HEAD_DIM], soft.astype(bfloat))
            outs.append(out * (1.0 / total))
        mixed_ref[at : at + QUERY_STEP] = jnp.concatenate(outs, axis=0).T.astype(bfloat)


def attend(x, weights, biases, first, width):
    tokens, features = x.shape
    pairs = width // LANES
    start = first // width
    stride = weights.shape[1] // 3 // width
    weight = lambda i: pl.BlockSpec((features, width), lambda h: (0, i * stride + start))
    bias = lambda i: pl.BlockSpec((1, width), lambda h: (0, i * stride + start))
    full = pl.BlockSpec((tokens, width), lambda h: (0, 0))
    column = pl.BlockSpec((tokens, LANES), lambda h: (0, h))
    lows = jax.ShapeDtypeStruct((tokens, width), bfloat)
    return pl.pallas_call(
        attend_kernel,
        grid=(pairs,),
        in_specs=[pl.BlockSpec((tokens, features), lambda h: (0, 0))]
        + [weight(0), weight(1), weight(2), bias(0), bias(1)],
        out_specs=[full] * 3 + [column] + [pl.BlockSpec((1, 2, tokens), lambda h: (h, 0, 0))],
        out_shape=[lows] * 4 + [jax.ShapeDtypeStruct((pairs, 2, tokens), single)],
        compiler_params=params(60),
        cost_estimate=cost(
            6 * tokens * features * width + 16 * tokens * tokens * width,
            2 * tokens * features + 8 * tokens * width + 6 * features * width,
            2 * pairs * tokens * tokens,
        ),
        name="attend",
    )(x, weights, weights, weights, biases, biases)


def attend_back_kernel(others, *refs):
    q_ref, k_ref, v_ref, mixed_ref, grad_ref, log_ref = refs[:6]
    if others is None:
        dq_ref, dk_ref, dv_ref, dk_sum, dv_sum = refs[6:]
    else:
        sources = refs[6 : 7 + others]
        dq_ref, dk_ref, dv_ref, out_ref, dk_sum, dv_sum, own_grads = refs[7 + others : 14 + others]
        held = refs[14 + others : 15 + 2 * others]
        sems = refs[15 + 2 * others]
        copies = [
            pltpu.make_async_copy(source, kept, sems.at[n])
            for n, (source, kept) in enumerate(zip(sources, held))
        ]

        @pl.when(pl.program_id(0) == 0)
        def _():
            for c in copies:
                c.start()

    tokens = q_ref.shape[0]
    scale = 1.0 / math.sqrt(HEAD_DIM)
    base = math.log2(math.e) * scale
    keys = k_ref[...]
    values = v_ref[...]
    keys_turned = keys.T
    lane = lax.broadcasted_iota(jnp.int32, (QUERY_STEP_BACK, LANES), 1)
    for at in range(0, tokens, QUERY_STEP_BACK):
        rows = slice(at, at + QUERY_STEP_BACK)
        part = q_ref[rows]
        grad = grad_ref[rows]
        shares = (grad.astype(single) * mixed_ref[rows].astype(single)).T
        outs = []
        for head in range(LANES // HEAD_DIM):
            mine = lane // HEAD_DIM == head
            own = jnp.where(mine, part, jnp.zeros_like(part))
            own_grad = jnp.where(mine, grad, jnp.zeros_like(grad))
            share = jnp.sum(
                shares[head * HEAD_DIM : (head + 1) * HEAD_DIM], axis=0, keepdims=True
            )
            soft = jnp.exp2(dot_nt(keys, own) * base - log_ref[0, head : head + 1, rows])
            d_scores = (soft * (dot_nt(values, own_grad) - share)).astype(bfloat)
            dv_part = dot(soft.astype(bfloat), own_grad)
            dk_part = dot(d_scores, own)
            if at == 0 and head == 0:
                dv_sum[...] = dv_part
                dk_sum[...] = dk_part
            else:
                dv_sum[...] += dv_part
                dk_sum[...] += dk_part
            outs.append(dot(keys_turned[head * HEAD_DIM : (head + 1) * HEAD_DIM], d_scores))
        dq_ref[rows] = (jnp.concatenate(outs, axis=0) * scale).T.astype(bfloat)
    dk_ref[...] = (dk_sum[...] * scale).astype(bfloat)
    dv_ref[...] = dv_sum[...].astype(bfloat)
    if others is None:
        return
    pair = pl.ds(pl.multiple_of(pl.program_id(0) * LANES, LANES), LANES)
    for i, ref in enumerate((dq_ref, dk_ref, dv_ref)):
        own_grads[i, :, pair] = ref[...]

    @pl.when(pl.program_id(0) == pl.num_programs(0) - 1)
    def _():
        for c in copies:
            c.wait()
        weight = held[0]
        third = weight.shape[1] // 3
        piece = own_grads.shape[2]
        total = None
        for i in range(3):
            parts = [held[1 + 3 * c + i][...] for c in range(others // 3)] + [own_grads[i]]
            for c, part in enumerate(parts):
                at = i * third + c * piece
                term = dot_nt(part, weight[:, at : at + piece])
                total = term if total is None else total + term
        out_ref[...] = total.astype(bfloat)


def attend_back(q, k, v, mixed, grad, logs, weight=None, earlier=()):
    tokens, width = q.shape
    pairs = width // LANES
    column = pl.BlockSpec((tokens, LANES), lambda h: (0, h))
    lows = jax.ShapeDtypeStruct((tokens, width), bfloat)
    sums = [pltpu.VMEM((tokens, LANES), single)] * 2
    sources, outs, shapes, scratch = (), [], [], []
    if weight is not None:
        sources = (weight,) + tuple(earlier)
        outs = [pl.BlockSpec((tokens, weight.shape[0]), lambda h: (0, 0))]
        shapes = [jax.ShapeDtypeStruct((tokens, weight.shape[0]), bfloat)]
        scratch = (
            [pltpu.VMEM((3, tokens, width), bfloat)]
            + [pltpu.VMEM(a.shape, bfloat) for a in sources]
            + [pltpu.SemaphoreType.DMA((len(sources),))]
        )
    return pl.pallas_call(
        partial(attend_back_kernel, None if weight is None else len(earlier)),
        grid=(pairs,),
        in_specs=[column] * 5
        + [pl.BlockSpec((1, 2, tokens), lambda h: (h, 0, 0))]
        + [pl.BlockSpec(memory_space=pl.ANY)] * len(sources),
        out_specs=[column] * 3 + outs,
        out_shape=[lows] * 3 + shapes,
        scratch_shapes=sums + scratch,
        compiler_params=params(60),
        cost_estimate=cost(
            40 * tokens * tokens * width, 16 * tokens * width, 2 * pairs * tokens * tokens
        ),
        name="attend_back",
    )(q, k, v, mixed, grad, logs, *sources)


def input_grad_kernel(*refs):
    x_ref, other_ref = refs[0], refs[1]
    parts = refs[2:-2]
    out_ref, sums_ref = refs[-2:]
    count = len(parts) // 3
    tokens, piece = parts[0].shape
    third = count * piece
    turned = x_ref[...].T
    for c in range(count):
        for i in range(3):
            at = i * third + c * piece
            out_ref[:, at : at + piece] = dot(turned, parts[3 * c + i][...]).astype(bfloat)
    out_ref[:, 3 * third :] = other_ref[...]

    @pl.when(pl.program_id(0) == 0)
    def _():
        ones = jnp.ones((16, tokens), bfloat)
        for c in range(count):
            for i in (0, 2):
                total = dot(ones, parts[3 * c + i][...])
                sums_ref[:, i // 2 * third + c * piece : i // 2 * third + (c + 1) * piece] = total[:8]


def input_grad(x, other, parts):
    tokens, features = x.shape
    piece = parts[0].shape[1]
    third = piece * len(parts) // 3
    step = 256
    return pl.pallas_call(
        input_grad_kernel,
        grid=(features // step,),
        in_specs=[
            pl.BlockSpec((tokens, step), lambda t: (0, t)),
            pl.BlockSpec((step, other.shape[1]), lambda t: (t, 0)),
        ]
        + [pl.BlockSpec((tokens, piece), lambda t: (0, 0))] * len(parts),
        out_specs=[
            pl.BlockSpec((step, 3 * third + other.shape[1]), lambda t: (t, 0)),
            pl.BlockSpec((8, 2 * third), lambda t: (0, 0)),
        ],
        out_shape=[
            jax.ShapeDtypeStruct((features, 3 * third + other.shape[1]), bfloat),
            jax.ShapeDtypeStruct((8, 2 * third), single),
        ],
        compiler_params=params(60),
        cost_estimate=cost(6 * tokens * features * third, 2 * tokens * features * 5),
        name="input_grad",
    )(x, other, *parts)


def middle_kernel(
    parts, *refs
):
    mixed_refs = refs[:parts]
    weight_ref, bias_ref, x_ref, gate_ref, scale_ref, shift_ref = refs[parts : parts + 6]
    attended_ref, middle_ref, normed_ref, first_ref, last_ref, grouped = refs[parts + 6 :]
    rows, columns, features = x_ref.shape[1:]
    sub = columns // COLUMN_PARTS
    quarter = rows * columns // 4
    total = bias_ref[...]
    at = 0
    for ref in mixed_refs:
        width = ref.shape[-1]
        total = total + dot(ref[0].reshape(4 * quarter, width), weight_ref[at : at + width])
        at += width
    grouped[...] = total.reshape(4, quarter, features)
    gate = gate_ref[0]
    scale = 1.0 + scale_ref[0]
    shift = shift_ref[0]

    for pair in range(rows // 2):
        for a in range(2):
            row = pair * 2 + a
            for j in range(COLUMN_PARTS):
                line = slice(j * sub, (j + 1) * sub)
                cells = grouped[
                    2 * a + j % 2, pl.ds((pair * 2 + j // 2) * sub, sub)
                ]
                attended_ref[0, row, line] = cells
                middle = x_ref[0, row, line].astype(single) + gate * cells
                middle_ref[0, row, line] = middle
                low = (norm_parts(middle)[0] * scale + shift).astype(bfloat)
                normed_ref[0, row, line] = low
                if row < 2:
                    first_ref[0, row, line] = low
                if row >= rows - 2:
                    last_ref[0, row - rows + 2, line] = low


def middle_part(mixed, weight, bias, kept, gate, scale, shift):
    count, rows, columns, features = kept.shape
    quarter = rows * columns // 4
    image = pl.BlockSpec((1, rows, columns, features), lambda l: (l, 0, 0, 0))
    vector = pl.BlockSpec((1, 1, features), lambda l: (l, 0, 0))
    return pl.pallas_call(
        partial(middle_kernel, len(mixed)),
        grid=(count,),
        in_specs=[
            pl.BlockSpec((1, 4, quarter, m.shape[-1]), lambda l: (l, 0, 0, 0)) for m in mixed
        ]
        + [
            pl.BlockSpec((features, features), lambda l: (0, 0)),
            pl.BlockSpec((1, features), lambda l: (0, 0)),
            image, vector, vector, vector,
        ],
        out_specs=[image] * 3
        + [pl.BlockSpec((1, 2, columns, features), lambda l: (l, 0, 0, 0))] * 2,
        out_shape=[
            jax.ShapeDtypeStruct(kept.shape, single),
            jax.ShapeDtypeStruct(kept.shape, single),
            jax.ShapeDtypeStruct(kept.shape, bfloat),
        ]
        + [jax.ShapeDtypeStruct((count, 2, columns, features), bfloat)] * 2,
        scratch_shapes=[pltpu.VMEM((4, quarter, features), single)],
        compiler_params=params(60),
        cost_estimate=cost(2 * kept.size * features, 14 * kept.size),
        name="middle",
    )(*mixed, weight, bias, kept, gate, scale, shift)


def feed_upstream_kernel(db_ref, ws_ref, out_ref):
    out_ref[...] = dot_nt(db_ref[...], ws_ref[...]).astype(bfloat)


def feed_upstream(db, ws):
    count, tall, columns, features = db.shape
    hidden = ws.shape[0]
    lines = count * tall * columns
    return pl.pallas_call(
        feed_upstream_kernel,
        grid=(hidden // features,),
        in_specs=[
            pl.BlockSpec((lines, features), lambda s: (0, 0)),
            pl.BlockSpec((features, features), lambda s: (s, 0)),
        ],
        out_specs=pl.BlockSpec((lines, features), lambda s: (0, s)),
        out_shape=jax.ShapeDtypeStruct((lines, hidden), bfloat),
        compiler_params=params(60),
        cost_estimate=cost(2 * lines * features * hidden, 2 * lines * (features + hidden)),
        name="feed_upstream",
    )(db.reshape(lines, features), ws)


TURN_ROWS = 4


def feed_turn_kernel(parts, feeds, turns, *refs):
    (
        edge_ref, nb_ref, top_ref, bottom_ref, d_act_ref, we_ref, be_ref, taps_ref, bm_ref,
        middle_ref, attended_ref, g_ref, gate_b_ref, scale_ref, gate_a_ref, shrink_ref,
        ws_hbm, we_hbm, wo_hbm,
    ) = refs[:19]
    mixed_refs = refs[19 : 19 + parts]
    small_ref, act_hbm, d_hid_hbm, result_ref, d_middle_ref = refs[19 + parts : 24 + parts]
    d_mixed_refs = refs[24 + parts : 24 + 2 * parts]
    (
        gw_ref, sums_ref,
        nb_wide, hidden, wide, d_wide, act_s, d_hid_s, ws, we, wo, gw_sum, grouped, branch_s, e_s, sums,
        weight_sem, act_sem, d_hid_sem,
    ) = refs[24 + 2 * parts :]
    step = pl.program_id(0)
    columns, features = nb_ref.shape[2:]
    sub = columns // COLUMN_PARTS
    weights = (
        pltpu.make_async_copy(ws_hbm, ws, weight_sem.at[0]),
        pltpu.make_async_copy(we_hbm, we, weight_sem.at[1]),
        pltpu.make_async_copy(wo_hbm, wo, weight_sem.at[2]),
    )

    def out_copies(n):
        at = pl.ds(pl.multiple_of(n * features, features), features)
        return (
            pltpu.make_async_copy(act_s.at[:, at], act_hbm.at[:, at], act_sem.at[n]),
            pltpu.make_async_copy(d_hid_s.at[:, at], d_hid_hbm.at[:, at], d_hid_sem.at[n]),
        )

    @pl.when(step == 0)
    def _():
        count, rows = nb_ref.shape[:2]
        own = rows * columns
        tall = (rows + 4) * columns
        for c in weights:
            c.start()
        for l in range(count):
            nb_wide[l * tall : l * tall + 2 * columns] = top_ref[l].reshape(2 * columns, features)
            nb_wide[l * tall + 2 * columns : (l + 1) * tall - 2 * columns] = nb_ref[l].reshape(
                own, features
            )
            nb_wide[(l + 1) * tall - 2 * columns : (l + 1) * tall] = bottom_ref[l].reshape(
                2 * columns, features
            )

    @pl.when(step < feeds)
    def _():
        feed_step(
            step, edge_ref, d_act_ref, we_ref, be_ref, taps_ref, bm_ref, small_ref,
            nb_wide, hidden, wide, d_wide, act_s, d_hid_s, nb_ref.shape,
        )
        for c in out_copies(step):
            c.start()

    @pl.when(step == feeds)
    def _():
        for c in weights:
            c.wait()

    @pl.when(step >= feeds)
    def _():
        turn_step(
            step, feeds, turns, middle_ref, attended_ref, g_ref, gate_b_ref, scale_ref, gate_a_ref,
            shrink_ref, mixed_refs, result_ref, d_middle_ref, d_mixed_refs, gw_ref, sums_ref,
            act_s, d_hid_s, ws, we, wo, gw_sum, grouped, branch_s, e_s, sums,
        )

    @pl.when(step == pl.num_programs(0) - 1)
    def _():
        for n in range(feeds):
            for c in out_copies(n):
                c.wait()


def feed_step(
    step, edge_ref, d_act_ref, we_ref, be_ref, taps_ref, bm_ref, small_ref,
    nb_wide, hidden, wide, d_wide, act_s, d_hid_s, shape,
):
    count, rows, columns, features = shape
    sub = columns // COLUMN_PARTS
    block = we_ref.shape[1]
    own = rows * columns
    tall = (rows + 4) * columns
    mid = (rows + 2) * columns
    hidden[...] = (dot(nb_wide[...], we_ref[...]) + be_ref[...]).astype(bfloat)
    small_ref[...] = jnp.zeros_like(small_ref)

    c0 = math.sqrt(2.0 / math.pi)
    c1 = c0 * 0.044715

    @pl.loop(0, count * (block // LANES))
    def _(index):
        l = index // (block // LANES)
        at = pl.ds(pl.multiple_of((index % (block // LANES)) * LANES, LANES), LANES)
        out = pl.ds(
            pl.multiple_of(step * block + index % (block // LANES) * LANES, LANES), LANES
        )
        taps = [taps_ref[t : t + 1, at] for t in range(9)]
        bias = bm_ref[:, at]
        for row in range(rows + 4):
            cells = hidden[pl.ds(pl.multiple_of(l * tall + row * columns, columns), columns), at]
            if row < 2:
                cells = cells * edge_ref[0].astype(bfloat)
            if row >= rows + 2:
                cells = cells * edge_ref[1].astype(bfloat)
            put_wide(wide, row, cells.reshape(COLUMN_PARTS, sub, LANES))
        taps = [(t + jnp.zeros((sub, LANES), single)).astype(bfloat) for t in taps]
        for row in range(rows + 2):
            v = conv_low(wide, row, taps).astype(single) + bias
            cube = (v * v) * c1
            half = 0.5 * jnp.tanh(v * (cube + c0)) + 0.5
            gelu = v * half
            slope = half + gelu * (1.0 - half) * (6.0 * cube + 2.0 * c0)
            if 1 <= row <= rows:
                act_s[
                    pl.ds(pl.multiple_of(l * own + (row - 1) * columns, columns), columns), out
                ] = gelu.reshape(columns, LANES).astype(bfloat)
            grad = d_act_ref[pl.ds(pl.multiple_of(l * mid + row * columns, columns), columns), at]
            grad = grad.astype(single).reshape(COLUMN_PARTS, sub, LANES) * slope
            put_wide(d_wide, row, grad.astype(bfloat))
        sums = [jnp.zeros((sub, LANES), single) for _ in range(11)]
        for row in range(rows):
            d_in = conv_back_row(d_wide, row, taps).astype(bfloat)
            d_hid_s[pl.ds(pl.multiple_of(l * own + row * columns, columns), columns), out] = (
                d_in.reshape(columns, LANES)
            )
            center = d_wide[row + 1, 1 : COLUMN_PARTS + 1]
            for i in range(3):
                for j in range(3):
                    term = center * wide[row + 1 + i, j : j + COLUMN_PARTS]
                    term = (term[0] + term[1]) + (term[2] + term[3])
                    sums[3 * i + j] += term.astype(single)
            sums[9] += jnp.sum(center.astype(single), axis=0)
            sums[10] += jnp.sum(d_in.astype(single), axis=0)
        for t in range(11):
            small_ref[t : t + 1, at] += jnp.sum(sums[t], axis=0, keepdims=True)


def turn_step(
    step, feeds, turns, middle_ref, attended_ref, g_ref, gate_b_ref, scale_ref, gate_a_ref,
    shrink_ref, mixed_refs, result_ref, d_middle_ref, d_mixed_refs, gw_ref, sums_ref,
    act_s, d_hid_s, ws, we, wo, gw_sum, grouped, branch_s, e_s, sums,
):
    columns, features = g_ref.shape[2:]
    sub = columns // COLUMN_PARTS
    rows = g_ref.shape[1]
    quarter = rows * columns // 4
    back = column_order(columns, True)
    gate_b = gate_b_ref[0]
    scale = 1.0 + scale_ref[0]
    gate_a = gate_a_ref[0]
    piece_of = step - feeds
    lines = pl.ds(pl.multiple_of(piece_of * rows * columns, rows * columns), rows * columns)

    branch_s[...] = dot(act_s[lines], ws[...]) + shrink_ref[...]
    e_s[...] = dot_nt(d_hid_s[lines], we[...])

    @pl.when(piece_of % turns == 0)
    def _():
        sums[...] = jnp.zeros_like(sums)

    for pair in range(rows // 2):
        for a in range(2):
            row = pair * 2 + a
            lows = []
            for j in range(COLUMN_PARTS):
                line = slice(j * sub, (j + 1) * sub)
                at = pl.ds(row * columns + j * sub, sub)
                branch = branch_s[at]
                middle = middle_ref[0, row, line]
                g = g_ref[0, row, line].astype(single)
                lows.append((middle + gate_b * branch).astype(bfloat))
                normed, inverse = norm_parts(middle)
                e = e_s[at]
                d_middle = g + norm_back(normed, inverse, e * scale)
                d_middle_ref[0, row, line] = d_middle
                low = (d_middle * gate_a).astype(bfloat)
                grouped[
                    2 * a + j % 2, pl.ds((pair * 2 + j // 2) * sub, sub)
                ] = low
                terms = (
                    g * branch, e, e * normed, d_middle * attended_ref[0, row, line], low.astype(single)
                )
                for t, term in enumerate(terms):
                    sums[t] += jnp.sum(term.reshape(sub // 8, 8, features), axis=0)
            result_ref[0, row] = dot(back, jnp.concatenate(lows, axis=0)).astype(bfloat)

    for t in range(5):
        sums_ref[0, t : t + 1] = jnp.sum(sums[t], axis=0, keepdims=True)
    sums_ref[0, 5:8] = jnp.zeros((3, features), single)
    grad = grouped[...].reshape(4 * quarter, features)
    at = 0
    for mixed_ref, d_ref in zip(mixed_refs, d_mixed_refs):
        width = mixed_ref.shape[-1]
        piece = slice(at, at + width)
        d_ref[0] = dot_nt(grad, wo[piece]).astype(bfloat).reshape(4, quarter, width)
        part = dot_tn(mixed_ref[0].reshape(4 * quarter, width), grad)

        @pl.when(piece_of == 0)
        def _():
            gw_sum[piece] = part

        @pl.when(piece_of > 0)
        def _():
            gw_sum[piece] += part

        at += width

    @pl.when(step == pl.num_programs(0) - 1)
    def _():
        gw_ref[...] = gw_sum[...].astype(bfloat)


def feed_turn(
    edge, nb, top, bottom, d_act, we, be, taps, bm, ws, middle, attended, g, gate_b, scale, gate_a,
    shrink_bias, wo, mixed,
):
    count, rows, columns, features = nb.shape
    hidden = we.shape[1]
    block = features
    feeds = hidden // block
    tokens = count * rows * columns
    tall = count * (rows + 4) * columns
    mid = count * (rows + 2) * columns
    sub = columns // COLUMN_PARTS
    some = min(TURN_ROWS, rows)
    turns = rows // some
    quarter = some * columns // 4
    whole = lambda a: pl.BlockSpec(a.shape, lambda s: (0,) * a.ndim)
    feed = lambda s: jnp.minimum(s, feeds - 1)
    place = lambda s: jnp.maximum(s - feeds, 0)
    column = lambda n: pl.BlockSpec((n, block), lambda s: (0, feed(s)))
    image = pl.BlockSpec(
        (1, some, columns, features), lambda s: (place(s) // turns, place(s) % turns, 0, 0)
    )
    vector = pl.BlockSpec((1, 1, features), lambda s: (place(s) // turns, 0, 0))
    groups = [
        pl.BlockSpec(
            (1, 4, quarter, m.shape[-1]), lambda s: (place(s) // turns, 0, place(s) % turns, 0)
        )
        for m in mixed
    ]
    hbm = pl.BlockSpec(memory_space=pl.ANY)
    return pl.pallas_call(
        partial(feed_turn_kernel, len(mixed), feeds, turns),
        grid=(feeds + count * turns,),
        in_specs=[
            pl.BlockSpec(memory_space=pltpu.SMEM),
            whole(nb), whole(top), whole(bottom),
            column(mid), column(features), column(1), column(16), column(1),
            image, image, image, vector, vector, vector, whole(shrink_bias), hbm, hbm, hbm,
        ]
        + groups,
        out_specs=[column(16), hbm, hbm, image, image]
        + groups
        + [
            pl.BlockSpec((features, features), lambda s: (0, 0)),
            pl.BlockSpec((1, 8, features), lambda s: (place(s) // turns, 0, 0)),
        ],
        out_shape=[
            jax.ShapeDtypeStruct((16, hidden), single),
            jax.ShapeDtypeStruct((tokens, hidden), bfloat),
            jax.ShapeDtypeStruct((tokens, hidden), bfloat),
            jax.ShapeDtypeStruct(g.shape, bfloat),
            jax.ShapeDtypeStruct(g.shape, single),
        ]
        + [jax.ShapeDtypeStruct(m.shape, bfloat) for m in mixed]
        + [
            jax.ShapeDtypeStruct((features, features), bfloat),
            jax.ShapeDtypeStruct((count, 8, features), single),
        ],
        scratch_shapes=[
            pltpu.VMEM((tall, features), bfloat),
            pltpu.VMEM((tall, block), bfloat),
            pltpu.VMEM((rows + 4, COLUMN_PARTS + 2, sub, LANES), bfloat),
            pltpu.VMEM((rows + 2, COLUMN_PARTS + 2, sub, LANES), bfloat),
            pltpu.VMEM((tokens, hidden), bfloat),
            pltpu.VMEM((tokens, hidden), bfloat),
            pltpu.VMEM((hidden, features), bfloat),
            pltpu.VMEM((features, hidden), bfloat),
            pltpu.VMEM((features, features), bfloat),
            pltpu.VMEM((features, features), single),
            pltpu.VMEM((4, quarter, features), bfloat),
            pltpu.VMEM((some * columns, features), single),
            pltpu.VMEM((some * columns, features), single),
            pltpu.VMEM((5, 8, features), single),
            pltpu.SemaphoreType.DMA((3,)),
            pltpu.SemaphoreType.DMA((feeds,)),
            pltpu.SemaphoreType.DMA((feeds,)),
        ],
        compiler_params=params(62),
        cost_estimate=cost(
            2 * features * hidden * (tall + 2 * tokens) + 4 * g.size * features,
            30 * g.size + 8 * features * hidden + 6 * tokens * hidden,
            mid * hidden,
        ),
        name="feed_turn",
    )(
        edge, nb, top, bottom, d_act, we, be, taps, bm, middle, attended, g, gate_b, scale, gate_a,
        shrink_bias, ws, we, wo, *mixed,
    )


def feed_grads_kernel(
    act_ref, d_hid_ref, nb_ref, db_ref, out_ref, db_own, shrink_s, expand_s, shrink_sem, expand_sem
):
    count, rows, columns, features = nb_ref.shape
    own = rows * columns
    step = pl.program_id(0)
    steps = pl.num_programs(0)
    some, slots, unit = shrink_s.shape[:3]

    @pl.when(step == 0)
    def _():
        for l in range(count):
            db_own[l * own : (l + 1) * own] = db_ref[l, 1 : rows + 1].reshape(own, features)

    def copies(s):
        return (
            pltpu.make_async_copy(
                shrink_s, out_ref.at[pl.ds(s * some, some), pl.ds(0, slots)], shrink_sem
            ),
            pltpu.make_async_copy(expand_s, out_ref.at[:, slots + s], expand_sem),
        )

    shrink = dot_tn(act_ref[...], db_own[...])
    expand = dot_tn(nb_ref[...].reshape(count * own, features), d_hid_ref[...])

    @pl.when(step > 0)
    def _():
        for c in copies(step - 1):
            c.wait()

    shrink_s[...] = shrink.reshape(shrink_s.shape).astype(bfloat)
    expand_s[...] = expand.reshape(expand_s.shape).astype(bfloat)
    for c in copies(step):
        c.start()

    @pl.when(step == steps - 1)
    def _():
        for c in copies(step):
            c.wait()


def feed_grads(act, d_hid, nb, db, devices):
    count, rows, columns, features = nb.shape
    tokens, hidden = act.shape
    block = features
    steps = hidden // block
    unit = features // devices
    if unit % 8:
        shrink = dot_tn(act, db[:, 1:-1].reshape(tokens, features))
        expand = dot_tn(nb.reshape(tokens, features), d_hid)
        return jnp.concatenate(
            [
                shrink.reshape(devices, steps, unit, features),
                expand.reshape(devices, unit, steps, features).transpose(0, 2, 1, 3),
            ],
            axis=1,
        ).astype(bfloat)
    whole = lambda a: pl.BlockSpec(a.shape, lambda s: (0,) * a.ndim)
    return pl.pallas_call(
        feed_grads_kernel,
        grid=(steps,),
        in_specs=[
            pl.BlockSpec((tokens, block), lambda s: (0, s)),
            pl.BlockSpec((tokens, block), lambda s: (0, s)),
            whole(nb), whole(db),
        ],
        out_specs=pl.BlockSpec(memory_space=pl.ANY),
        out_shape=jax.ShapeDtypeStruct((devices, 2 * steps, unit, features), bfloat),
        scratch_shapes=[
            pltpu.VMEM((tokens, features), bfloat),
            pltpu.VMEM((devices // steps, steps, unit, features), bfloat),
            pltpu.VMEM((devices, unit, features), bfloat),
            pltpu.SemaphoreType.DMA,
            pltpu.SemaphoreType.DMA,
        ],
        compiler_params=params(60),
        cost_estimate=cost(4 * features * hidden * tokens, 8 * features * hidden + 4 * tokens * hidden),
        name="feed_grads",
    )(act, d_hid, nb, db)


def final_kernel(
    d_ref, top_ref, bottom_ref, normed_ref, x_ref, d_middle_ref, scale_ref, taps_ref,
    out_ref, taps_out_ref, sums_ref, wide, d_wide,
):
    rows, columns, features = x_ref.shape[1:]
    sub = columns // COLUMN_PARTS
    back = column_order(columns, True)
    scale = 1.0 + scale_ref[0]

    def piece(ref, a, start):
        parts = [
            ref[0, 2 * a + j % 2, pl.ds(pl.multiple_of(start + (j // 2) * sub, sub), sub)]
            for j in range(COLUMN_PARTS)
        ]
        return jnp.stack(parts, axis=0).astype(single)

    def halo(ref):
        parts = [
            ref[0, j % 2, pl.ds((j // 2) * sub, sub)] for j in range(COLUMN_PARTS)
        ]
        return jnp.stack(parts, axis=0).astype(single)

    put_wide(d_wide, 0, halo(top_ref))
    put_wide(d_wide, rows + 1, halo(bottom_ref))

    @pl.loop(0, rows // 2)
    def _(pair):
        for a in range(2):
            put_wide(d_wide, pair * 2 + a + 1, piece(d_ref, a, pair * 2 * sub))

    @pl.loop(0, rows + 2)
    def _(row):
        for j in range(COLUMN_PARTS):
            put_part(wide, row, j, normed_ref[0, row, j * sub : (j + 1) * sub].astype(single))

    @pl.when(pl.program_id(0) == 0)
    def _():
        taps_out_ref[...] = jnp.zeros_like(taps_out_ref)

    d_normed = wide
    for lane in range(0, features, LANES):
        at = pl.ds(lane, LANES)
        taps = [taps_ref[t : t + 1, at] for t in range(9)]

        def step(row, sums):
            total = None
            center = d_wide[row + 1, 1 : COLUMN_PARTS + 1, :, at]
            sums = list(sums)
            for i in range(3):
                for j in range(3):
                    term = taps[3 * i + j] * d_wide[row + 2 - i, 2 - j : 2 - j + COLUMN_PARTS, :, at]
                    total = term if total is None else total + term
                    sums[3 * i + j] = sums[3 * i + j] + jnp.sum(
                        center * wide[row + i, j : j + COLUMN_PARTS, :, at], axis=0
                    )
            sums[9] = sums[9] + jnp.sum(center, axis=0)
            d_normed[row, 1 : COLUMN_PARTS + 1, :, at] = total
            return tuple(sums)

        sums = lax.fori_loop(
            0, rows, step, tuple(jnp.zeros((sub, LANES), single) for _ in range(10))
        )
        for t in range(10):
            taps_out_ref[t : t + 1, at] += jnp.sum(sums[t], axis=0, keepdims=True)

    def last(row, sums):
        lows = []
        for j in range(COLUMN_PARTS):
            line = slice(j * sub, (j + 1) * sub)
            cells = d_normed[row, j + 1]
            normed, inverse = norm_parts(x_ref[0, row, line].astype(single))
            grad = d_middle_ref[0, row, line] + norm_back(normed, inverse, cells * scale)
            lows.append(grad.astype(bfloat))
            sums = tuple(
                s + jnp.sum(t.reshape(sub // 8, 8, features), axis=0)
                for s, t in zip(sums, (cells, cells * normed))
            )
        out_ref[0, row] = dot(back, jnp.concatenate(lows, axis=0)).astype(bfloat)
        return sums

    sums = tuple(jnp.zeros((8, features), single) for _ in range(2))
    for row in range(rows):
        sums = last(row, sums)
    for t in range(2):
        sums_ref[0, t : t + 1] = jnp.sum(sums[t], axis=0, keepdims=True)
    sums_ref[0, 2:8] = jnp.zeros((6, features), single)


def final(d_reduced, top, bottom, normed, kept, d_middle, scale, taps):
    count, rows, columns, features = kept.shape
    quarter = rows * columns // 4
    sub = columns // COLUMN_PARTS
    image = lambda r: pl.BlockSpec((1, r, columns, features), lambda l: (l, 0, 0, 0))
    vector = pl.BlockSpec((1, 1, features), lambda l: (l, 0, 0))
    side = pl.BlockSpec((1, 2, 2 * sub, features), lambda l: (l, 0, 0, 0))
    return pl.pallas_call(
        final_kernel,
        grid=(count,),
        in_specs=[
            pl.BlockSpec((1, 4, quarter, features), lambda l: (l, 0, 0, 0)),
            side, side, image(rows + 2), image(rows), image(rows), vector,
            pl.BlockSpec((16, features), lambda l: (0, 0)),
        ],
        out_specs=[
            image(rows),
            pl.BlockSpec((16, features), lambda l: (0, 0)),
            pl.BlockSpec((1, 8, features), lambda l: (l, 0, 0)),
        ],
        out_shape=[
            jax.ShapeDtypeStruct(kept.shape, bfloat),
            jax.ShapeDtypeStruct((16, features), single),
            jax.ShapeDtypeStruct((count, 8, features), single),
        ],
        scratch_shapes=[pltpu.VMEM((rows + 2, COLUMN_PARTS + 2, sub, features), single)] * 2,
        compiler_params=params(60),
        cost_estimate=cost(kept.size * 180, kept.size * 12),
        name="final",
    )(d_reduced, top, bottom, normed, kept, d_middle, scale, taps)


def from_above(tail):
    count = lax.axis_size("strips")
    return lax.ppermute(tail, "strips", [(i, i + 1) for i in range(count - 1)])


def from_below(head):
    count = lax.axis_size("strips")
    return lax.ppermute(head, "strips", [(i + 1, i) for i in range(count - 1)])


def time_features(timesteps, halves):
    frequency = jnp.exp(-math.log(10000.0) * jnp.arange(halves, dtype=jnp.float32) / halves)
    phase = timesteps.astype(jnp.float32)[:, None] * frequency[None, :]
    return jnp.concatenate([jnp.cos(phase), jnp.sin(phase)], axis=1)


def thirds(value):
    high = value.astype(bfloat)
    rest = value - high.astype(single)
    middle = rest.astype(bfloat)
    low = (rest - middle.astype(single)).astype(bfloat)
    return jnp.concatenate([high, middle, low], axis=0)


def exact(value, weight, nt=False):
    n = value.shape[0]
    out = (dot_nt if nt else dot)(thirds(value), weight)
    return out[:n] + out[n : 2 * n] + out[2 * n :]


def silu(value):
    return value * (1.0 / (1.0 + jnp.exp(-value)))


def silu_slope(value):
    gate = 1.0 / (1.0 + jnp.exp(-value))
    return gate * (1.0 + value * (1.0 - gate))


def label_rows(labels, classes):
    return (lax.broadcasted_iota(jnp.int32, (labels.shape[0], classes), 1) == labels).astype(bfloat)


def condition(sinus, labels, wi_ref, bi_ref, wo_ref, bo_ref, table_ref):
    before = exact(sinus, wi_ref[...]) + bi_ref[...]
    inner = silu(before)
    onehot = label_rows(labels, table_ref.shape[1])
    cond = exact(inner, wo_ref[...]) + bo_ref[...] + dot_nt(onehot, table_ref[...])
    return before, inner, cond


def modulate_kernel(
    sinus_ref, label_ref, wi_ref, bi_ref, wo_ref, bo_ref, table_ref, ada_ref, ab_ref, out_ref, active
):
    @pl.when(pl.program_id(0) == 0)
    def _():
        cond = condition(
            sinus_ref[...], label_ref[...], wi_ref, bi_ref, wo_ref, bo_ref, table_ref
        )[2]
        active[...] = silu(cond)

    out_ref[0] = exact(active[...], ada_ref[...]) + ab_ref[...]


def modulate(sinus, labels, weights, ada, ada_bias):
    n = sinus.shape[0]
    features = ada.shape[0]
    whole = lambda a: pl.BlockSpec(a.shape, lambda s: (0,) * a.ndim)
    return pl.pallas_call(
        modulate_kernel,
        grid=(6,),
        in_specs=[whole(a) for a in (sinus, labels) + weights]
        + [
            pl.BlockSpec((features, features), lambda s: (0, s)),
            pl.BlockSpec((1, features), lambda s: (0, s)),
        ],
        out_specs=pl.BlockSpec((1, n, features), lambda s: (s, 0, 0)),
        out_shape=jax.ShapeDtypeStruct((6, n, features), single),
        scratch_shapes=[pltpu.VMEM((n, features), single)],
        compiler_params=params(16),
        cost_estimate=cost(50 * n * ada.size, 2 * ada.size),
        name="modulate",
    )(sinus, labels, *weights, ada, ada_bias)


def own_rows(me_ref, value, size):
    width = value.shape[1]
    place = lax.broadcasted_iota(jnp.int32, (size, width), 1)
    line = lax.broadcasted_iota(jnp.int32, (size, width), 0)
    pick = (place == me_ref[0] * size + line).astype(single)
    return lax.dot_general(
        pick, value, (((1,), (1,)), ((), ())), precision=highest, preferred_element_type=single
    )


def exact_small(a, b):
    return lax.dot_general(
        a, b, (((1,), (0,)), ((), ())), precision=highest, preferred_element_type=single
    )


def strip_sum(ref, kinds, count, features):
    lines = []
    for item in range(ref.shape[0]):
        for l in range(count):
            at = l * kinds * features
            lines.append(jnp.sum(
                    ref[item, :, at : at + kinds * features].astype(single), axis=0, keepdims=True
                ))
    return jnp.concatenate(lines, axis=0)


def early_kernel(
    count, me_ref, parts_ref, sinus_ref, label_ref, wi_ref, bi_ref, wo_ref, bo_ref, table_ref, ada_ref,
    before_ref, cond_ref, d_active_ref, ada_out_ref, d_mod_ref,
):
    features = ada_ref.shape[0]
    d_mod = strip_sum(parts_ref, 4, count, features)
    before, _, cond = condition(
        sinus_ref[...], label_ref[...], wi_ref, bi_ref, wo_ref, bo_ref, table_ref
    )
    before_ref[...] = before
    cond_ref[...] = cond
    d_active_ref[...] = exact(d_mod, ada_ref[:, 2 * features :], nt=True)
    size = ada_out_ref.shape[0]
    ada_out_ref[...] = exact_small(own_rows(me_ref, silu(cond), size), d_mod)
    d_mod_ref[...] = jnp.sum(d_mod, axis=0, keepdims=True)


def early_condition(me, parts, count, sinus, labels, weights, ada, size):
    n = sinus.shape[0]
    features = ada.shape[0]
    whole = lambda a: pl.BlockSpec(a.shape, lambda s: (0,) * a.ndim)
    shapes = [
        jax.ShapeDtypeStruct((n, features), single),
        jax.ShapeDtypeStruct((n, features), single),
        jax.ShapeDtypeStruct((n, features), single),
        jax.ShapeDtypeStruct((size, 4 * features), single),
        jax.ShapeDtypeStruct((1, 4 * features), single),
    ]
    return pl.pallas_call(
        partial(early_kernel, count),
        grid=(1,),
        in_specs=[pl.BlockSpec(memory_space=pltpu.SMEM)]
        + [whole(a) for a in (parts, sinus, labels) + weights + (ada,)],
        out_specs=[whole(a) for a in shapes],
        out_shape=shapes,
        compiler_params=params(28),
        cost_estimate=cost(50 * n * ada.size, 2 * ada.size),
        name="early_condition",
    )(me, parts, sinus, labels, *weights, ada)


def late_kernel(
    count, me_ref, parts_ref, before_ref, cond_ref, d_active_ref, ada_early_ref, d_mod_early_ref,
    sinus_ref, label_ref, wo_ref, ada_ref,
    ada_out_ref, d_mod_ref, table_out_ref, wo_out_ref, wi_out_ref, d_cond_ref, d_before_ref,
):
    features = wo_ref.shape[0]
    before = before_ref[...]
    cond = cond_ref[...]
    d_mod = strip_sum(parts_ref, 2, count, features)
    d_active = d_active_ref[...] + exact(d_mod, ada_ref[...], nt=True)
    d_cond = d_active * silu_slope(cond)
    d_before = exact(d_cond, wo_ref[...], nt=True) * silu_slope(before)
    size = ada_out_ref.shape[0]
    ada_out_ref[:, : 2 * features] = exact_small(own_rows(me_ref, silu(cond), size), d_mod)
    ada_out_ref[:, 2 * features :] = ada_early_ref[...]
    d_mod_ref[:, : 2 * features] = jnp.sum(d_mod, axis=0, keepdims=True)
    d_mod_ref[:, 2 * features :] = d_mod_early_ref[...]
    onehot = label_rows(label_ref[...], table_out_ref.shape[1]).astype(single)
    table_out_ref[...] = exact_small(own_rows(me_ref, d_cond, size), onehot)
    wo_out_ref[...] = exact_small(own_rows(me_ref, silu(before), size), d_cond)
    wi_out_ref[...] = exact_small(
        own_rows(me_ref, sinus_ref[...], wi_out_ref.shape[0]), d_before
    )
    d_cond_ref[...] = jnp.sum(d_cond, axis=0, keepdims=True)
    d_before_ref[...] = jnp.sum(d_before, axis=0, keepdims=True)


def late_condition(
    me, parts, count, before, cond, d_active, ada_early, d_mod_early, sinus, labels, wo, ada, classes,
    devices,
):
    features = ada.shape[0]
    size = features // devices
    whole = lambda a: pl.BlockSpec(a.shape, lambda s: (0,) * a.ndim)
    shapes = [
        jax.ShapeDtypeStruct((size, 6 * features), single),
        jax.ShapeDtypeStruct((1, 6 * features), single),
        jax.ShapeDtypeStruct((size, classes), single),
        jax.ShapeDtypeStruct((size, features), single),
        jax.ShapeDtypeStruct((sinus.shape[1] // devices, features), single),
        jax.ShapeDtypeStruct((1, features), single),
        jax.ShapeDtypeStruct((1, features), single),
    ]
    return pl.pallas_call(
        partial(late_kernel, count),
        grid=(1,),
        in_specs=[pl.BlockSpec(memory_space=pltpu.SMEM)]
        + [
            whole(a)
            for a in (parts, before, cond, d_active, ada_early, d_mod_early, sinus, labels, wo)
        ]
        + [pl.BlockSpec((features, 2 * features), lambda s: (0, 0))],
        out_specs=[whole(a) for a in shapes],
        out_shape=shapes,
        compiler_params=params(16),
        cost_estimate=cost(20 * ada.size, ada.size),
        name="late_condition",
    )(me, parts, before, cond, d_active, ada_early, d_mod_early, sinus, labels, wo, ada)


def sum_cores(keep, give):
    strips = lax.axis_size("strips")
    got = lax.ppermute(give, "strips", [(i, i ^ 1) for i in range(strips)])
    return (keep.astype(single) + got.astype(single)).astype(bfloat)


def sum_axis(part, axis, size, place, step):
    pick = lambda k: lax.dynamic_index_in_dim(part, place ^ k, 0, keepdims=False)
    count = lax.axis_size(axis)
    got = [
        lax.ppermute(pick(k), axis, [(i, i ^ (k * step)) for i in range(count)])
        for k in range(1, size)
    ]
    total = pick(0).astype(single)
    for g in got:
        total = total + g.astype(single)
    return total


def sum_items(part):
    return sum_axis(part, "items", lax.axis_size("items"), lax.axis_index("items"), 1).astype(bfloat)


def sum_strips(part):
    strip = lax.axis_index("strips")
    return sum_axis(part, "strips", lax.axis_size("strips") // 2, strip // 2, 2)


def after(value, *others):
    return lax.optimization_barrier((value,) + others)[0]


def tap_rows(kernel):
    return jnp.pad(kernel.astype(single).T, ((0, 7), (0, 0)))


def per_device(
    latents,
    timesteps,
    labels,
    time_in_weight,
    time_in_bias,
    time_out_weight,
    time_out_bias,
    label_table,
    ada_weight,
    ada_bias,
    down_kernel,
    down_bias,
    input_weight,
    query_bias,
    value_bias,
    output_weight,
    output_bias,
    expand_weight,
    expand_bias,
    mixer_kernel,
    mixer_bias,
    shrink_weight,
    shrink_bias,
    cotangent,
):
    count, rows, columns, features = latents.shape
    strips = lax.axis_size("strips")
    items = lax.axis_size("items")
    devices = strips * items
    strip = lax.axis_index("strips")
    item = lax.axis_index("items")
    me = item * strips + strip
    sub = columns // COLUMN_PARTS
    quarter = rows * columns // 4
    groups = count * 4
    share = strips // groups
    width = features // share
    row_vector = lambda v: v.astype(single).reshape(1, -1)
    edge = jnp.stack([strip > 0, strip < strips - 1]).astype(single)

    lines = -(-count // 8) * 8
    weights = (
        time_in_weight, row_vector(time_in_bias), time_out_weight, row_vector(time_out_bias),
        label_table,
    )
    waves = time_in_weight.shape[0] // 2
    modulation = modulate(
        time_features(jnp.pad(timesteps, (0, lines - count)), waves),
        jnp.pad(labels, (0, lines - count))[:, None],
        weights,
        ada_weight,
        row_vector(ada_bias),
    )
    shift_a, scale_a, gate_a, shift_b, scale_b, gate_b = (
        modulation[i, :count, None, :] for i in range(6)
    )

    ends = jnp.concatenate([latents[:, -1:], cotangent[:, -1:]], axis=1)
    starts = jnp.concatenate([latents[:, :1], cotangent[:, :1]], axis=1)
    above = from_above(ends)
    below = from_below(starts)

    down_taps = tap_rows(down_kernel)
    grouped, normed_a, kept = front(
        edge, latents, above[:, :1], below[:, :1], scale_a, shift_a, down_taps, row_vector(down_bias)
    )

    def spread(array):
        flat = array.reshape(groups, quarter, array.shape[-1])
        if share > 1:
            flat = jnp.repeat(flat, share, axis=0)
        got = lax.all_to_all(flat, "strips", 0, 0, tiled=True)
        return got.reshape(strips * quarter, array.shape[-1])

    def collect(array):
        flat = array.reshape(strips, quarter, array.shape[-1])
        return lax.all_to_all(flat, "strips", 0, 0, tiled=True)

    group = spread(grouped)
    g_kept, d_branch, grad_shrink_bias = upstream_parts(
        cotangent, above[:, 1:], below[:, 1:], gate_b
    )

    head_at = (strip % share) * width
    def own_columns(array, axis):
        return array if share == 1 else lax.dynamic_slice_in_dim(array, head_at, width, axis=axis)

    own_weight = jnp.concatenate(
        [own_columns(input_weight[:, i * features : (i + 1) * features], 1) for i in range(3)], axis=1
    ) if share > 1 else input_weight
    own_bias = jnp.concatenate(
        [own_columns(row_vector(b), 1) for b in (query_bias, value_bias)], axis=1
    )
    chunks = next(c for c in CHUNKS if width // LANES % c == 0)
    piece = width // chunks
    saved = []
    mixed = []
    d_act = feed_upstream(d_branch, shrink_weight)
    group, d_act, expand_line, mixer_taps, mixer_line, output_line, shrink_line = (
        lax.optimization_barrier(
            (
                group,
                d_act,
                row_vector(expand_bias),
                tap_rows(mixer_kernel),
                row_vector(mixer_bias),
                row_vector(output_bias),
                row_vector(shrink_bias),
            )
        )
    )
    for c in range(chunks):
        saved.append(attend(group, own_weight, own_bias, c * piece, piece))
        mixed.append(collect(saved[c][3]))
    if share == 1:
        mixed = [m.reshape(count, 4, quarter, piece) for m in mixed]
    else:
        joined = jnp.concatenate(mixed, axis=-1).reshape(groups, share, quarter, width)
        joined = joined.transpose(0, 2, 1, 3).reshape(count, 4, quarter, features)
        mixed = [joined]

    attended, middle, normed_b, first_rows, last_rows = middle_part(
        mixed, output_weight, output_line, kept, gate_a, scale_b, shift_b
    )
    feed_small, act, d_hid, *turned = feed_turn(
        edge,
        normed_b,
        from_above(last_rows),
        from_below(first_rows),
        d_act,
        expand_weight,
        expand_line,
        mixer_taps,
        mixer_line,
        shrink_weight,
        middle,
        attended,
        g_kept,
        gate_b,
        scale_b,
        gate_a,
        shrink_line,
        output_weight,
        mixed,
    )
    result, d_middle = turned[:2]
    d_mixed = turned[2:-2]
    grad_output, turn_sums = turned[-2:]

    hidden = expand_weight.shape[1]
    steps = hidden // features
    early = feed_grads(act, d_hid, normed_b, d_branch, devices)
    early_sum = lax.psum_scatter(early, both, scatter_dimension=0, tiled=False).astype(single)

    if share == 1:
        d_mixed = [spread(d) for d in d_mixed]
    else:
        parts = d_mixed[0].reshape(groups, quarter, share, width).transpose(0, 2, 1, 3)
        got = lax.all_to_all(parts.reshape(strips, quarter, width), "strips", 0, 0, tiled=True)
        got = got.reshape(strips * quarter, width)
        d_mixed = [got[:, c * piece : (c + 1) * piece] for c in range(chunks)]
    grads = []
    for c in range(chunks):
        if c == 0:
            d_mixed[c], _ = lax.optimization_barrier((d_mixed[c], early))
        q, k, v, out, logs = saved[c]
        if c < chunks - 1:
            grads.append(attend_back(q, k, v, out, d_mixed[c], logs))
        else:
            earlier = [g for chunk in grads for g in chunk]
            *last_grads, d_group = attend_back(
                q, k, v, out, d_mixed[c], logs, own_weight, earlier
            )
            grads.append(last_grads)
    size = features // devices
    narrow = jnp.stack([jnp.sum(turn_sums[:, 4], axis=0), jnp.sum(grad_shrink_bias[:, 0], axis=0)])
    to_all = jnp.concatenate(
        [
            turn_sums[:, 3], turn_sums[:, 1], turn_sums[:, 2], turn_sums[:, 0],
        ],
        axis=1,
    ).reshape(-1)
    whole_numbers = jnp.concatenate([timesteps // 32, timesteps % 32, labels // 32, labels % 32])
    to_all = jnp.concatenate([to_all, whole_numbers.astype(single)])
    fill = -(to_all.shape[0] + 11 * (hidden // devices) + 2 * size) % LANES
    early_small = jnp.concatenate(
        [
            jnp.broadcast_to(to_all, (devices, to_all.shape[0])),
            feed_small[:11].reshape(11, devices, -1).transpose(1, 0, 2).reshape(devices, -1),
            narrow.reshape(2, devices, -1).transpose(1, 0, 2).reshape(devices, -1),
            jnp.zeros((devices, fill), single),
        ],
        axis=1,
    ).astype(bfloat)
    early_small = after(early_small, *(grads[0][:1] if chunks > 1 else ()), *d_mixed)
    early_got = lax.all_to_all(early_small, both, 0, 0, tiled=True)

    parts = [g for chunk in grads for g in chunk]
    d_reduced = collect(d_group)
    if share > 1:
        d_reduced = jnp.sum(
            d_reduced.reshape(groups, share, quarter, features).astype(single), axis=1
        ).astype(bfloat)
    d_reduced = d_reduced.reshape(count, 4, quarter, features)
    late, d_sums = input_grad(after(group, d_group), grad_output, parts)
    d_query_sum = d_sums[0, :width]
    d_value_sum = d_sums[0, width:]
    if share > 1:
        zero = jnp.zeros((features, 3, features), bfloat)
        grad_input = lax.dynamic_update_slice(
            zero, late[:, : 3 * width].reshape(features, 3, width), (0, 0, head_at)
        ).reshape(features, 3 * features)
        late = jnp.concatenate([grad_input, grad_output], axis=1)
        flat = jnp.zeros((features,), single)
        d_query_sum = lax.dynamic_update_slice(flat, d_query_sum, (head_at,))
        d_value_sum = lax.dynamic_update_slice(flat, d_value_sum, (head_at,))
    late = late.reshape(items, strips // 2, 2, size, 4 * features)
    core = strip % 2
    keep = lax.dynamic_index_in_dim(late, core, 2, keepdims=False)
    give = lax.dynamic_index_in_dim(late, 1 - core, 2, keepdims=False)

    per_latent = count * 4 * features
    parts_early = early_got[:, :per_latent].reshape(items, strips, per_latent)
    first = early_got.reshape(items, strips, -1)[:, 0, per_latent : per_latent + 4 * count]
    first = first.astype(single).reshape(items, 4, count)
    all_times = (first[:, 0] * 32.0 + first[:, 1]).reshape(-1)
    all_labels = (first[:, 2] * 32.0 + first[:, 3]).reshape(-1, 1).astype(jnp.int32)
    sinus = time_features(all_times, waves)
    early_sums = jnp.sum(early_got[:, per_latent + 4 * count :].astype(single), axis=0)
    cut = 11 * (hidden // devices)
    feed_sum = early_sums[:cut].reshape(11, -1)
    narrow_sum = early_sums[cut : cut + 2 * size].reshape(2, size)
    index = jnp.reshape(me, (1,)).astype(jnp.int32)
    before, cond, d_active, grad_ada_early, d_mod_early = early_condition(
        index, parts_early, count, sinus, all_labels, weights, ada_weight, size
    )

    d_reduced, before, keep, give = lax.optimization_barrier((d_reduced, before, keep, give))
    late_part = sum_items(sum_cores(keep, give))
    grad_latents, down_small, final_sums = final(
        d_reduced,
        from_above(d_reduced[:, 2:, -2 * sub :]),
        from_below(d_reduced[:, :2, : 2 * sub]),
        normed_a,
        kept,
        d_middle,
        scale_a,
        down_taps,
    )

    late_narrow = jnp.concatenate([d_query_sum[None], d_value_sum[None], down_small[:10]], axis=0)
    to_all = final_sums[:, :2].reshape(-1)
    fill = -(to_all.shape[0] + 12 * size) % LANES
    late_small = jnp.concatenate(
        [
            jnp.broadcast_to(to_all, (devices, to_all.shape[0])),
            late_narrow.reshape(12, devices, size).transpose(1, 0, 2).reshape(devices, -1),
            jnp.zeros((devices, fill), single),
        ],
        axis=1,
    ).astype(bfloat)
    late_got = lax.all_to_all(late_small, both, 0, 0, tiled=True)
    late_got, late_part = lax.optimization_barrier((late_got, late_part))
    late_sum = sum_strips(late_part)
    late_sums = jnp.sum(late_got[:, to_all.shape[0] :].astype(single), axis=0)[: 12 * size].reshape(12, size)
    (
        grad_ada, d_mod, grad_table, grad_time_out, grad_time_in, d_cond, d_before,
    ) = late_condition(
        index,
        late_got[:, : to_all.shape[0]].reshape(items, strips, -1),
        count,
        before,
        cond,
        d_active,
        grad_ada_early,
        d_mod_early,
        sinus,
        all_labels,
        time_out_weight,
        ada_weight,
        label_table.shape[1],
        devices,
    )

    def mine(array):
        part = array.shape[-1] // devices
        return lax.dynamic_slice_in_dim(array[0], me * part, part, axis=0)

    return (
        result,
        grad_latents,
        grad_time_in,
        mine(d_before),
        grad_time_out,
        mine(d_cond),
        grad_table,
        grad_ada,
        mine(d_mod),
        late_sums[2:11].T,
        late_sums[11],
        late_sum[:, : 3 * features],
        late_sums[0],
        late_sums[1],
        late_sum[:, 3 * features :],
        narrow_sum[0],
        early_sum[steps:].transpose(1, 0, 2).reshape(size, hidden),
        feed_sum[10],
        feed_sum[:9].T,
        feed_sum[9],
        early_sum[:steps].reshape(hidden // devices, features),
        narrow_sum[1],
    )


def solution(mesh):
    image = P("items", "strips", None, None)
    split = P(both, None)
    line = P(both)
    return jax.shard_map(
        per_device,
        mesh=mesh,
        in_specs=(image, P("items"), P("items")) + (P(),) * 20 + (image,),
        out_specs=(
            image, image, split, line, split, line, split, split, line, split, line,
            split, line, line, split, line, split, line, split, line, split, line,
        ),
        check_vma=False,
    )
```

```python
from functools import partial
import math

import jax
import jax.numpy as jnp
from jax import lax
from jax.experimental import pallas as pl
from jax.experimental.pallas import tpu as pltpu
from jax.sharding import PartitionSpec as P

HEADS = 12
HEAD_DIM = 64
LANES = 128
COLUMN_PARTS = 4
CHUNKS = (2, 3, 1)

highest = lax.Precision.HIGHEST
epsilon = 1e-06
bfloat = jnp.bfloat16
single = jnp.float32
both = ("items", "strips")


def params(mebibytes):
    return pltpu.CompilerParams(vmem_limit_bytes=mebibytes * 1024 * 1024)


def cost(flops, moved, exps=0):
    return pl.CostEstimate(flops=int(flops), bytes_accessed=int(moved), transcendentals=int(exps))


def dot(a, b):
    return lax.dot_general(a, b, (((1,), (0,)), ((), ())), preferred_element_type=single)


def dot_nt(a, b):
    return lax.dot_general(a, b, (((1,), (1,)), ((), ())), preferred_element_type=single)


def dot_tn(a, b):
    return lax.dot_general(a, b, (((0,), (0,)), ((), ())), preferred_element_type=single)


def column_order(columns, back):
    sub = columns // COLUMN_PARTS
    first = lax.broadcasted_iota(jnp.int32, (columns, columns), 0)
    second = lax.broadcasted_iota(jnp.int32, (columns, columns), 1)
    kept, column = (second, first) if back else (first, second)
    return (column == COLUMN_PARTS * (kept % sub) + kept // sub).astype(bfloat)


def norm_parts(value):
    center = value - jnp.mean(value, axis=-1, keepdims=True)
    inverse = lax.rsqrt(jnp.mean(center * center, axis=-1, keepdims=True) + epsilon)
    return center * inverse, inverse


def norm_back(normed, inverse, grad):
    return inverse * (
        grad
        - jnp.mean(grad, axis=-1, keepdims=True)
        - normed * jnp.mean(grad * normed, axis=-1, keepdims=True)
    )


def put_wide(ref, row, cells):
    sub = cells.shape[1]
    place = lax.broadcasted_iota(jnp.int32, cells.shape[1:], 0)
    last = cells[COLUMN_PARTS - 1].astype(single)
    first = cells[0].astype(single)
    ref[row, 1 : COLUMN_PARTS + 1] = cells
    ref[row, 0] = jnp.where(place == 0, 0.0, pltpu.roll(last, 1, 0)).astype(ref.dtype)
    ref[row, COLUMN_PARTS + 1] = jnp.where(
        place == sub - 1, 0.0, pltpu.roll(first, sub - 1, 0)
    ).astype(ref.dtype)


def put_part(ref, row, j, cells):
    sub = cells.shape[0]
    place = lax.broadcasted_iota(jnp.int32, cells.shape, 0)
    ref[row, j + 1] = cells
    if j == COLUMN_PARTS - 1:
        ref[row, 0] = jnp.where(place == 0, 0.0, pltpu.roll(cells, 1, 0))
    if j == 0:
        ref[row, COLUMN_PARTS + 1] = jnp.where(place == sub - 1, 0.0, pltpu.roll(cells, sub - 1, 0))


def conv_low(ref, row, taps):
    total = None
    for i in range(3):
        line = [taps[3 * i + j] * ref[row + i, j : j + COLUMN_PARTS] for j in range(3)]
        line = (line[0] + line[1]) + line[2]
        total = line if total is None else total + line
    return total


def conv_back_row(ref, row, taps):
    total = None
    for i in range(3):
        line = [
            taps[3 * i + j] * ref[row + 2 - i, 2 - j : 2 - j + COLUMN_PARTS] for j in range(3)
        ]
        line = (line[0] + line[1]) + line[2]
        total = line if total is None else total + line
    return total


def front_kernel(
    edge_ref, x_ref, top_ref, bottom_ref, scale_ref, shift_ref, taps_ref, bias_ref,
    grouped_ref, normed_ref, kept_ref, wide,
):
    rows, columns, features = x_ref.shape[1:]
    sub = columns // COLUMN_PARTS
    order = column_order(columns, False)
    scale = 1.0 + scale_ref[0]
    shift = shift_ref[0]

    def fill(row, raw, keep, kept_row=None):
        cells = dot(order, raw)
        if kept_row is not None:
            kept_ref[0, kept_row] = cells.astype(bfloat)
        for j in range(COLUMN_PARTS):
            line = slice(j * sub, (j + 1) * sub)
            normed = norm_parts(cells[line])[0] * scale + shift
            low = (normed if keep is None else normed * keep).astype(bfloat)
            normed_ref[0, row, line] = low
            put_part(wide, row, j, low.astype(single))

    fill(0, top_ref[0, 0], edge_ref[0])
    fill(rows + 1, bottom_ref[0, 0], edge_ref[1])

    for row in range(rows):
        fill(row + 1, x_ref[0, row], None, row)

    taps = [taps_ref[t : t + 1] for t in range(9)]
    bias = bias_ref[...]

    @pl.loop(0, rows // 2)
    def _(pair):
        for a in range(2):
            for lane in range(0, features, LANES):
                at = pl.ds(lane, LANES)
                total = jnp.zeros((COLUMN_PARTS, sub, LANES), single) + bias[:, lane : lane + LANES]
                for i in range(3):
                    for j in range(3):
                        total = total + taps[3 * i + j][:, lane : lane + LANES] * wide[
                            pair * 2 + a + i, j : j + COLUMN_PARTS, :, at
                        ]
                low = total.astype(bfloat)
                for j in range(COLUMN_PARTS):
                    grouped_ref[
                        0, 2 * a + j % 2, pl.ds(pl.multiple_of((pair * 2 + j // 2) * sub, sub), sub), at
                    ] = low[j]


def front(edge, latents, top, bottom, scale, shift, taps, bias):
    count, rows, columns, features = latents.shape
    quarter = rows * columns // 4
    sub = columns // COLUMN_PARTS
    image = lambda r: pl.BlockSpec((1, r, columns, features), lambda l: (l, 0, 0, 0))
    vector = pl.BlockSpec((1, 1, features), lambda l: (l, 0, 0))
    return pl.pallas_call(
        front_kernel,
        grid=(count,),
        in_specs=[
            pl.BlockSpec(memory_space=pltpu.SMEM),
            image(rows), image(1), image(1), vector, vector,
            pl.BlockSpec((16, features), lambda l: (0, 0)),
            pl.BlockSpec((1, features), lambda l: (0, 0)),
        ],
        out_specs=[
            pl.BlockSpec((1, 4, quarter, features), lambda l: (l, 0, 0, 0)),
            image(rows + 2), image(rows),
        ],
        out_shape=[
            jax.ShapeDtypeStruct((count, 4, quarter, features), bfloat),
            jax.ShapeDtypeStruct((count, rows + 2, columns, features), bfloat),
            jax.ShapeDtypeStruct((count, rows, columns, features), bfloat),
        ],
        scratch_shapes=[pltpu.VMEM((rows + 2, COLUMN_PARTS + 2, sub, features), single)],
        compiler_params=params(18),
        cost_estimate=cost(count * rows * columns * features * 150, count * rows * columns * features * 8),
        name="front",
    )(edge, latents, top, bottom, scale, shift, taps, bias)


def upstream_kernel(g_ref, top_ref, bottom_ref, gate_ref, kept_ref, branch_ref, bias_ref):
    rows, columns, features = g_ref.shape[1:]
    order = column_order(columns, False)
    gate = gate_ref[0]

    def low(raw):
        cells = dot(order, raw)
        return cells, (cells * gate).astype(bfloat)

    branch_ref[0, 0] = low(top_ref[0, 0])[1]
    branch_ref[0, rows + 1] = low(bottom_ref[0, 0])[1]

    def step(row, total):
        cells, grad = low(g_ref[0, row])
        kept_ref[0, row] = cells.astype(bfloat)
        branch_ref[0, row + 1] = grad
        return total + jnp.sum(grad.astype(single), axis=0, keepdims=True)

    total = jnp.zeros((1, features), single)
    for row in range(rows):
        total = step(row, total)
    bias_ref[0] = total


def upstream_parts(cotangent, top, bottom, gate):
    count, rows, columns, features = cotangent.shape
    image = lambda r: pl.BlockSpec((1, r, columns, features), lambda l: (l, 0, 0, 0))
    vector = pl.BlockSpec((1, 1, features), lambda l: (l, 0, 0))
    return pl.pallas_call(
        upstream_kernel,
        grid=(count,),
        in_specs=[image(rows), image(1), image(1), vector],
        out_specs=[image(rows), image(rows + 2), vector],
        out_shape=[
            jax.ShapeDtypeStruct((count, rows, columns, features), bfloat),
            jax.ShapeDtypeStruct((count, rows + 2, columns, features), bfloat),
            jax.ShapeDtypeStruct((count, 1, features), single),
        ],
        compiler_params=params(14),
        cost_estimate=cost(count * rows * columns * features * 130, count * rows * columns * features * 6),
        name="upstream",
    )(cotangent, top, bottom, gate)


QUERY_STEP = 1024
QUERY_STEP_BACK = 256


def attend_kernel(
    x_ref, wq_ref, wk_ref, wv_ref, bq_ref, bv_ref, q_ref, k_ref, v_ref, mixed_ref, log_ref
):
    tokens = x_ref.shape[0]
    base = math.log2(math.e) / math.sqrt(HEAD_DIM)

    @pl.when(pl.program_id(0) == 0)
    def _():
        x = x_ref[...]
        q_ref[...] = (dot(x, wq_ref[...]) + bq_ref[...]).astype(bfloat)
        k_ref[...] = dot(x, wk_ref[...]).astype(bfloat)
        v_ref[...] = (dot(x, wv_ref[...]) + bv_ref[...]).astype(bfloat)

    pair = pl.ds(pl.multiple_of(pl.program_id(0) * LANES, LANES), LANES)
    keys = k_ref[:, pair]
    values = v_ref[:, pair].T
    lane = lax.broadcasted_iota(jnp.int32, (QUERY_STEP, LANES), 1)
    for at in range(0, tokens, QUERY_STEP):
        part = q_ref[at : at + QUERY_STEP, pair]
        outs = []
        for head in range(LANES // HEAD_DIM):
            own = jnp.where(lane // HEAD_DIM == head, part, jnp.zeros_like(part))
            scores = dot_nt(keys, own)
            peak = jnp.max(scores, axis=0, keepdims=True) * base
            soft = jnp.exp2(scores * base - peak)
            total = jnp.sum(soft, axis=0, keepdims=True)
            log_ref[0, head : head + 1, at : at + QUERY_STEP] = peak + jnp.log2(total)
            out = dot(values[head * HEAD_DIM : (head + 1) * HEAD_DIM], soft.astype(bfloat))
            outs.append(out * (1.0 / total))
        mixed_ref[at : at + QUERY_STEP] = jnp.concatenate(outs, axis=0).T.astype(bfloat)


def attend(x, weights, biases, first, width):
    tokens, features = x.shape
    pairs = width // LANES
    start = first // width
    stride = weights.shape[1] // 3 // width
    weight = lambda i: pl.BlockSpec((features, width), lambda h: (0, i * stride + start))
    bias = lambda i: pl.BlockSpec((1, width), lambda h: (0, i * stride + start))
    full = pl.BlockSpec((tokens, width), lambda h: (0, 0))
    column = pl.BlockSpec((tokens, LANES), lambda h: (0, h))
    lows = jax.ShapeDtypeStruct((tokens, width), bfloat)
    return pl.pallas_call(
        attend_kernel,
        grid=(pairs,),
        in_specs=[pl.BlockSpec((tokens, features), lambda h: (0, 0))]
        + [weight(0), weight(1), weight(2), bias(0), bias(1)],
        out_specs=[full] * 3 + [column] + [pl.BlockSpec((1, 2, tokens), lambda h: (h, 0, 0))],
        out_shape=[lows] * 4 + [jax.ShapeDtypeStruct((pairs, 2, tokens), single)],
        compiler_params=params(60),
        cost_estimate=cost(
            6 * tokens * features * width + 16 * tokens * tokens * width,
            2 * tokens * features + 8 * tokens * width + 6 * features * width,
            2 * pairs * tokens * tokens,
        ),
        name="attend",
    )(x, weights, weights, weights, biases, biases)


def attend_back_kernel(others, *refs):
    q_ref, k_ref, v_ref, mixed_ref, grad_ref, log_ref = refs[:6]
    if others is None:
        dq_ref, dk_ref, dv_ref, dk_sum, dv_sum = refs[6:]
    else:
        sources = refs[6 : 7 + others]
        dq_ref, dk_ref, dv_ref, out_ref, dk_sum, dv_sum, own_grads = refs[7 + others : 14 + others]
        held = refs[14 + others : 15 + 2 * others]
        sems = refs[15 + 2 * others]
        copies = [
            pltpu.make_async_copy(source, kept, sems.at[n])
            for n, (source, kept) in enumerate(zip(sources, held))
        ]

        @pl.when(pl.program_id(0) == 0)
        def _():
            for c in copies:
                c.start()

    tokens = q_ref.shape[0]
    scale = 1.0 / math.sqrt(HEAD_DIM)
    base = math.log2(math.e) * scale
    keys = k_ref[...]
    values = v_ref[...]
    keys_turned = keys.T
    lane = lax.broadcasted_iota(jnp.int32, (QUERY_STEP_BACK, LANES), 1)
    for at in range(0, tokens, QUERY_STEP_BACK):
        rows = slice(at, at + QUERY_STEP_BACK)
        part = q_ref[rows]
        grad = grad_ref[rows]
        shares = (grad.astype(single) * mixed_ref[rows].astype(single)).T
        outs = []
        for head in range(LANES // HEAD_DIM):
            mine = lane // HEAD_DIM == head
            own = jnp.where(mine, part, jnp.zeros_like(part))
            own_grad = jnp.where(mine, grad, jnp.zeros_like(grad))
            share = jnp.sum(
                shares[head * HEAD_DIM : (head + 1) * HEAD_DIM], axis=0, keepdims=True
            )
            soft = jnp.exp2(dot_nt(keys, own) * base - log_ref[0, head : head + 1, rows])
            d_scores = (soft * (dot_nt(values, own_grad) - share)).astype(bfloat)
            dv_part = dot(soft.astype(bfloat), own_grad)
            dk_part = dot(d_scores, own)
            if at == 0 and head == 0:
                dv_sum[...] = dv_part
                dk_sum[...] = dk_part
            else:
                dv_sum[...] += dv_part
                dk_sum[...] += dk_part
            outs.append(dot(keys_turned[head * HEAD_DIM : (head + 1) * HEAD_DIM], d_scores))
        dq_ref[rows] = (jnp.concatenate(outs, axis=0) * scale).T.astype(bfloat)
    dk_ref[...] = (dk_sum[...] * scale).astype(bfloat)
    dv_ref[...] = dv_sum[...].astype(bfloat)
    if others is None:
        return
    pair = pl.ds(pl.multiple_of(pl.program_id(0) * LANES, LANES), LANES)
    for i, ref in enumerate((dq_ref, dk_ref, dv_ref)):
        own_grads[i, :, pair] = ref[...]

    @pl.when(pl.program_id(0) == pl.num_programs(0) - 1)
    def _():
        for c in copies:
            c.wait()
        weight = held[0]
        third = weight.shape[1] // 3
        piece = own_grads.shape[2]
        total = None
        for i in range(3):
            parts = [held[1 + 3 * c + i][...] for c in range(others // 3)] + [own_grads[i]]
            for c, part in enumerate(parts):
                at = i * third + c * piece
                term = dot_nt(part, weight[:, at : at + piece])
                total = term if total is None else total + term
        out_ref[...] = total.astype(bfloat)


def attend_back(q, k, v, mixed, grad, logs, weight=None, earlier=()):
    tokens, width = q.shape
    pairs = width // LANES
    column = pl.BlockSpec((tokens, LANES), lambda h: (0, h))
    lows = jax.ShapeDtypeStruct((tokens, width), bfloat)
    sums = [pltpu.VMEM((tokens, LANES), single)] * 2
    sources, outs, shapes, scratch = (), [], [], []
    if weight is not None:
        sources = (weight,) + tuple(earlier)
        outs = [pl.BlockSpec((tokens, weight.shape[0]), lambda h: (0, 0))]
        shapes = [jax.ShapeDtypeStruct((tokens, weight.shape[0]), bfloat)]
        scratch = (
            [pltpu.VMEM((3, tokens, width), bfloat)]
            + [pltpu.VMEM(a.shape, bfloat) for a in sources]
            + [pltpu.SemaphoreType.DMA((len(sources),))]
        )
    return pl.pallas_call(
        partial(attend_back_kernel, None if weight is None else len(earlier)),
        grid=(pairs,),
        in_specs=[column] * 5
        + [pl.BlockSpec((1, 2, tokens), lambda h: (h, 0, 0))]
        + [pl.BlockSpec(memory_space=pl.ANY)] * len(sources),
        out_specs=[column] * 3 + outs,
        out_shape=[lows] * 3 + shapes,
        scratch_shapes=sums + scratch,
        compiler_params=params(60),
        cost_estimate=cost(
            40 * tokens * tokens * width, 16 * tokens * width, 2 * pairs * tokens * tokens
        ),
        name="attend_back",
    )(q, k, v, mixed, grad, logs, *sources)


def input_grad_kernel(*refs):
    x_ref, other_ref = refs[0], refs[1]
    parts = refs[2:-2]
    out_ref, sums_ref = refs[-2:]
    count = len(parts) // 3
    tokens, piece = parts[0].shape
    third = count * piece
    turned = x_ref[...].T
    for c in range(count):
        for i in range(3):
            at = i * third + c * piece
            out_ref[:, at : at + piece] = dot(turned, parts[3 * c + i][...]).astype(bfloat)
    out_ref[:, 3 * third :] = other_ref[...]

    @pl.when(pl.program_id(0) == 0)
    def _():
        ones = jnp.ones((16, tokens), bfloat)
        for c in range(count):
            for i in (0, 2):
                total = dot(ones, parts[3 * c + i][...])
                sums_ref[:, i // 2 * third + c * piece : i // 2 * third + (c + 1) * piece] = total[:8]


def input_grad(x, other, parts):
    tokens, features = x.shape
    piece = parts[0].shape[1]
    third = piece * len(parts) // 3
    step = 256
    return pl.pallas_call(
        input_grad_kernel,
        grid=(features // step,),
        in_specs=[
            pl.BlockSpec((tokens, step), lambda t: (0, t)),
            pl.BlockSpec((step, other.shape[1]), lambda t: (t, 0)),
        ]
        + [pl.BlockSpec((tokens, piece), lambda t: (0, 0))] * len(parts),
        out_specs=[
            pl.BlockSpec((step, 3 * third + other.shape[1]), lambda t: (t, 0)),
            pl.BlockSpec((8, 2 * third), lambda t: (0, 0)),
        ],
        out_shape=[
            jax.ShapeDtypeStruct((features, 3 * third + other.shape[1]), bfloat),
            jax.ShapeDtypeStruct((8, 2 * third), single),
        ],
        compiler_params=params(60),
        cost_estimate=cost(6 * tokens * features * third, 2 * tokens * features * 5),
        name="input_grad",
    )(x, other, *parts)


def middle_kernel(
    parts, *refs
):
    mixed_refs = refs[:parts]
    weight_ref, bias_ref, x_ref, gate_ref, scale_ref, shift_ref = refs[parts : parts + 6]
    attended_ref, middle_ref, normed_ref, first_ref, last_ref, grouped = refs[parts + 6 :]
    rows, columns, features = x_ref.shape[1:]
    sub = columns // COLUMN_PARTS
    quarter = rows * columns // 4
    total = bias_ref[...]
    at = 0
    for ref in mixed_refs:
        width = ref.shape[-1]
        total = total + dot(ref[0].reshape(4 * quarter, width), weight_ref[at : at + width])
        at += width
    grouped[...] = total.reshape(4, quarter, features)
    gate = gate_ref[0]
    scale = 1.0 + scale_ref[0]
    shift = shift_ref[0]

    for pair in range(rows // 2):
        for a in range(2):
            row = pair * 2 + a
            for j in range(COLUMN_PARTS):
                line = slice(j * sub, (j + 1) * sub)
                cells = grouped[
                    2 * a + j % 2, pl.ds((pair * 2 + j // 2) * sub, sub)
                ]
                attended_ref[0, row, line] = cells
                middle = x_ref[0, row, line].astype(single) + gate * cells
                middle_ref[0, row, line] = middle
                low = (norm_parts(middle)[0] * scale + shift).astype(bfloat)
                normed_ref[0, row, line] = low
                if row < 2:
                    first_ref[0, row, line] = low
                if row >= rows - 2:
                    last_ref[0, row - rows + 2, line] = low


def middle_part(mixed, weight, bias, kept, gate, scale, shift):
    count, rows, columns, features = kept.shape
    quarter = rows * columns // 4
    image = pl.BlockSpec((1, rows, columns, features), lambda l: (l, 0, 0, 0))
    vector = pl.BlockSpec((1, 1, features), lambda l: (l, 0, 0))
    return pl.pallas_call(
        partial(middle_kernel, len(mixed)),
        grid=(count,),
        in_specs=[
            pl.BlockSpec((1, 4, quarter, m.shape[-1]), lambda l: (l, 0, 0, 0)) for m in mixed
        ]
        + [
            pl.BlockSpec((features, features), lambda l: (0, 0)),
            pl.BlockSpec((1, features), lambda l: (0, 0)),
            image, vector, vector, vector,
        ],
        out_specs=[image] * 3
        + [pl.BlockSpec((1, 2, columns, features), lambda l: (l, 0, 0, 0))] * 2,
        out_shape=[
            jax.ShapeDtypeStruct(kept.shape, single),
            jax.ShapeDtypeStruct(kept.shape, single),
            jax.ShapeDtypeStruct(kept.shape, bfloat),
        ]
        + [jax.ShapeDtypeStruct((count, 2, columns, features), bfloat)] * 2,
        scratch_shapes=[pltpu.VMEM((4, quarter, features), single)],
        compiler_params=params(60),
        cost_estimate=cost(2 * kept.size * features, 14 * kept.size),
        name="middle",
    )(*mixed, weight, bias, kept, gate, scale, shift)


def feed_upstream_kernel(db_ref, ws_ref, out_ref):
    out_ref[...] = dot_nt(db_ref[...], ws_ref[...]).astype(bfloat)


def feed_upstream(db, ws):
    count, tall, columns, features = db.shape
    hidden = ws.shape[0]
    lines = count * tall * columns
    return pl.pallas_call(
        feed_upstream_kernel,
        grid=(hidden // features,),
        in_specs=[
            pl.BlockSpec((lines, features), lambda s: (0, 0)),
            pl.BlockSpec((features, features), lambda s: (s, 0)),
        ],
        out_specs=pl.BlockSpec((lines, features), lambda s: (0, s)),
        out_shape=jax.ShapeDtypeStruct((lines, hidden), bfloat),
        compiler_params=params(60),
        cost_estimate=cost(2 * lines * features * hidden, 2 * lines * (features + hidden)),
        name="feed_upstream",
    )(db.reshape(lines, features), ws)


TURN_ROWS = 8


def feed_turn_kernel(parts, feeds, turns, *refs):
    (
        edge_ref, nb_ref, top_ref, bottom_ref, d_act_ref, we_ref, be_ref, taps_ref, bm_ref,
        middle_ref, attended_ref, g_ref, gate_b_ref, scale_ref, gate_a_ref, shrink_ref,
        ws_hbm, we_hbm, wo_hbm,
    ) = refs[:19]
    mixed_refs = refs[19 : 19 + parts]
    small_ref, act_hbm, d_hid_hbm, result_ref, d_middle_ref = refs[19 + parts : 24 + parts]
    d_mixed_refs = refs[24 + parts : 24 + 2 * parts]
    (
        gw_ref, sums_ref,
        nb_wide, hidden, wide, d_wide, act_s, d_hid_s, ws, we, wo, gw_sum, grouped, branch_s, e_s, sums,
        weight_sem, act_sem, d_hid_sem,
    ) = refs[24 + 2 * parts :]
    step = pl.program_id(0)
    columns, features = nb_ref.shape[2:]
    sub = columns // COLUMN_PARTS
    weights = (
        pltpu.make_async_copy(ws_hbm, ws, weight_sem.at[0]),
        pltpu.make_async_copy(we_hbm, we, weight_sem.at[1]),
        pltpu.make_async_copy(wo_hbm, wo, weight_sem.at[2]),
    )

    def out_copies(n):
        at = pl.ds(pl.multiple_of(n * features, features), features)
        return (
            pltpu.make_async_copy(act_s.at[:, at], act_hbm.at[:, at], act_sem.at[n]),
            pltpu.make_async_copy(d_hid_s.at[:, at], d_hid_hbm.at[:, at], d_hid_sem.at[n]),
        )

    @pl.when(step == 0)
    def _():
        count, rows = nb_ref.shape[:2]
        own = rows * columns
        tall = (rows + 4) * columns
        for c in weights:
            c.start()
        for l in range(count):
            nb_wide[l * tall : l * tall + 2 * columns] = top_ref[l].reshape(2 * columns, features)
            nb_wide[l * tall + 2 * columns : (l + 1) * tall - 2 * columns] = nb_ref[l].reshape(
                own, features
            )
            nb_wide[(l + 1) * tall - 2 * columns : (l + 1) * tall] = bottom_ref[l].reshape(
                2 * columns, features
            )

    @pl.when(step < feeds)
    def _():
        feed_step(
            step, edge_ref, d_act_ref, we_ref, be_ref, taps_ref, bm_ref, small_ref,
            nb_wide, hidden, wide, d_wide, act_s, d_hid_s, nb_ref.shape,
        )
        for c in out_copies(step):
            c.start()

    @pl.when(step == feeds)
    def _():
        for c in weights:
            c.wait()

    @pl.when(step >= feeds)
    def _():
        turn_step(
            step, feeds, turns, middle_ref, attended_ref, g_ref, gate_b_ref, scale_ref, gate_a_ref,
            shrink_ref, mixed_refs, result_ref, d_middle_ref, d_mixed_refs, gw_ref, sums_ref,
            act_s, d_hid_s, ws, we, wo, gw_sum, grouped, branch_s, e_s, sums,
        )

    @pl.when(step == pl.num_programs(0) - 1)
    def _():
        for n in range(feeds):
            for c in out_copies(n):
                c.wait()


def feed_step(
    step, edge_ref, d_act_ref, we_ref, be_ref, taps_ref, bm_ref, small_ref,
    nb_wide, hidden, wide, d_wide, act_s, d_hid_s, shape,
):
    count, rows, columns, features = shape
    sub = columns // COLUMN_PARTS
    block = we_ref.shape[1]
    own = rows * columns
    tall = (rows + 4) * columns
    mid = (rows + 2) * columns
    hidden[...] = (dot(nb_wide[...], we_ref[...]) + be_ref[...]).astype(bfloat)
    small_ref[...] = jnp.zeros_like(small_ref)

    c0 = math.sqrt(2.0 / math.pi)
    c1 = c0 * 0.044715

    @pl.loop(0, count * (block // LANES))
    def _(index):
        l = index // (block // LANES)
        at = pl.ds(pl.multiple_of((index % (block // LANES)) * LANES, LANES), LANES)
        out = pl.ds(
            pl.multiple_of(step * block + index % (block // LANES) * LANES, LANES), LANES
        )
        taps = [taps_ref[t : t + 1, at] for t in range(9)]
        bias = bm_ref[:, at]
        for row in range(rows + 4):
            cells = hidden[pl.ds(pl.multiple_of(l * tall + row * columns, columns), columns), at]
            if row < 2:
                cells = cells * edge_ref[0].astype(bfloat)
            if row >= rows + 2:
                cells = cells * edge_ref[1].astype(bfloat)
            put_wide(wide, row, cells.reshape(COLUMN_PARTS, sub, LANES))
        taps = [(t + jnp.zeros((sub, LANES), single)).astype(bfloat) for t in taps]
        for row in range(rows + 2):
            v = conv_low(wide, row, taps).astype(single) + bias
            cube = (v * v) * c1
            half = 0.5 * jnp.tanh(v * (cube + c0)) + 0.5
            gelu = v * half
            slope = half + gelu * (1.0 - half) * (6.0 * cube + 2.0 * c0)
            if 1 <= row <= rows:
                act_s[
                    pl.ds(pl.multiple_of(l * own + (row - 1) * columns, columns), columns), out
                ] = gelu.reshape(columns, LANES).astype(bfloat)
            grad = d_act_ref[pl.ds(pl.multiple_of(l * mid + row * columns, columns), columns), at]
            grad = grad.astype(single).reshape(COLUMN_PARTS, sub, LANES) * slope
            put_wide(d_wide, row, grad.astype(bfloat))
        sums = [jnp.zeros((sub, LANES), single) for _ in range(11)]
        for row in range(rows):
            d_in = conv_back_row(d_wide, row, taps).astype(bfloat)
            d_hid_s[pl.ds(pl.multiple_of(l * own + row * columns, columns), columns), out] = (
                d_in.reshape(columns, LANES)
            )
            center = d_wide[row + 1, 1 : COLUMN_PARTS + 1]
            for i in range(3):
                for j in range(3):
                    term = center * wide[row + 1 + i, j : j + COLUMN_PARTS]
                    term = (term[0] + term[1]) + (term[2] + term[3])
                    sums[3 * i + j] += term.astype(single)
            sums[9] += jnp.sum(center.astype(single), axis=0)
            sums[10] += jnp.sum(d_in.astype(single), axis=0)
        for t in range(11):
            small_ref[t : t + 1, at] += jnp.sum(sums[t], axis=0, keepdims=True)


def turn_step(
    step, feeds, turns, middle_ref, attended_ref, g_ref, gate_b_ref, scale_ref, gate_a_ref,
    shrink_ref, mixed_refs, result_ref, d_middle_ref, d_mixed_refs, gw_ref, sums_ref,
    act_s, d_hid_s, ws, we, wo, gw_sum, grouped, branch_s, e_s, sums,
):
    columns, features = g_ref.shape[2:]
    sub = columns // COLUMN_PARTS
    rows = g_ref.shape[1]
    quarter = rows * columns // 4
    back = column_order(columns, True)
    gate_b = gate_b_ref[0]
    scale = 1.0 + scale_ref[0]
    gate_a = gate_a_ref[0]
    piece_of = step - feeds
    lines = pl.ds(pl.multiple_of(piece_of * rows * columns, rows * columns), rows * columns)

    branch_s[...] = dot(act_s[lines], ws[...]) + shrink_ref[...]
    e_s[...] = dot_nt(d_hid_s[lines], we[...])

    @pl.when(piece_of % turns == 0)
    def _():
        sums[...] = jnp.zeros_like(sums)

    for pair in range(rows // 2):
        for a in range(2):
            row = pair * 2 + a
            lows = []
            for j in range(COLUMN_PARTS):
                line = slice(j * sub, (j + 1) * sub)
                at = pl.ds(row * columns + j * sub, sub)
                branch = branch_s[at]
                middle = middle_ref[0, row, line]
                g = g_ref[0, row, line].astype(single)
                lows.append((middle + gate_b * branch).astype(bfloat))
                normed, inverse = norm_parts(middle)
                e = e_s[at]
                d_middle = g + norm_back(normed, inverse, e * scale)
                d_middle_ref[0, row, line] = d_middle
                low = (d_middle * gate_a).astype(bfloat)
                grouped[
                    2 * a + j % 2, pl.ds((pair * 2 + j // 2) * sub, sub)
                ] = low
                terms = (
                    g * branch, e, e * normed, d_middle * attended_ref[0, row, line], low.astype(single)
                )
                for t, term in enumerate(terms):
                    sums[t] += jnp.sum(term.reshape(sub // 8, 8, features), axis=0)
            result_ref[0, row] = dot(back, jnp.concatenate(lows, axis=0)).astype(bfloat)

    for t in range(5):
        sums_ref[0, t : t + 1] = jnp.sum(sums[t], axis=0, keepdims=True)
    sums_ref[0, 5:8] = jnp.zeros((3, features), single)
    grad = grouped[...].reshape(4 * quarter, features)
    at = 0
    for mixed_ref, d_ref in zip(mixed_refs, d_mixed_refs):
        width = mixed_ref.shape[-1]
        piece = slice(at, at + width)
        d_ref[0] = dot_nt(grad, wo[piece]).astype(bfloat).reshape(4, quarter, width)
        part = dot_tn(mixed_ref[0].reshape(4 * quarter, width), grad)

        @pl.when(piece_of == 0)
        def _():
            gw_sum[piece] = part

        @pl.when(piece_of > 0)
        def _():
            gw_sum[piece] += part

        at += width

    @pl.when(step == pl.num_programs(0) - 1)
    def _():
        gw_ref[...] = gw_sum[...].astype(bfloat)


def feed_turn(
    edge, nb, top, bottom, d_act, we, be, taps, bm, ws, middle, attended, g, gate_b, scale, gate_a,
    shrink_bias, wo, mixed,
):
    count, rows, columns, features = nb.shape
    hidden = we.shape[1]
    block = features
    feeds = hidden // block
    tokens = count * rows * columns
    tall = count * (rows + 4) * columns
    mid = count * (rows + 2) * columns
    sub = columns // COLUMN_PARTS
    some = min(TURN_ROWS, rows)
    turns = rows // some
    quarter = some * columns // 4
    whole = lambda a: pl.BlockSpec(a.shape, lambda s: (0,) * a.ndim)
    feed = lambda s: jnp.minimum(s, feeds - 1)
    place = lambda s: jnp.maximum(s - feeds, 0)
    column = lambda n: pl.BlockSpec((n, block), lambda s: (0, feed(s)))
    image = pl.BlockSpec(
        (1, some, columns, features), lambda s: (place(s) // turns, place(s) % turns, 0, 0)
    )
    vector = pl.BlockSpec((1, 1, features), lambda s: (place(s) // turns, 0, 0))
    groups = [
        pl.BlockSpec(
            (1, 4, quarter, m.shape[-1]), lambda s: (place(s) // turns, 0, place(s) % turns, 0)
        )
        for m in mixed
    ]
    hbm = pl.BlockSpec(memory_space=pl.ANY)
    return pl.pallas_call(
        partial(feed_turn_kernel, len(mixed), feeds, turns),
        grid=(feeds + count * turns,),
        in_specs=[
            pl.BlockSpec(memory_space=pltpu.SMEM),
            whole(nb), whole(top), whole(bottom),
            column(mid), column(features), column(1), column(16), column(1),
            image, image, image, vector, vector, vector, whole(shrink_bias), hbm, hbm, hbm,
        ]
        + groups,
        out_specs=[column(16), hbm, hbm, image, image]
        + groups
        + [
            pl.BlockSpec((features, features), lambda s: (0, 0)),
            pl.BlockSpec((1, 8, features), lambda s: (place(s) // turns, 0, 0)),
        ],
        out_shape=[
            jax.ShapeDtypeStruct((16, hidden), single),
            jax.ShapeDtypeStruct((tokens, hidden), bfloat),
            jax.ShapeDtypeStruct((tokens, hidden), bfloat),
            jax.ShapeDtypeStruct(g.shape, bfloat),
            jax.ShapeDtypeStruct(g.shape, single),
        ]
        + [jax.ShapeDtypeStruct(m.shape, bfloat) for m in mixed]
        + [
            jax.ShapeDtypeStruct((features, features), bfloat),
            jax.ShapeDtypeStruct((count, 8, features), single),
        ],
        scratch_shapes=[
            pltpu.VMEM((tall, features), bfloat),
            pltpu.VMEM((tall, block), bfloat),
            pltpu.VMEM((rows + 4, COLUMN_PARTS + 2, sub, LANES), bfloat),
            pltpu.VMEM((rows + 2, COLUMN_PARTS + 2, sub, LANES), bfloat),
            pltpu.VMEM((tokens, hidden), bfloat),
            pltpu.VMEM((tokens, hidden), bfloat),
            pltpu.VMEM((hidden, features), bfloat),
            pltpu.VMEM((features, hidden), bfloat),
            pltpu.VMEM((features, features), bfloat),
            pltpu.VMEM((features, features), single),
            pltpu.VMEM((4, quarter, features), bfloat),
            pltpu.VMEM((some * columns, features), single),
            pltpu.VMEM((some * columns, features), single),
            pltpu.VMEM((5, 8, features), single),
            pltpu.SemaphoreType.DMA((3,)),
            pltpu.SemaphoreType.DMA((feeds,)),
            pltpu.SemaphoreType.DMA((feeds,)),
        ],
        compiler_params=params(62),
        cost_estimate=cost(
            2 * features * hidden * (tall + 2 * tokens) + 4 * g.size * features,
            30 * g.size + 8 * features * hidden + 6 * tokens * hidden,
            mid * hidden,
        ),
        name="feed_turn",
    )(
        edge, nb, top, bottom, d_act, we, be, taps, bm, middle, attended, g, gate_b, scale, gate_a,
        shrink_bias, ws, we, wo, *mixed,
    )


def feed_grads_kernel(
    act_ref, d_hid_ref, nb_ref, db_ref, out_ref, db_own, shrink_s, expand_s, shrink_sem, expand_sem
):
    count, rows, columns, features = nb_ref.shape
    own = rows * columns
    step = pl.program_id(0)
    steps = pl.num_programs(0)
    some, slots, unit = shrink_s.shape[:3]

    @pl.when(step == 0)
    def _():
        for l in range(count):
            db_own[l * own : (l + 1) * own] = db_ref[l, 1 : rows + 1].reshape(own, features)

    def copies(s):
        return (
            pltpu.make_async_copy(
                shrink_s, out_ref.at[pl.ds(s * some, some), pl.ds(0, slots)], shrink_sem
            ),
            pltpu.make_async_copy(expand_s, out_ref.at[:, slots + s], expand_sem),
        )

    shrink = dot_tn(act_ref[...], db_own[...])
    expand = dot_tn(nb_ref[...].reshape(count * own, features), d_hid_ref[...])

    @pl.when(step > 0)
    def _():
        for c in copies(step - 1):
            c.wait()

    shrink_s[...] = shrink.reshape(shrink_s.shape).astype(bfloat)
    expand_s[...] = expand.reshape(expand_s.shape).astype(bfloat)
    for c in copies(step):
        c.start()

    @pl.when(step == steps - 1)
    def _():
        for c in copies(step):
            c.wait()


def feed_grads(act, d_hid, nb, db, devices):
    count, rows, columns, features = nb.shape
    tokens, hidden = act.shape
    block = features
    steps = hidden // block
    unit = features // devices
    if unit % 8:
        shrink = dot_tn(act, db[:, 1:-1].reshape(tokens, features))
        expand = dot_tn(nb.reshape(tokens, features), d_hid)
        return jnp.concatenate(
            [
                shrink.reshape(devices, steps, unit, features),
                expand.reshape(devices, unit, steps, features).transpose(0, 2, 1, 3),
            ],
            axis=1,
        ).astype(bfloat)
    whole = lambda a: pl.BlockSpec(a.shape, lambda s: (0,) * a.ndim)
    return pl.pallas_call(
        feed_grads_kernel,
        grid=(steps,),
        in_specs=[
            pl.BlockSpec((tokens, block), lambda s: (0, s)),
            pl.BlockSpec((tokens, block), lambda s: (0, s)),
            whole(nb), whole(db),
        ],
        out_specs=pl.BlockSpec(memory_space=pl.ANY),
        out_shape=jax.ShapeDtypeStruct((devices, 2 * steps, unit, features), bfloat),
        scratch_shapes=[
            pltpu.VMEM((tokens, features), bfloat),
            pltpu.VMEM((devices // steps, steps, unit, features), bfloat),
            pltpu.VMEM((devices, unit, features), bfloat),
            pltpu.SemaphoreType.DMA,
            pltpu.SemaphoreType.DMA,
        ],
        compiler_params=params(60),
        cost_estimate=cost(4 * features * hidden * tokens, 8 * features * hidden + 4 * tokens * hidden),
        name="feed_grads",
    )(act, d_hid, nb, db)


def final_kernel(
    d_ref, top_ref, bottom_ref, normed_ref, x_ref, d_middle_ref, scale_ref, taps_ref,
    out_ref, taps_out_ref, sums_ref, wide, d_wide,
):
    rows, columns, features = x_ref.shape[1:]
    sub = columns // COLUMN_PARTS
    back = column_order(columns, True)
    scale = 1.0 + scale_ref[0]

    def piece(ref, a, start):
        parts = [
            ref[0, 2 * a + j % 2, pl.ds(pl.multiple_of(start + (j // 2) * sub, sub), sub)]
            for j in range(COLUMN_PARTS)
        ]
        return jnp.stack(parts, axis=0).astype(single)

    def halo(ref):
        parts = [
            ref[0, j % 2, pl.ds((j // 2) * sub, sub)] for j in range(COLUMN_PARTS)
        ]
        return jnp.stack(parts, axis=0).astype(single)

    put_wide(d_wide, 0, halo(top_ref))
    put_wide(d_wide, rows + 1, halo(bottom_ref))

    @pl.loop(0, rows // 2)
    def _(pair):
        for a in range(2):
            put_wide(d_wide, pair * 2 + a + 1, piece(d_ref, a, pair * 2 * sub))

    @pl.loop(0, rows + 2)
    def _(row):
        for j in range(COLUMN_PARTS):
            put_part(wide, row, j, normed_ref[0, row, j * sub : (j + 1) * sub].astype(single))

    @pl.when(pl.program_id(0) == 0)
    def _():
        taps_out_ref[...] = jnp.zeros_like(taps_out_ref)

    d_normed = wide
    for lane in range(0, features, LANES):
        at = pl.ds(lane, LANES)
        taps = [taps_ref[t : t + 1, at] for t in range(9)]

        def step(row, sums):
            total = None
            center = d_wide[row + 1, 1 : COLUMN_PARTS + 1, :, at]
            sums = list(sums)
            for i in range(3):
                for j in range(3):
                    term = taps[3 * i + j] * d_wide[row + 2 - i, 2 - j : 2 - j + COLUMN_PARTS, :, at]
                    total = term if total is None else total + term
                    sums[3 * i + j] = sums[3 * i + j] + jnp.sum(
                        center * wide[row + i, j : j + COLUMN_PARTS, :, at], axis=0
                    )
            sums[9] = sums[9] + jnp.sum(center, axis=0)
            d_normed[row, 1 : COLUMN_PARTS + 1, :, at] = total
            return tuple(sums)

        sums = lax.fori_loop(
            0, rows, step, tuple(jnp.zeros((sub, LANES), single) for _ in range(10))
        )
        for t in range(10):
            taps_out_ref[t : t + 1, at] += jnp.sum(sums[t], axis=0, keepdims=True)

    def last(row, sums):
        lows = []
        for j in range(COLUMN_PARTS):
            line = slice(j * sub, (j + 1) * sub)
            cells = d_normed[row, j + 1]
            normed, inverse = norm_parts(x_ref[0, row, line].astype(single))
            grad = d_middle_ref[0, row, line] + norm_back(normed, inverse, cells * scale)
            lows.append(grad.astype(bfloat))
            sums = tuple(
                s + jnp.sum(t.reshape(sub // 8, 8, features), axis=0)
                for s, t in zip(sums, (cells, cells * normed))
            )
        out_ref[0, row] = dot(back, jnp.concatenate(lows, axis=0)).astype(bfloat)
        return sums

    sums = tuple(jnp.zeros((8, features), single) for _ in range(2))
    for row in range(rows):
        sums = last(row, sums)
    for t in range(2):
        sums_ref[0, t : t + 1] = jnp.sum(sums[t], axis=0, keepdims=True)
    sums_ref[0, 2:8] = jnp.zeros((6, features), single)


def final(d_reduced, top, bottom, normed, kept, d_middle, scale, taps):
    count, rows, columns, features = kept.shape
    quarter = rows * columns // 4
    sub = columns // COLUMN_PARTS
    image = lambda r: pl.BlockSpec((1, r, columns, features), lambda l: (l, 0, 0, 0))
    vector = pl.BlockSpec((1, 1, features), lambda l: (l, 0, 0))
    side = pl.BlockSpec((1, 2, 2 * sub, features), lambda l: (l, 0, 0, 0))
    return pl.pallas_call(
        final_kernel,
        grid=(count,),
        in_specs=[
            pl.BlockSpec((1, 4, quarter, features), lambda l: (l, 0, 0, 0)),
            side, side, image(rows + 2), image(rows), image(rows), vector,
            pl.BlockSpec((16, features), lambda l: (0, 0)),
        ],
        out_specs=[
            image(rows),
            pl.BlockSpec((16, features), lambda l: (0, 0)),
            pl.BlockSpec((1, 8, features), lambda l: (l, 0, 0)),
        ],
        out_shape=[
            jax.ShapeDtypeStruct(kept.shape, bfloat),
            jax.ShapeDtypeStruct((16, features), single),
            jax.ShapeDtypeStruct((count, 8, features), single),
        ],
        scratch_shapes=[pltpu.VMEM((rows + 2, COLUMN_PARTS + 2, sub, features), single)] * 2,
        compiler_params=params(60),
        cost_estimate=cost(kept.size * 180, kept.size * 12),
        name="final",
    )(d_reduced, top, bottom, normed, kept, d_middle, scale, taps)


def from_above(tail):
    count = lax.axis_size("strips")
    return lax.ppermute(tail, "strips", [(i, i + 1) for i in range(count - 1)])


def from_below(head):
    count = lax.axis_size("strips")
    return lax.ppermute(head, "strips", [(i + 1, i) for i in range(count - 1)])


def time_features(timesteps, halves):
    frequency = jnp.exp(-math.log(10000.0) * jnp.arange(halves, dtype=jnp.float32) / halves)
    phase = timesteps.astype(jnp.float32)[:, None] * frequency[None, :]
    return jnp.concatenate([jnp.cos(phase), jnp.sin(phase)], axis=1)


def thirds(value):
    high = value.astype(bfloat)
    rest = value - high.astype(single)
    middle = rest.astype(bfloat)
    low = (rest - middle.astype(single)).astype(bfloat)
    return jnp.concatenate([high, middle, low], axis=0)


def exact(value, weight, nt=False):
    n = value.shape[0]
    out = (dot_nt if nt else dot)(thirds(value), weight)
    return out[:n] + out[n : 2 * n] + out[2 * n :]


def silu(value):
    return value * (1.0 / (1.0 + jnp.exp(-value)))


def silu_slope(value):
    gate = 1.0 / (1.0 + jnp.exp(-value))
    return gate * (1.0 + value * (1.0 - gate))


def label_rows(labels, classes):
    return (lax.broadcasted_iota(jnp.int32, (labels.shape[0], classes), 1) == labels).astype(bfloat)


def condition(sinus, labels, wi_ref, bi_ref, wo_ref, bo_ref, table_ref):
    before = exact(sinus, wi_ref[...]) + bi_ref[...]
    inner = silu(before)
    onehot = label_rows(labels, table_ref.shape[1])
    cond = exact(inner, wo_ref[...]) + bo_ref[...] + dot_nt(onehot, table_ref[...])
    return before, inner, cond


def modulate_kernel(
    sinus_ref, label_ref, wi_ref, bi_ref, wo_ref, bo_ref, table_ref, ada_ref, ab_ref, out_ref, active
):
    @pl.when(pl.program_id(0) == 0)
    def _():
        cond = condition(
            sinus_ref[...], label_ref[...], wi_ref, bi_ref, wo_ref, bo_ref, table_ref
        )[2]
        active[...] = silu(cond)

    out_ref[0] = exact(active[...], ada_ref[...]) + ab_ref[...]


def modulate(sinus, labels, weights, ada, ada_bias):
    n = sinus.shape[0]
    features = ada.shape[0]
    whole = lambda a: pl.BlockSpec(a.shape, lambda s: (0,) * a.ndim)
    return pl.pallas_call(
        modulate_kernel,
        grid=(6,),
        in_specs=[whole(a) for a in (sinus, labels) + weights]
        + [
            pl.BlockSpec((features, features), lambda s: (0, s)),
            pl.BlockSpec((1, features), lambda s: (0, s)),
        ],
        out_specs=pl.BlockSpec((1, n, features), lambda s: (s, 0, 0)),
        out_shape=jax.ShapeDtypeStruct((6, n, features), single),
        scratch_shapes=[pltpu.VMEM((n, features), single)],
        compiler_params=params(16),
        cost_estimate=cost(50 * n * ada.size, 2 * ada.size),
        name="modulate",
    )(sinus, labels, *weights, ada, ada_bias)


def own_rows(me_ref, value, size):
    width = value.shape[1]
    place = lax.broadcasted_iota(jnp.int32, (size, width), 1)
    line = lax.broadcasted_iota(jnp.int32, (size, width), 0)
    pick = (place == me_ref[0] * size + line).astype(single)
    return lax.dot_general(
        pick, value, (((1,), (1,)), ((), ())), precision=highest, preferred_element_type=single
    )


def exact_small(a, b):
    return lax.dot_general(
        a, b, (((1,), (0,)), ((), ())), precision=highest, preferred_element_type=single
    )


def strip_sum(ref, kinds, count, features):
    lines = []
    for item in range(ref.shape[0]):
        for l in range(count):
            at = l * kinds * features
            lines.append(jnp.sum(
                    ref[item, :, at : at + kinds * features].astype(single), axis=0, keepdims=True
                ))
    return jnp.concatenate(lines, axis=0)


def early_kernel(
    count, me_ref, parts_ref, sinus_ref, label_ref, wi_ref, bi_ref, wo_ref, bo_ref, table_ref, ada_ref,
    before_ref, cond_ref, d_active_ref, ada_out_ref, d_mod_ref,
):
    features = ada_ref.shape[0]
    d_mod = strip_sum(parts_ref, 4, count, features)
    before, _, cond = condition(
        sinus_ref[...], label_ref[...], wi_ref, bi_ref, wo_ref, bo_ref, table_ref
    )
    before_ref[...] = before
    cond_ref[...] = cond
    d_active_ref[...] = exact(d_mod, ada_ref[:, 2 * features :], nt=True)
    size = ada_out_ref.shape[0]
    ada_out_ref[...] = exact_small(own_rows(me_ref, silu(cond), size), d_mod)
    d_mod_ref[...] = jnp.sum(d_mod, axis=0, keepdims=True)


def early_condition(me, parts, count, sinus, labels, weights, ada, size):
    n = sinus.shape[0]
    features = ada.shape[0]
    whole = lambda a: pl.BlockSpec(a.shape, lambda s: (0,) * a.ndim)
    shapes = [
        jax.ShapeDtypeStruct((n, features), single),
        jax.ShapeDtypeStruct((n, features), single),
        jax.ShapeDtypeStruct((n, features), single),
        jax.ShapeDtypeStruct((size, 4 * features), single),
        jax.ShapeDtypeStruct((1, 4 * features), single),
    ]
    return pl.pallas_call(
        partial(early_kernel, count),
        grid=(1,),
        in_specs=[pl.BlockSpec(memory_space=pltpu.SMEM)]
        + [whole(a) for a in (parts, sinus, labels) + weights + (ada,)],
        out_specs=[whole(a) for a in shapes],
        out_shape=shapes,
        compiler_params=params(28),
        cost_estimate=cost(50 * n * ada.size, 2 * ada.size),
        name="early_condition",
    )(me, parts, sinus, labels, *weights, ada)


def late_kernel(
    count, me_ref, parts_ref, before_ref, cond_ref, d_active_ref, ada_early_ref, d_mod_early_ref,
    sinus_ref, label_ref, wo_ref, ada_ref,
    ada_out_ref, d_mod_ref, table_out_ref, wo_out_ref, wi_out_ref, d_cond_ref, d_before_ref,
):
    features = wo_ref.shape[0]
    before = before_ref[...]
    cond = cond_ref[...]
    d_mod = strip_sum(parts_ref, 2, count, features)
    d_active = d_active_ref[...] + exact(d_mod, ada_ref[...], nt=True)
    d_cond = d_active * silu_slope(cond)
    d_before = exact(d_cond, wo_ref[...], nt=True) * silu_slope(before)
    size = ada_out_ref.shape[0]
    ada_out_ref[:, : 2 * features] = exact_small(own_rows(me_ref, silu(cond), size), d_mod)
    ada_out_ref[:, 2 * features :] = ada_early_ref[...]
    d_mod_ref[:, : 2 * features] = jnp.sum(d_mod, axis=0, keepdims=True)
    d_mod_ref[:, 2 * features :] = d_mod_early_ref[...]
    onehot = label_rows(label_ref[...], table_out_ref.shape[1]).astype(single)
    table_out_ref[...] = exact_small(own_rows(me_ref, d_cond, size), onehot)
    wo_out_ref[...] = exact_small(own_rows(me_ref, silu(before), size), d_cond)
    wi_out_ref[...] = exact_small(
        own_rows(me_ref, sinus_ref[...], wi_out_ref.shape[0]), d_before
    )
    d_cond_ref[...] = jnp.sum(d_cond, axis=0, keepdims=True)
    d_before_ref[...] = jnp.sum(d_before, axis=0, keepdims=True)


def late_condition(
    me, parts, count, before, cond, d_active, ada_early, d_mod_early, sinus, labels, wo, ada, classes,
    devices,
):
    features = ada.shape[0]
    size = features // devices
    whole = lambda a: pl.BlockSpec(a.shape, lambda s: (0,) * a.ndim)
    shapes = [
        jax.ShapeDtypeStruct((size, 6 * features), single),
        jax.ShapeDtypeStruct((1, 6 * features), single),
        jax.ShapeDtypeStruct((size, classes), single),
        jax.ShapeDtypeStruct((size, features), single),
        jax.ShapeDtypeStruct((sinus.shape[1] // devices, features), single),
        jax.ShapeDtypeStruct((1, features), single),
        jax.ShapeDtypeStruct((1, features), single),
    ]
    return pl.pallas_call(
        partial(late_kernel, count),
        grid=(1,),
        in_specs=[pl.BlockSpec(memory_space=pltpu.SMEM)]
        + [
            whole(a)
            for a in (parts, before, cond, d_active, ada_early, d_mod_early, sinus, labels, wo)
        ]
        + [pl.BlockSpec((features, 2 * features), lambda s: (0, 0))],
        out_specs=[whole(a) for a in shapes],
        out_shape=shapes,
        compiler_params=params(16),
        cost_estimate=cost(20 * ada.size, ada.size),
        name="late_condition",
    )(me, parts, before, cond, d_active, ada_early, d_mod_early, sinus, labels, wo, ada)


def sum_cores(keep, give):
    strips = lax.axis_size("strips")
    got = lax.ppermute(give, "strips", [(i, i ^ 1) for i in range(strips)])
    return (keep.astype(single) + got.astype(single)).astype(bfloat)


def sum_axis(part, axis, size, place, step):
    pick = lambda k: lax.dynamic_index_in_dim(part, place ^ k, 0, keepdims=False)
    count = lax.axis_size(axis)
    got = [
        lax.ppermute(pick(k), axis, [(i, i ^ (k * step)) for i in range(count)])
        for k in range(1, size)
    ]
    total = pick(0).astype(single)
    for g in got:
        total = total + g.astype(single)
    return total


def sum_items(part):
    return sum_axis(part, "items", lax.axis_size("items"), lax.axis_index("items"), 1).astype(bfloat)


def sum_strips(part):
    strip = lax.axis_index("strips")
    return sum_axis(part, "strips", lax.axis_size("strips") // 2, strip // 2, 2)


def after(value, *others):
    return lax.optimization_barrier((value,) + others)[0]


def tap_rows(kernel):
    return jnp.pad(kernel.astype(single).T, ((0, 7), (0, 0)))


def per_device(
    latents,
    timesteps,
    labels,
    time_in_weight,
    time_in_bias,
    time_out_weight,
    time_out_bias,
    label_table,
    ada_weight,
    ada_bias,
    down_kernel,
    down_bias,
    input_weight,
    query_bias,
    value_bias,
    output_weight,
    output_bias,
    expand_weight,
    expand_bias,
    mixer_kernel,
    mixer_bias,
    shrink_weight,
    shrink_bias,
    cotangent,
):
    count, rows, columns, features = latents.shape
    strips = lax.axis_size("strips")
    items = lax.axis_size("items")
    devices = strips * items
    strip = lax.axis_index("strips")
    item = lax.axis_index("items")
    me = item * strips + strip
    sub = columns // COLUMN_PARTS
    quarter = rows * columns // 4
    groups = count * 4
    share = strips // groups
    width = features // share
    row_vector = lambda v: v.astype(single).reshape(1, -1)
    edge = jnp.stack([strip > 0, strip < strips - 1]).astype(single)

    lines = -(-count // 8) * 8
    weights = (
        time_in_weight, row_vector(time_in_bias), time_out_weight, row_vector(time_out_bias),
        label_table,
    )
    waves = time_in_weight.shape[0] // 2
    modulation = modulate(
        time_features(jnp.pad(timesteps, (0, lines - count)), waves),
        jnp.pad(labels, (0, lines - count))[:, None],
        weights,
        ada_weight,
        row_vector(ada_bias),
    )
    shift_a, scale_a, gate_a, shift_b, scale_b, gate_b = (
        modulation[i, :count, None, :] for i in range(6)
    )

    ends = jnp.concatenate([latents[:, -1:], cotangent[:, -1:]], axis=1)
    starts = jnp.concatenate([latents[:, :1], cotangent[:, :1]], axis=1)
    above = from_above(ends)
    below = from_below(starts)

    down_taps = tap_rows(down_kernel)
    grouped, normed_a, kept = front(
        edge, latents, above[:, :1], below[:, :1], scale_a, shift_a, down_taps, row_vector(down_bias)
    )

    def spread(array):
        flat = array.reshape(groups, quarter, array.shape[-1])
        if share > 1:
            flat = jnp.repeat(flat, share, axis=0)
        got = lax.all_to_all(flat, "strips", 0, 0, tiled=True)
        return got.reshape(strips * quarter, array.shape[-1])

    def collect(array):
        flat = array.reshape(strips, quarter, array.shape[-1])
        return lax.all_to_all(flat, "strips", 0, 0, tiled=True)

    group = spread(grouped)
    g_kept, d_branch, grad_shrink_bias = upstream_parts(
        cotangent, above[:, 1:], below[:, 1:], gate_b
    )

    head_at = (strip % share) * width
    def own_columns(array, axis):
        return array if share == 1 else lax.dynamic_slice_in_dim(array, head_at, width, axis=axis)

    own_weight = jnp.concatenate(
        [own_columns(input_weight[:, i * features : (i + 1) * features], 1) for i in range(3)], axis=1
    ) if share > 1 else input_weight
    own_bias = jnp.concatenate(
        [own_columns(row_vector(b), 1) for b in (query_bias, value_bias)], axis=1
    )
    chunks = next(c for c in CHUNKS if width // LANES % c == 0)
    piece = width // chunks
    saved = []
    mixed = []
    d_act = feed_upstream(d_branch, shrink_weight)
    group, d_act, expand_line, mixer_taps, mixer_line, output_line, shrink_line = (
        lax.optimization_barrier(
            (
                group,
                d_act,
                row_vector(expand_bias),
                tap_rows(mixer_kernel),
                row_vector(mixer_bias),
                row_vector(output_bias),
                row_vector(shrink_bias),
            )
        )
    )
    for c in range(chunks):
        saved.append(attend(group, own_weight, own_bias, c * piece, piece))
        mixed.append(collect(saved[c][3]))
    if share == 1:
        mixed = [m.reshape(count, 4, quarter, piece) for m in mixed]
    else:
        joined = jnp.concatenate(mixed, axis=-1).reshape(groups, share, quarter, width)
        joined = joined.transpose(0, 2, 1, 3).reshape(count, 4, quarter, features)
        mixed = [joined]

    attended, middle, normed_b, first_rows, last_rows = middle_part(
        mixed, output_weight, output_line, kept, gate_a, scale_b, shift_b
    )
    feed_small, act, d_hid, *turned = feed_turn(
        edge,
        normed_b,
        from_above(last_rows),
        from_below(first_rows),
        d_act,
        expand_weight,
        expand_line,
        mixer_taps,
        mixer_line,
        shrink_weight,
        middle,
        attended,
        g_kept,
        gate_b,
        scale_b,
        gate_a,
        shrink_line,
        output_weight,
        mixed,
    )
    result, d_middle = turned[:2]
    d_mixed = turned[2:-2]
    grad_output, turn_sums = turned[-2:]

    hidden = expand_weight.shape[1]
    steps = hidden // features
    early = feed_grads(act, d_hid, normed_b, d_branch, devices)
    early_sum = lax.psum_scatter(early, both, scatter_dimension=0, tiled=False).astype(single)

    if share == 1:
        d_mixed = [spread(d) for d in d_mixed]
    else:
        parts = d_mixed[0].reshape(groups, quarter, share, width).transpose(0, 2, 1, 3)
        got = lax.all_to_all(parts.reshape(strips, quarter, width), "strips", 0, 0, tiled=True)
        got = got.reshape(strips * quarter, width)
        d_mixed = [got[:, c * piece : (c + 1) * piece] for c in range(chunks)]
    grads = []
    for c in range(chunks):
        if c == 0:
            d_mixed[c], _ = lax.optimization_barrier((d_mixed[c], early))
        q, k, v, out, logs = saved[c]
        if c < chunks - 1:
            grads.append(attend_back(q, k, v, out, d_mixed[c], logs))
        else:
            earlier = [g for chunk in grads for g in chunk]
            *last_grads, d_group = attend_back(
                q, k, v, out, d_mixed[c], logs, own_weight, earlier
            )
            grads.append(last_grads)
    size = features // devices
    narrow = jnp.stack([jnp.sum(turn_sums[:, 4], axis=0), jnp.sum(grad_shrink_bias[:, 0], axis=0)])
    to_all = jnp.concatenate(
        [
            turn_sums[:, 3], turn_sums[:, 1], turn_sums[:, 2], turn_sums[:, 0],
        ],
        axis=1,
    ).reshape(-1)
    whole_numbers = jnp.concatenate([timesteps // 32, timesteps % 32, labels // 32, labels % 32])
    to_all = jnp.concatenate([to_all, whole_numbers.astype(single)])
    fill = -(to_all.shape[0] + 11 * (hidden // devices) + 2 * size) % LANES
    early_small = jnp.concatenate(
        [
            jnp.broadcast_to(to_all, (devices, to_all.shape[0])),
            feed_small[:11].reshape(11, devices, -1).transpose(1, 0, 2).reshape(devices, -1),
            narrow.reshape(2, devices, -1).transpose(1, 0, 2).reshape(devices, -1),
            jnp.zeros((devices, fill), single),
        ],
        axis=1,
    ).astype(bfloat)
    early_small = after(early_small, *(grads[0][:1] if chunks > 1 else ()), *d_mixed)
    early_got = lax.all_to_all(early_small, both, 0, 0, tiled=True)

    parts = [g for chunk in grads for g in chunk]
    d_reduced = collect(d_group)
    if share > 1:
        d_reduced = jnp.sum(
            d_reduced.reshape(groups, share, quarter, features).astype(single), axis=1
        ).astype(bfloat)
    d_reduced = d_reduced.reshape(count, 4, quarter, features)
    late, d_sums = input_grad(after(group, d_group), grad_output, parts)
    d_query_sum = d_sums[0, :width]
    d_value_sum = d_sums[0, width:]
    if share > 1:
        zero = jnp.zeros((features, 3, features), bfloat)
        grad_input = lax.dynamic_update_slice(
            zero, late[:, : 3 * width].reshape(features, 3, width), (0, 0, head_at)
        ).reshape(features, 3 * features)
        late = jnp.concatenate([grad_input, grad_output], axis=1)
        flat = jnp.zeros((features,), single)
        d_query_sum = lax.dynamic_update_slice(flat, d_query_sum, (head_at,))
        d_value_sum = lax.dynamic_update_slice(flat, d_value_sum, (head_at,))
    late = late.reshape(items, strips // 2, 2, size, 4 * features)
    core = strip % 2
    keep = lax.dynamic_index_in_dim(late, core, 2, keepdims=False)
    give = lax.dynamic_index_in_dim(late, 1 - core, 2, keepdims=False)

    per_latent = count * 4 * features
    parts_early = early_got[:, :per_latent].reshape(items, strips, per_latent)
    first = early_got.reshape(items, strips, -1)[:, 0, per_latent : per_latent + 4 * count]
    first = first.astype(single).reshape(items, 4, count)
    all_times = (first[:, 0] * 32.0 + first[:, 1]).reshape(-1)
    all_labels = (first[:, 2] * 32.0 + first[:, 3]).reshape(-1, 1).astype(jnp.int32)
    sinus = time_features(all_times, waves)
    early_sums = jnp.sum(early_got[:, per_latent + 4 * count :].astype(single), axis=0)
    cut = 11 * (hidden // devices)
    feed_sum = early_sums[:cut].reshape(11, -1)
    narrow_sum = early_sums[cut : cut + 2 * size].reshape(2, size)
    index = jnp.reshape(me, (1,)).astype(jnp.int32)
    before, cond, d_active, grad_ada_early, d_mod_early = early_condition(
        index, parts_early, count, sinus, all_labels, weights, ada_weight, size
    )

    d_reduced, before, keep, give = lax.optimization_barrier((d_reduced, before, keep, give))
    late_part = sum_items(sum_cores(keep, give))
    grad_latents, down_small, final_sums = final(
        d_reduced,
        from_above(d_reduced[:, 2:, -2 * sub :]),
        from_below(d_reduced[:, :2, : 2 * sub]),
        normed_a,
        kept,
        d_middle,
        scale_a,
        down_taps,
    )

    late_narrow = jnp.concatenate([d_query_sum[None], d_value_sum[None], down_small[:10]], axis=0)
    to_all = final_sums[:, :2].reshape(-1)
    fill = -(to_all.shape[0] + 12 * size) % LANES
    late_small = jnp.concatenate(
        [
            jnp.broadcast_to(to_all, (devices, to_all.shape[0])),
            late_narrow.reshape(12, devices, size).transpose(1, 0, 2).reshape(devices, -1),
            jnp.zeros((devices, fill), single),
        ],
        axis=1,
    ).astype(bfloat)
    late_got = lax.all_to_all(late_small, both, 0, 0, tiled=True)
    late_got, late_part = lax.optimization_barrier((late_got, late_part))
    late_sum = sum_strips(late_part)
    late_sums = jnp.sum(late_got[:, to_all.shape[0] :].astype(single), axis=0)[: 12 * size].reshape(12, size)
    (
        grad_ada, d_mod, grad_table, grad_time_out, grad_time_in, d_cond, d_before,
    ) = late_condition(
        index,
        late_got[:, : to_all.shape[0]].reshape(items, strips, -1),
        count,
        before,
        cond,
        d_active,
        grad_ada_early,
        d_mod_early,
        sinus,
        all_labels,
        time_out_weight,
        ada_weight,
        label_table.shape[1],
        devices,
    )

    def mine(array):
        part = array.shape[-1] // devices
        return lax.dynamic_slice_in_dim(array[0], me * part, part, axis=0)

    return (
        result,
        grad_latents,
        grad_time_in,
        mine(d_before),
        grad_time_out,
        mine(d_cond),
        grad_table,
        grad_ada,
        mine(d_mod),
        late_sums[2:11].T,
        late_sums[11],
        late_sum[:, : 3 * features],
        late_sums[0],
        late_sums[1],
        late_sum[:, 3 * features :],
        narrow_sum[0],
        early_sum[steps:].transpose(1, 0, 2).reshape(size, hidden),
        feed_sum[10],
        feed_sum[:9].T,
        feed_sum[9],
        early_sum[:steps].reshape(hidden // devices, features),
        narrow_sum[1],
    )


def solution(mesh):
    image = P("items", "strips", None, None)
    split = P(both, None)
    line = P(both)
    return jax.shard_map(
        per_device,
        mesh=mesh,
        in_specs=(image, P("items"), P("items")) + (P(),) * 20 + (image,),
        out_specs=(
            image, image, split, line, split, line, split, split, line, split, line,
            split, line, line, split, line, split, line, split, line, split, line,
        ),
        check_vma=False,
    )
```
